32 devices in a mesh: tile: 32 (over z, y, x, core).
Axes of the slice: x: 2, y: 2, z: 4, core: 2. Of those that a mesh axis runs over, the one named last changes fastest.
Arguments:
- adjoint_zonal: bfloat16 [32, 8, 512, 128], P(None, None, 'tile'), may hold values from -70 to 70
- adjoint_meridional: bfloat16 [32, 8, 512, 128], P(None, None, 'tile'), may hold values from -70 to 70
- cell_fraction: bfloat16 [8, 512, 128], P(None, 'tile'), may hold values from 0.19921875 to 1
- level_thickness: float32 [8], replicated, may hold values from 0.5 to 2
- land_mask: int32 [512, 128], P('tile'), may hold values 0 or 1
- edge_codes: int32 [32, 4], P('tile'), may hold values from 0 to 1, as said below
Outputs:
- surface_adjoint: float32 [32, 512, 128], P(None, 'tile')
- residual: float32 [32, 512, 128], P(None, 'tile')
The draws below stay inside these ranges and needn't reach their ends.
Inputs may be any that keep to these rules, and one draw needn't show every extreme that they name: edge_codes[t, 1] equals edge_codes[t - 1, 0] and edge_codes[t, 3] equals edge_codes[t - 16, 2], tile numbers taken modulo 32.
All inputs are finite; a program needn't handle non-finite values. No bound on the sum of `land_mask` on one device may be relied on, other than what follows from the above.
Results may differ from the reference program's by a relative error of at most 0.0003.
Values may be sent and summed in bfloat16 or wider, within the bound.
No kernel may reach another device: no remote copies, remote signals or barrier semaphores. Data moves between devices by JAX's collectives and lax.ppermute only.
A program may use at most 64 MiB of HBM per device.

```python
import math
from functools import partial
import jax
import jax.numpy as jnp
from jax import lax

TY = 16
TX = 128
MEMB = 32
LEV = 8
NTX = 16
ITERS = 4
ROWS = 512
N_TILE = 32


def adjoint_field(key, salt):
    folded = jax.random.fold_in(key, salt)
    key_set = jax.random.split(folded, 3)
    row_scale = jnp.exp(jax.random.uniform(key_set[0], (ROWS,), jnp.float32, 0.0, math.log(3.2)))
    col_scale = jnp.exp(jax.random.uniform(key_set[1], (TX,), jnp.float32, 0.0, math.log(3.2)))
    tile_of_row = (jnp.arange(ROWS) // TY).astype(jnp.float32)
    tile_factor = 3.0 ** (tile_of_row / max(N_TILE - 1, 1))
    scaling = 0.25 * (row_scale * tile_factor)[:, None] * col_scale[None, :]
    jitter = jnp.clip(jax.random.normal(key_set[2], (MEMB, LEV, ROWS, TX), jnp.float32), -6.0, 6.0)
    values = jitter * scaling
    return values.astype(jnp.bfloat16)


def draw_adjoint_zonal(key, part):
    return adjoint_field(key, 11)


def draw_adjoint_meridional(key, part):
    return adjoint_field(key, 23)


def draw_edge_codes(key, part):
    key_pair = jax.random.split(jax.random.fold_in(key, 37), 2)
    east_flip = jax.random.randint(key_pair[0], (N_TILE,), 0, 2).astype(jnp.int32)
    north_flip = jax.random.randint(key_pair[1], (N_TILE,), 0, 2).astype(jnp.int32)
    return jnp.stack([east_flip, jnp.roll(east_flip, 1), north_flip, jnp.roll(north_flip, NTX)], axis=1).astype(jnp.int32)


def touch_ends(result, key, least, largest):
    dims = result.shape
    place = [jax.random.randint(jax.random.fold_in(key, axis), (), 0, dims[axis]) for axis in range(len(dims))]
    result = result.at[tuple(place)].set(least)
    longest = dims.index(max(dims))
    place[longest] = (place[longest] + 1) % dims[longest]
    return result.at[tuple(place)].set(largest)


def steps_of(stream_key, extent, shards, least, largest):
    def one(position, blocks):
        steps = jax.random.uniform(jax.random.fold_in(jax.random.fold_in(stream_key, 6), position), (blocks,), jnp.float32, least / len(shards), largest / len(shards))
        return jnp.repeat(jnp.exp(steps), extent[position] // blocks).reshape((-1,) + (1,) * (len(extent) - position - 1))

    factor_of = one(*shards[0])
    for cut in shards[1:]:
        factor_of = factor_of * one(*cut)
    return factor_of


def setup_inputs(seed: int = 0) -> dict:
    arg_keys = jax.random.split(jax.random.key(seed), 7)
    return {
        "adjoint_zonal": draw_adjoint_zonal(jax.random.fold_in(arg_keys[6], 71), 0),
        "adjoint_meridional": draw_adjoint_meridional(jax.random.fold_in(arg_keys[6], 71), 0),
        "cell_fraction": jnp.clip(0.19921875 + 0.80078125 * jax.random.uniform(arg_keys[2], (LEV, ROWS, TX), jnp.float32) ** steps_of(arg_keys[2], (LEV, ROWS, TX), ((1, 32),), -0.2, 0.2), 0.19921875, 1.0).astype(jnp.bfloat16),
        "level_thickness": jnp.clip(jnp.exp(jax.random.uniform(arg_keys[3], (LEV,), jnp.float32, math.log(0.5), math.log(2.0))), 0.5, 2.0),
        "land_mask": touch_ends((jax.random.randint(arg_keys[4], (ROWS, TX), 0, 5) < 4).astype(jnp.int32), jax.random.fold_in(arg_keys[4], 1), 0, 1),
        "edge_codes": draw_edge_codes(jax.random.fold_in(arg_keys[6], 71), 0),
    }


storage_coef = 1.0
coupling_coef = 0.25

def reverse_where(edge_values, reverse_flag):
    return jnp.where(reverse_flag == 1, jnp.flip(edge_values, -1), edge_values)

def attach(field_now, east_edge, west_edge, north_edge, south_edge):
    east_full = jnp.concatenate([field_now[..., 1:], east_edge[..., None]], axis=-1)
    west_full = jnp.concatenate([west_edge[..., None], field_now[..., :-1]], axis=-1)
    north_full = jnp.concatenate([field_now[..., 1:, :], north_edge[..., None, :]], axis=-2)
    south_full = jnp.concatenate([south_edge[..., None, :], field_now[..., :-1, :]], axis=-2)
    return (east_full, west_full, north_full, south_full)

def neighbour_fields(field_now, link_codes):
    east_edge = reverse_where(jnp.roll(field_now[..., :, 0], -1, axis=-2), link_codes[:, 0:1])
    west_edge = reverse_where(jnp.roll(field_now[..., :, -1], 1, axis=-2), link_codes[:, 1:2])
    north_edge = reverse_where(jnp.roll(field_now[..., 0, :], -NTX, axis=-2), link_codes[:, 2:3])
    south_edge = reverse_where(jnp.roll(field_now[..., -1, :], NTX, axis=-2), link_codes[:, 3:4])
    return attach(field_now, east_edge, west_edge, north_edge, south_edge)

def column_sum(values, fraction, thickness):
    running = thickness[0] * fraction[0].astype(jnp.float32) * values[:, 0].astype(jnp.float32)
    for level_index in range(1, values.shape[1]):
        running = running + thickness[level_index] * fraction[level_index].astype(jnp.float32) * values[:, level_index].astype(jnp.float32)
    return running

def column_depth(fraction, thickness, wet_cells):
    running = thickness[0] * fraction[0].astype(jnp.float32)
    for level_index in range(1, fraction.shape[0]):
        running = running + thickness[level_index] * fraction[level_index].astype(jnp.float32)
    return wet_cells * running

def apply_operator(field_now, diagonal, weights, neighbours):
    east_full, west_full, north_full, south_full = neighbours(field_now)
    return diagonal * field_now + weights[0] * (field_now - east_full) + weights[1] * (field_now - west_full) + weights[2] * (field_now - north_full) + weights[3] * (field_now - south_full)

def member_sum(first_field, second_field):
    return lax.optimization_barrier(jnp.sum(first_field * second_field, axis=(1, 2, 3)))

def widen(member_values):
    return member_values[:, None, None, None]

def reference(adjoint_zonal, adjoint_meridional, cell_fraction, level_thickness, land_mask, edge_codes):
    members = adjoint_zonal.shape[0]
    levels = adjoint_zonal.shape[1]
    zonal_tiles = adjoint_zonal.reshape(members, levels, N_TILE, TY, TX)
    meridional_tiles = adjoint_meridional.reshape(members, levels, N_TILE, TY, TX)
    fraction_tiles = cell_fraction.reshape(levels, N_TILE, TY, TX)
    wet_cells = land_mask.astype(jnp.float32).reshape(N_TILE, TY, TX)
    neighbours = partial(neighbour_fields, link_codes=edge_codes)
    water_depth = column_depth(fraction_tiles, level_thickness, wet_cells)
    transport_u = column_sum(zonal_tiles, fraction_tiles, level_thickness)
    transport_v = column_sum(meridional_tiles, fraction_tiles, level_thickness)
    east_transport = neighbours(transport_u)[0]
    north_transport = neighbours(transport_v)[2]
    right_side = wet_cells * (transport_u - east_transport + transport_v - north_transport)
    depth_east, depth_west, depth_north, depth_south = neighbours(water_depth)
    weights = (coupling_coef * jnp.sqrt(water_depth * depth_east), coupling_coef * jnp.sqrt(water_depth * depth_west), coupling_coef * jnp.sqrt(water_depth * depth_north), coupling_coef * jnp.sqrt(water_depth * depth_south))
    diagonal = storage_coef * wet_cells + (1.0 - wet_cells)
    solution = jnp.zeros_like(right_side)
    residual = right_side
    direction = right_side
    norm_now = member_sum(residual, residual)
    for step_index in range(ITERS):
        applied = apply_operator(direction, diagonal, weights, neighbours)
        step_size = norm_now / member_sum(direction, applied)
        solution = solution + widen(step_size) * direction
        residual = residual - widen(step_size) * applied
        norm_next = member_sum(residual, residual)
        direction = residual + widen(norm_next / norm_now) * direction
        norm_now = norm_next
    return (solution.reshape(members, N_TILE * TY, TX), residual.reshape(members, N_TILE * TY, TX))
```

```python
import jax
import jax.numpy as jnp
from jax import lax
from jax.sharding import PartitionSpec as P

NTX = 16
ITERS = 4

coupling_coef = 0.25


def column_sum(values, fraction, thickness):
    running = thickness[0] * fraction[0].astype(jnp.float32) * values[:, 0].astype(jnp.float32)
    for level in range(1, values.shape[1]):
        running = running + thickness[level] * fraction[level].astype(jnp.float32) * values[
            :, level
        ].astype(jnp.float32)
    return running


def column_depth(fraction, thickness, wet_cells):
    running = thickness[0] * fraction[0].astype(jnp.float32)
    for level in range(1, fraction.shape[0]):
        running = running + thickness[level] * fraction[level].astype(jnp.float32)
    return wet_cells * running


def reverse_where(edge, flags):
    return jnp.where(flags[:, None] == 1, jnp.flip(edge, -1), edge)


def east_edge_of(column, codes):
    return reverse_where(jnp.roll(column, -1, axis=0), codes[:, 0])


def west_edge_of(column, codes):
    return reverse_where(jnp.roll(column, 1, axis=0), codes[:, 1])


def north_edge_of(row, codes):
    return reverse_where(jnp.roll(row, -NTX, axis=0), codes[:, 2])


def south_edge_of(row, codes):
    return reverse_where(jnp.roll(row, NTX, axis=0), codes[:, 3])


def neighbours(field, codes):
    east = jnp.concatenate([field[:, :, 1:], east_edge_of(field[:, :, 0], codes)[:, :, None]], 2)
    west = jnp.concatenate([west_edge_of(field[:, :, -1], codes)[:, :, None], field[:, :, :-1]], 2)
    north = jnp.concatenate([field[:, 1:, :], north_edge_of(field[:, 0, :], codes)[:, None]], 1)
    south = jnp.concatenate([south_edge_of(field[:, -1, :], codes)[:, None], field[:, :-1, :]], 1)
    return east, west, north, south


def conjugate_gradients(right_side, depth, codes):
    weights = [
        coupling_coef * jnp.sqrt(depth * other) for other in neighbours(depth, codes)
    ]

    def operator(field):
        image = field
        for weight, other in zip(weights, neighbours(field, codes)):
            image = image + weight * (field - other)
        return image

    surface = jnp.zeros_like(right_side)
    residual = right_side
    direction = right_side
    norm_now = jnp.sum(residual * residual)
    for _ in range(ITERS):
        image = operator(direction)
        step_size = norm_now / jnp.sum(direction * image)
        surface = surface + step_size * direction
        residual = residual - step_size * image
        norm_next = jnp.sum(residual * residual)
        direction = residual + (norm_next / norm_now) * direction
        norm_now = norm_next
    return surface, residual


def on_device(zonal, meridional, fraction, thickness, land_mask, edge_codes):
    tiles = lax.axis_size("tile")
    members, _, rows, columns = zonal.shape
    slots = max(1, -(-members // tiles))
    wet = land_mask.astype(jnp.float32)
    depth = column_depth(fraction, thickness, wet)
    transport_u = column_sum(zonal, fraction, thickness)
    transport_v = column_sum(meridional, fraction, thickness)
    part = (
        transport_u
        - jnp.pad(transport_u[..., 1:], ((0, 0), (0, 0), (0, 1)))
        + transport_v
        - jnp.pad(transport_v[:, 1:], ((0, 0), (0, 1), (0, 0)))
    )
    small = jnp.concatenate(
        [
            transport_u[..., 0],
            jnp.broadcast_to(edge_codes[0].astype(jnp.float32), (members, 4)),
            jnp.zeros((members, columns - rows - 4), jnp.float32),
        ],
        axis=1,
    )
    message = jnp.concatenate(
        [
            part,
            jnp.broadcast_to(depth, (members, rows, columns)),
            transport_v[:, :1],
            small[:, None],
        ],
        axis=1,
    )
    message = jnp.pad(message, ((0, slots * tiles - members), (0, 0), (0, 0)))
    got = lax.all_to_all(message, "tile", split_axis=0, concat_axis=0, tiled=True)
    got = got.reshape(tiles, slots, 2 * rows + 2, columns)
    codes = got[:, 0, 2 * rows + 1, rows : rows + 4].astype(jnp.int32)
    depth_all = got[:, 0, rows : 2 * rows]
    wet_all = (depth_all > 0).astype(jnp.float32)

    def one(mine):
        field = mine[:, :rows]
        east = east_edge_of(mine[:, 2 * rows + 1, :rows], codes)
        north = north_edge_of(mine[:, 2 * rows], codes)
        field = field.at[:, :, columns - 1].add(-east).at[:, rows - 1].add(-north)
        return jnp.concatenate(conjugate_gradients(wet_all * field, depth_all, codes), axis=1)

    back = jnp.stack([one(got[:, slot]) for slot in range(slots)], axis=1)
    back = back.reshape(tiles * slots, 2 * rows, columns)
    home = lax.all_to_all(back, "tile", split_axis=0, concat_axis=0, tiled=True)[:members]
    return home[:, :rows], home[:, rows:]


def solution(mesh):
    in_specs = (
        P(None, None, "tile", None),
        P(None, None, "tile", None),
        P(None, "tile", None),
        P(),
        P("tile", None),
        P("tile", None),
    )
    out_specs = (P(None, "tile", None), P(None, "tile", None))
    return jax.shard_map(
        on_device, mesh=mesh, in_specs=in_specs, out_specs=out_specs, check_vma=False
    )
```

```python
import functools

import jax
import jax.numpy as jnp
from jax import lax
from jax.experimental import pallas as pl
from jax.experimental.pallas import tpu as pltpu
from jax.sharding import PartitionSpec as P

NTX = 16
ITERS = 4
CHUNK = 32
EXTRA = 8
LIMIT = 56 * 1024 * 1024

coupling_coef = 0.25


def column_depth(fraction, thickness, wet_cells):
    running = thickness[0] * fraction[0].astype(jnp.float32)
    for level in range(1, fraction.shape[0]):
        running = running + thickness[level] * fraction[level].astype(jnp.float32)
    return wet_cells * running


def message_kernel(thickness_ref, codes_ref, zonal_ref, meridional_ref, fraction_ref, out_ref):
    members, levels, rows, columns = zonal_ref.shape
    lane = lax.broadcasted_iota(jnp.int32, (rows, columns), 1)
    row = lax.broadcasted_iota(jnp.int32, (rows, columns), 0)
    place = lax.broadcasted_iota(jnp.int32, (EXTRA, columns), 0)
    wide = lax.broadcasted_iota(jnp.int32, (EXTRA, columns), 1)
    code = [jnp.where(codes_ref[0, side] == 1, 1.0, 0.0) for side in range(4)]
    flags = jnp.where(place == 2, jnp.where(wide >= columns // 2, code[0], code[1]), 0.0)
    flags = jnp.where(place == 3, code[2], jnp.where(place == 4, code[3], flags))
    parts = [
        thickness_ref[level] * fraction_ref[level].astype(jnp.float32) for level in range(levels)
    ]
    for member in range(members):
        along = parts[0] * zonal_ref[member, 0].astype(jnp.float32)
        across = parts[0] * meridional_ref[member, 0].astype(jnp.float32)
        for level in range(1, levels):
            along = along + parts[level] * zonal_ref[member, level].astype(jnp.float32)
            across = across + parts[level] * meridional_ref[member, level].astype(jnp.float32)
        east = jnp.where(lane == columns - 1, 0.0, pltpu.roll(along, columns - 1, 1))
        north = jnp.where(row == rows - 1, 0.0, pltpu.roll(across, rows - 1, 0))
        out_ref[member, 0:rows] = along - east + across - north
        first = jnp.where(lane == row, along[:, 0:1], 0.0)
        first = jnp.sum(first, axis=0, keepdims=True)
        out_ref[member, rows : rows + EXTRA] = jnp.where(
            place == 0, across[0:1], jnp.where(place == 1, first, flags)
        )


def message_of(zonal, meridional, fraction, thickness, codes):
    members, levels, rows, columns = zonal.shape
    step = 8 if members % 8 == 0 else 1
    field = pl.BlockSpec((step, levels, rows, columns), lambda at: (at, 0, 0, 0))
    return pl.pallas_call(
        message_kernel,
        grid=(members // step,),
        in_specs=[
            pl.BlockSpec(memory_space=pltpu.SMEM),
            pl.BlockSpec(memory_space=pltpu.SMEM),
            field,
            field,
            pl.BlockSpec((levels, rows, columns), lambda at: (0, 0, 0)),
        ],
        out_specs=pl.BlockSpec((step, rows + EXTRA, columns), lambda at: (at, 0, 0)),
        out_shape=jax.ShapeDtypeStruct((members, rows + EXTRA, columns), jnp.float32),
        compiler_params=pltpu.CompilerParams(vmem_limit_bytes=LIMIT),
    )(thickness, codes, zonal, meridional, fraction)


def reversed_rows(values):
    groups = values.shape[0] // 8
    index = 7 - lax.broadcasted_iota(jnp.int32, (8, values.shape[1]), 0)
    pieces = [
        jnp.take_along_axis(
            values[8 * at : 8 * at + 8], index, axis=0, mode="promise_in_bounds"
        )
        for at in reversed(range(groups))
    ]
    return jnp.concatenate(pieces, axis=0)


def reversed_lanes(values):
    columns = values.shape[1]
    index = columns - 1 - lax.broadcasted_iota(jnp.int32, values.shape, 1)
    return jnp.take_along_axis(values, index, axis=1, mode="promise_in_bounds")


def cg_kernel(
    got_ref, depth_ref, out_ref, direction_ref, image_ref, east_ref, west_ref, north_ref, south_ref, total_ref
):
    tiles, rows, columns = depth_ref.shape
    lane = lax.broadcasted_iota(jnp.int32, (rows, columns), 1)
    row = lax.broadcasted_iota(jnp.int32, (rows, columns), 0)
    near = lax.broadcasted_iota(jnp.int32, (8, columns), 0)
    chunk = min(CHUNK, tiles)

    def over_tiles(body, carry):
        if tiles == chunk:
            for tile in range(tiles):
                carry = body(tile, carry)
            return carry

        def some(at, inner):
            for tile in range(chunk):
                inner = body(at * chunk + tile, inner)
            return inner

        return lax.fori_loop(0, tiles // chunk, some, carry)

    def shift(tile, by):
        if isinstance(tile, int):
            return (tile + by) % tiles
        return lax.rem(tile + by + tiles, tiles)

    def neighbours(ref, tile):
        own = ref[tile]
        flip_sides = got_ref[tile, rows + 2 : rows + 3, :] > 0.5
        side = jnp.where(
            lane == columns - 1,
            pltpu.roll(ref[shift(tile, 1)], columns - 1, 1),
            pltpu.roll(ref[shift(tile, -1)], 1, 1),
        )
        side = jnp.where(flip_sides, reversed_rows(side), side)
        east = jnp.where(lane == columns - 1, side, pltpu.roll(own, columns - 1, 1))
        west = jnp.where(lane == 0, side, pltpu.roll(own, 1, 1))
        flip_ends = (
            jnp.where(
                near == 7,
                got_ref[tile, rows + 3 : rows + 4, :],
                got_ref[tile, rows + 4 : rows + 5, :],
            )
            > 0.5
        )
        ends = jnp.where(
            near == 7,
            ref[shift(tile, NTX), 0:1, :],
            ref[shift(tile, -NTX), rows - 1 : rows, :],
        )
        ends = jnp.where(flip_ends, reversed_lanes(ends), ends)
        ends = jnp.concatenate([ends] * (rows // 8), axis=0)
        north = jnp.where(row == rows - 1, ends, pltpu.roll(own, rows - 1, 0))
        south = jnp.where(row == 0, ends, pltpu.roll(own, 1, 0))
        return own, east, west, north, south

    def prepare(tile, carry):
        image_ref[tile] = jnp.sqrt(depth_ref[tile])
        return carry

    over_tiles(prepare, 0)

    def begin(tile, norm):
        own, east, west, north, south = neighbours(image_ref, tile)
        scaled = coupling_coef * own
        east, west, north, south = scaled * east, scaled * west, scaled * north, scaled * south
        east_ref[tile], west_ref[tile], north_ref[tile], south_ref[tile] = east, west, north, south
        total_ref[tile] = 1.0 + ((east + west) + (north + south))
        flip_east = got_ref[tile, rows + 2 : rows + 3, columns - 1 : columns] > 0.5
        target = jnp.where(flip_east, rows - 1 - row, row)
        edge = jnp.where(lane == target, got_ref[shift(tile, 1), rows + 1 : rows + 2, :], 0.0)
        edge = jnp.sum(edge, axis=1, keepdims=True)
        flip_north = got_ref[tile, rows + 3 : rows + 4, :] > 0.5
        end = jnp.broadcast_to(got_ref[shift(tile, NTX), rows : rows + 1, :], (8, columns))
        end = jnp.where(flip_north, reversed_lanes(end), end)
        end = jnp.concatenate([end] * (rows // 8), axis=0)
        field = got_ref[tile, 0:rows]
        field = field - jnp.where(lane == columns - 1, edge, 0.0)
        field = field - jnp.where(row == rows - 1, end, 0.0)
        field = jnp.where(depth_ref[tile] > 0.0, field, 0.0)
        out_ref[tile, rows : 2 * rows] = field
        direction_ref[tile] = field
        out_ref[tile, 0:rows] = jnp.zeros_like(field)
        return norm + field * field

    def all_of(total):
        return jnp.sum(total, keepdims=True)

    zero = jnp.zeros((rows, columns), jnp.float32)

    def iteration(_, norm):
        def apply(tile, total):
            own, east, west, north, south = neighbours(direction_ref, tile)
            image = total_ref[tile] * own - (
                (east_ref[tile] * east + west_ref[tile] * west)
                + (north_ref[tile] * north + south_ref[tile] * south)
            )
            image_ref[tile] = image
            return total + own * image

        step = norm / all_of(over_tiles(apply, zero))

        def advance(tile, total):
            out_ref[tile, 0:rows] = out_ref[tile, 0:rows] + step * direction_ref[tile]
            residual = out_ref[tile, rows : 2 * rows] - step * image_ref[tile]
            out_ref[tile, rows : 2 * rows] = residual
            return total + residual * residual

        later = all_of(over_tiles(advance, zero))
        ratio = later / norm

        def turn(tile, carry):
            direction_ref[tile] = out_ref[tile, rows : 2 * rows] + ratio * direction_ref[tile]
            return carry

        over_tiles(turn, 0)
        return later

    lax.fori_loop(0, ITERS, iteration, all_of(over_tiles(begin, zero)))


def cg_of(got, depth):
    tiles, rows, columns = depth.shape
    field = pltpu.VMEM((tiles, rows, columns), jnp.float32)
    return pl.pallas_call(
        cg_kernel,
        in_specs=[pl.BlockSpec(memory_space=pltpu.VMEM)] * 2,
        out_specs=pl.BlockSpec(memory_space=pltpu.VMEM),
        out_shape=jax.ShapeDtypeStruct((tiles, 2 * rows, columns), jnp.float32),
        scratch_shapes=[field] * 7,
        compiler_params=pltpu.CompilerParams(vmem_limit_bytes=LIMIT),
    )(got, depth)


def on_device(zonal, meridional, fraction, thickness, land_mask, edge_codes):
    tiles = lax.axis_size("tile")
    members, _, rows, columns = zonal.shape
    depth = column_depth(fraction, thickness, land_mask.astype(jnp.float32))
    depth = lax.all_gather(depth, "tile")
    message = message_of(zonal, meridional, fraction, thickness, edge_codes)
    if tiles > members:
        message = jnp.pad(message, ((0, tiles - members), (0, 0), (0, 0)))
    got = lax.all_to_all(message, "tile", split_axis=0, concat_axis=0, tiled=True)
    back = cg_of(got, depth)
    home = lax.all_to_all(back, "tile", split_axis=0, concat_axis=0, tiled=True)[:members]
    return home[:, :rows], home[:, rows:]


def solution(mesh):
    in_specs = (
        P(None, None, "tile", None),
        P(None, None, "tile", None),
        P(None, "tile", None),
        P(),
        P("tile", None),
        P("tile", None),
    )
    out_specs = (P(None, "tile", None), P(None, "tile", None))
    return jax.shard_map(
        on_device, mesh=mesh, in_specs=in_specs, out_specs=out_specs, check_vma=False
    )
```

```python
import functools

import jax
import jax.numpy as jnp
from jax import lax
from jax.experimental import pallas as pl
from jax.experimental.pallas import tpu as pltpu
from jax.sharding import PartitionSpec as P

NTX = 16
ITERS = 4
CHUNK = 32
STEPS = 262143.0
LIMIT = 56 * 1024 * 1024

coupling_coef = 0.25


def message_kernel(
    thickness_ref, codes_ref, zonal_ref, meridional_ref, fraction_ref, land_ref, out_ref
):
    members, levels, rows, columns = zonal_ref.shape
    lane = lax.broadcasted_iota(jnp.int32, (rows, columns), 1)
    row = lax.broadcasted_iota(jnp.int32, (rows, columns), 0)
    place = lax.broadcasted_iota(jnp.int32, (8, columns), 0)
    wide = lax.broadcasted_iota(jnp.int32, (8, columns), 1)
    code = [jnp.where(codes_ref[0, side] == 1, 1.0, 0.0) for side in range(4)]
    parts = [
        thickness_ref[level] * fraction_ref[level].astype(jnp.float32) for level in range(levels)
    ]
    depth = functools.reduce(lambda one, other: one + other, parts)
    whole = sum_of(thickness_ref, levels)
    steps = jnp.floor(jnp.where(land_ref[...] == 1, depth * (STEPS / whole), 0.0) + 0.5)
    upper, lower = steps[0:8], steps[8:16]
    high = jnp.floor(lower * (1.0 / 64.0))
    words = upper + 262144.0 * (lower - 64.0 * high)
    rest = high + 4096.0 * pltpu.roll(high, 4, 0)
    rest = jnp.where(place == 6, jnp.where(wide >= columns // 2, code[0], code[1]), rest)
    rest = jnp.where(place == 7, code[2] + 2.0 * code[3], rest)
    for member in range(members):
        along = parts[0] * zonal_ref[member, 0].astype(jnp.float32)
        across = parts[0] * meridional_ref[member, 0].astype(jnp.float32)
        for level in range(1, levels):
            along = along + parts[level] * zonal_ref[member, level].astype(jnp.float32)
            across = across + parts[level] * meridional_ref[member, level].astype(jnp.float32)
        east = jnp.where(lane == columns - 1, 0.0, pltpu.roll(along, columns - 1, 1))
        north = jnp.where(row == rows - 1, 0.0, pltpu.roll(across, rows - 1, 0))
        out_ref[member, 0:rows] = along - east + across - north
        first = jnp.where(lane == row, along[:, 0:1], 0.0)
        first = jnp.sum(first, axis=0, keepdims=True)
        out_ref[member, rows : rows + 8] = words
        out_ref[member, rows + 8 : rows + 16] = jnp.where(
            place == 4, across[0:1], jnp.where(place == 5, first, rest)
        )


def sum_of(thickness_ref, levels):
    whole = thickness_ref[0]
    for level in range(1, levels):
        whole = whole + thickness_ref[level]
    return whole


def message_of(zonal, meridional, fraction, thickness, land_mask, codes):
    members, levels, rows, columns = zonal.shape
    step = 8 if members % 8 == 0 else 1
    field = pl.BlockSpec((step, levels, rows, columns), lambda at: (at, 0, 0, 0))
    return pl.pallas_call(
        message_kernel,
        grid=(members // step,),
        in_specs=[
            pl.BlockSpec(memory_space=pltpu.SMEM),
            pl.BlockSpec(memory_space=pltpu.SMEM),
            field,
            field,
            pl.BlockSpec((levels, rows, columns), lambda at: (0, 0, 0)),
            pl.BlockSpec((rows, columns), lambda at: (0, 0)),
        ],
        out_specs=pl.BlockSpec((step, 2 * rows, columns), lambda at: (at, 0, 0)),
        out_shape=jax.ShapeDtypeStruct((members, 2 * rows, columns), jnp.float32),
        compiler_params=pltpu.CompilerParams(vmem_limit_bytes=LIMIT),
    )(thickness, codes, zonal, meridional, fraction, land_mask)


def reversed_rows(values):
    groups = values.shape[0] // 8
    index = 7 - lax.broadcasted_iota(jnp.int32, (8, values.shape[1]), 0)
    pieces = [
        jnp.take_along_axis(
            values[8 * at : 8 * at + 8], index, axis=0, mode="promise_in_bounds"
        )
        for at in reversed(range(groups))
    ]
    return jnp.concatenate(pieces, axis=0)


def reversed_lanes(values):
    columns = values.shape[1]
    index = columns - 1 - lax.broadcasted_iota(jnp.int32, values.shape, 1)
    return jnp.take_along_axis(values, index, axis=1, mode="promise_in_bounds")


def cg_kernel(
    thickness_ref,
    got_ref,
    out_ref,
    field_ref,
    image_ref,
    east_ref,
    west_ref,
    north_ref,
    south_ref,
    total_ref,
    side_ref,
    turned_ref,
    ends_ref,
):
    tiles, rows, columns = image_ref.shape
    levels = thickness_ref.shape[0]
    lane = lax.broadcasted_iota(jnp.int32, (rows, columns), 1)
    row = lax.broadcasted_iota(jnp.int32, (rows, columns), 0)
    near = lax.broadcasted_iota(jnp.int32, (8, columns), 0)
    chunk = min(CHUNK, tiles)

    def over_tiles(body, carry):
        def some(base, inner):
            rolled = {}
            for step in range(chunk):
                inner = body(base, step, rolled, inner)
            return inner

        if tiles == chunk:
            return some(0, carry)
        return lax.fori_loop(0, tiles // chunk, lambda at, inner: some(at * chunk, inner), carry)

    def shift(base, by):
        if isinstance(base, int):
            return (base + by) % tiles
        return lax.rem(base + by + tiles, tiles)

    def first_row(tile):
        at = tile * rows + 8
        return at if isinstance(at, int) else pl.multiple_of(at, 8)

    def field(tile, by=0):
        return field_ref[pl.ds(first_row(tile) + by, rows), :]

    def turned(base, step, rolled, by):
        key = (step, by)
        if key not in rolled:
            rolled[key] = pltpu.roll(field(shift(base, step)), by, 1)
        return rolled[key]

    def flip_sides(tile):
        return got_ref[tile, 2 * rows - 2 : 2 * rows - 1, :] > 0.5

    def flip_ends(tile):
        both = got_ref[tile, 2 * rows - 1 : 2 * rows, :]
        south = jnp.where(both > 1.5, 1.0, 0.0)
        return jnp.where(near == 7, both - 2.0 * south, south) > 0.5

    def neighbours(base, step, rolled):
        tile = shift(base, step)
        own = field(tile)
        east = turned(base, step, rolled, columns - 1)
        west = turned(base, step, rolled, 1)
        side = jnp.where(
            lane >= columns // 2,
            turned(base, step + 1, rolled, columns - 1),
            turned(base, step - 1, rolled, 1),
        )
        ends = jnp.where(
            near == 7,
            field_ref[pl.ds(first_row(shift(base, step + NTX)), 1), :],
            field_ref[pl.ds(first_row(shift(base, step - NTX)) + rows - 1, 1), :],
        )
        ends = jnp.where(flip_ends(tile), reversed_lanes(ends), ends)
        return own, east, west, field(tile, 1), field(tile, -1), side, reversed_rows(side), ends

    levels_sum = sum_of(thickness_ref, levels)
    padding = jnp.zeros((8, columns), jnp.float32)
    field_ref[0:8, :] = padding
    field_ref[tiles * rows + 8 : tiles * rows + 16, :] = padding

    def read_depth(base, step, rolled, carry):
        tile = shift(base, step)
        words = got_ref[tile, rows : rows + 8, :]
        rest = got_ref[tile, rows + 8 : rows + 16, :]
        low = jnp.floor(words * (1.0 / 262144.0))
        upper = words - 262144.0 * low
        second = jnp.floor(rest * (1.0 / 4096.0))
        high = jnp.where(near < 4, rest - 4096.0 * second, pltpu.roll(second, 4, 0))
        lower = low + 64.0 * high
        depth = jnp.concatenate([upper, lower], axis=0) * (levels_sum / STEPS)
        field_ref[pl.ds(first_row(tile), rows), :] = jnp.sqrt(depth)
        return carry

    over_tiles(read_depth, 0)

    def weights(base, step, rolled, carry):
        tile = shift(base, step)
        own, east, west, north, south, side, side_turned, ends = neighbours(base, step, rolled)
        own = coupling_coef * own
        east = jnp.where(lane == columns - 1, 0.0, own * east)
        west = jnp.where(lane == 0, 0.0, own * west)
        north = jnp.where(row == rows - 1, 0.0, own * north)
        south = jnp.where(row == 0, 0.0, own * south)
        edge = jnp.logical_or(lane == 0, lane == columns - 1)
        side = jnp.where(edge, own * jnp.where(flip_sides(tile), side_turned, side), 0.0)
        upper = jnp.where(near == 0, own[0:8] * ends, 0.0)
        lower = jnp.where(near == 7, own[rows - 8 : rows] * ends, 0.0)
        east_ref[tile], west_ref[tile], north_ref[tile], south_ref[tile] = east, west, north, south
        side_ref[tile] = jnp.where(flip_sides(tile), 0.0, side)
        turned_ref[tile] = jnp.where(flip_sides(tile), side, 0.0)
        both = jnp.concatenate([upper, lower], axis=0)
        ends_ref[tile] = both
        total_ref[tile] = 1.0 + ((east + west) + (north + south)) + (side + both)
        return carry

    over_tiles(weights, 0)

    def begin(base, step, rolled, norm):
        tile = shift(base, step)
        wet = field(tile) > 0.0
        flip_east = got_ref[tile, 2 * rows - 2 : 2 * rows - 1, columns - 1 : columns] > 0.5
        target = jnp.where(flip_east, rows - 1 - row, row)
        edge = got_ref[shift(base, step + 1), 2 * rows - 3 : 2 * rows - 2, :]
        edge = jnp.sum(jnp.where(lane == target, edge, 0.0), axis=1, keepdims=True)
        end = got_ref[shift(base, step + NTX), 2 * rows - 4 : 2 * rows - 3, :]
        end = jnp.broadcast_to(end, (8, columns))
        end = jnp.where(flip_ends(tile), reversed_lanes(end), end)
        end = jnp.concatenate([end] * (rows // 8), axis=0)
        value = got_ref[tile, 0:rows]
        value = value - jnp.where(lane == columns - 1, edge, 0.0)
        value = value - jnp.where(row == rows - 1, end, 0.0)
        value = jnp.where(wet, value, 0.0)
        out_ref[tile, rows : 2 * rows] = value
        field_ref[pl.ds(first_row(tile), rows), :] = value
        out_ref[tile, 0:rows] = jnp.zeros_like(value)
        return norm + value * value

    def all_of(total):
        return jnp.sum(total, keepdims=True)

    zero = jnp.zeros((rows, columns), jnp.float32)

    def iteration(_, norm):
        def apply(base, step, rolled, total):
            tile = shift(base, step)
            own, east, west, north, south, side, side_turned, ends = neighbours(base, step, rolled)
            others = (
                (east_ref[tile] * east + west_ref[tile] * west)
                + (north_ref[tile] * north + south_ref[tile] * south)
                + (side_ref[tile] * side + turned_ref[tile] * side_turned)
                + ends_ref[tile] * jnp.concatenate([ends] * (rows // 8), axis=0)
            )
            image = total_ref[tile] * own - others
            image_ref[tile] = image
            return total + own * image

        step_size = norm / all_of(over_tiles(apply, zero))

        def advance(base, step, rolled, total):
            tile = shift(base, step)
            out_ref[tile, 0:rows] = out_ref[tile, 0:rows] + step_size * field(tile)
            residual = out_ref[tile, rows : 2 * rows] - step_size * image_ref[tile]
            out_ref[tile, rows : 2 * rows] = residual
            return total + residual * residual

        later = all_of(over_tiles(advance, zero))
        ratio = later / norm

        def turn(base, step, rolled, carry):
            tile = shift(base, step)
            field_ref[pl.ds(first_row(tile), rows), :] = (
                out_ref[tile, rows : 2 * rows] + ratio * field(tile)
            )
            return carry

        over_tiles(turn, 0)
        return later

    lax.fori_loop(0, ITERS, iteration, all_of(over_tiles(begin, zero)))


def cg_of(got, thickness, rows):
    tiles, _, columns = got.shape
    field = pltpu.VMEM((tiles, rows, columns), jnp.float32)
    return pl.pallas_call(
        cg_kernel,
        in_specs=[
            pl.BlockSpec(memory_space=pltpu.SMEM),
            pl.BlockSpec(memory_space=pltpu.VMEM),
        ],
        out_specs=pl.BlockSpec(memory_space=pltpu.VMEM),
        out_shape=jax.ShapeDtypeStruct((tiles, 2 * rows, columns), jnp.float32),
        scratch_shapes=[pltpu.VMEM((tiles * rows + 16, columns), jnp.float32)] + [field] * 9,
        compiler_params=pltpu.CompilerParams(vmem_limit_bytes=LIMIT),
    )(thickness, got)


def on_device(zonal, meridional, fraction, thickness, land_mask, edge_codes):
    tiles = lax.axis_size("tile")
    members, _, rows, columns = zonal.shape
    message = message_of(zonal, meridional, fraction, thickness, land_mask, edge_codes)
    if tiles > members:
        message = jnp.pad(message, ((0, tiles - members), (0, 0), (0, 0)))
    got = lax.all_to_all(message, "tile", split_axis=0, concat_axis=0, tiled=True)
    back = cg_of(got, thickness, rows)
    home = lax.all_to_all(back, "tile", split_axis=0, concat_axis=0, tiled=True)[:members]
    return home[:, :rows], home[:, rows:]


def solution(mesh):
    in_specs = (
        P(None, None, "tile", None),
        P(None, None, "tile", None),
        P(None, "tile", None),
        P(),
        P("tile", None),
        P("tile", None),
    )
    out_specs = (P(None, "tile", None), P(None, "tile", None))
    return jax.shard_map(
        on_device, mesh=mesh, in_specs=in_specs, out_specs=out_specs, check_vma=False
    )
```

```python
import functools

import jax
import jax.numpy as jnp
from jax import lax
from jax.experimental import pallas as pl
from jax.experimental.pallas import tpu as pltpu
from jax.sharding import PartitionSpec as P

NTX = 16
ITERS = 4
CHUNK = 32
STEPS = 1048575.0
MIDDLE = 4194304.0

coupling_coef = 0.25


def power_of_two(exponent):
    power = lax.shift_left(jnp.ones_like(exponent), exponent & 15).astype(jnp.float32)
    for bit in (16, 32, 64):
        power = jnp.where((exponent & bit) != 0, power * 2.0**bit, power)
    return power


def exponent_for(largest):
    for by in (4, 2, 1):
        largest = jnp.maximum(largest, pltpu.roll(largest, by, 0))
    log = jnp.log(jnp.maximum(largest, 2.0**-90)) * 1.4426950408889634
    return jnp.clip(jnp.floor(log + 0.01).astype(jnp.int32) + 97, 0, 127)


def steps_of(values, gain):
    shifted = jnp.minimum(values * gain + 3.0 * MIDDLE, 4.0 * MIDDLE - 1.0)
    return shifted.astype(jnp.int32) - int(2.0 * MIDDLE)


def packed(upper, lower, exponent, gain):
    upper = steps_of(upper, gain)
    lower = steps_of(lower, gain)
    words = upper | lax.shift_left(lower, 23)
    high = lax.shift_right_logical(lower, 9)
    sub = lax.broadcasted_iota(jnp.int32, high.shape, 0)
    part = lax.shift_right_logical(exponent, 4 * sub) & 15
    rest = high | lax.shift_left(pltpu.roll(high, 4, 0), 14) | lax.shift_left(part, 28)
    return words, rest


def gain_of(exponent):
    return power_of_two(127 - exponent) * 2.0**-9


def unpacked(words, rest):
    sub = lax.broadcasted_iota(jnp.int32, words.shape, 0)
    part = lax.shift_right_logical(rest, 28)
    exponent = part[0:1] + 16 * part[1:2]
    step = power_of_two(exponent) * 2.0**-118
    upper = words & 0x7FFFFF
    high = jnp.where(sub < 4, rest, pltpu.roll(lax.shift_right_logical(rest, 14), 4, 0)) & 0x3FFF
    lower = lax.shift_right_logical(words, 23) | lax.shift_left(high, 9)
    return (
        (upper.astype(jnp.float32) - MIDDLE) * step,
        (lower.astype(jnp.float32) - MIDDLE) * step,
        step,
    )


def message_kernel(
    thickness_ref, codes_ref, zonal_ref, meridional_ref, fraction_ref, land_ref, out_ref
):
    members, levels, rows, columns = zonal_ref.shape
    lane = lax.broadcasted_iota(jnp.int32, (rows, columns), 1)
    row = lax.broadcasted_iota(jnp.int32, (rows, columns), 0)
    place = lax.broadcasted_iota(jnp.int32, (8, columns), 0)
    code = [jnp.where(codes_ref[0, side] == 1, 1 << (23 + side), 0) for side in range(4)]
    flags = (code[0] + code[1]) + (code[2] + code[3])
    parts = [
        thickness_ref[level] * fraction_ref[level].astype(jnp.float32) for level in range(levels)
    ]
    depth = functools.reduce(lambda one, other: one + other, parts)
    scale = STEPS / sum_of(thickness_ref, levels)
    steps = jnp.where(land_ref[...] == 1, depth * scale + 0.5, 0.0).astype(jnp.int32)
    upper, lower = steps[0:8], steps[8:16]
    pairs = lax.shift_right_logical(upper, 4) | lax.shift_left(
        lax.shift_right_logical(lower, 4), 16
    )

    def gathered(values):
        values = lax.shift_left(values & 15, 4 * place)
        for by in (4, 2, 1):
            values = values | pltpu.roll(values, by, 0)
        return values

    low = jnp.where(place == 6, gathered(upper), gathered(lower))
    for member in range(members):
        along = parts[0] * zonal_ref[member, 0].astype(jnp.float32)
        across = parts[0] * meridional_ref[member, 0].astype(jnp.float32)
        for level in range(1, levels):
            along = along + parts[level] * zonal_ref[member, level].astype(jnp.float32)
            across = across + parts[level] * meridional_ref[member, level].astype(jnp.float32)
        east = jnp.where(lane == columns - 1, 0.0, pltpu.roll(along, columns - 1, 1))
        north = jnp.where(row == rows - 1, 0.0, pltpu.roll(across, rows - 1, 0))
        value = along - east + across - north
        first = jnp.where(lane == row, along[:, 0:1], 0.0)
        first = first[0:8] + first[8:16]
        for by in (4, 2, 1):
            first = first + pltpu.roll(first, by, 0)
        edges = jnp.where(place == 5, first, across[0:1])
        largest = jnp.maximum(jnp.abs(value[0:8]), jnp.abs(value[8:16]))
        exponent = exponent_for(jnp.maximum(largest, jnp.abs(edges)))
        gain = gain_of(exponent)
        words, rest = packed(value[0:8], value[8:16], exponent, gain)
        edges = steps_of(edges, gain) | flags
        out_ref[member, 0:8] = words
        out_ref[member, 8:16] = jnp.where(place < 4, rest, jnp.where(place < 6, edges, low))
        out_ref[member, 16:24] = pairs


def sum_of(thickness_ref, levels):
    whole = thickness_ref[0]
    for level in range(1, levels):
        whole = whole + thickness_ref[level]
    return whole


def message_of(zonal, meridional, fraction, thickness, land_mask, codes):
    members, levels, rows, columns = zonal.shape
    step = 8 if members % 8 == 0 else 1
    field = pl.BlockSpec((step, levels, rows, columns), lambda at: (at, 0, 0, 0))
    return pl.pallas_call(
        message_kernel,
        grid=(members // step,),
        in_specs=[
            pl.BlockSpec(memory_space=pltpu.SMEM),
            pl.BlockSpec(memory_space=pltpu.SMEM),
            field,
            field,
            pl.BlockSpec((levels, rows, columns), lambda at: (0, 0, 0)),
            pl.BlockSpec((rows, columns), lambda at: (0, 0)),
        ],
        out_specs=pl.BlockSpec((step, 24, columns), lambda at: (at, 0, 0)),
        out_shape=jax.ShapeDtypeStruct((members, 24, columns), jnp.int32),
        compiler_params=pltpu.CompilerParams(vmem_limit_bytes=8 << 20),
    )(thickness, codes, zonal, meridional, fraction, land_mask)


def reversed_rows(values):
    groups = values.shape[0] // 8
    index = 7 - lax.broadcasted_iota(jnp.int32, (8, values.shape[1]), 0)
    pieces = [
        jnp.take_along_axis(
            values[8 * at : 8 * at + 8], index, axis=0, mode="promise_in_bounds"
        )
        for at in reversed(range(groups))
    ]
    return jnp.concatenate(pieces, axis=0)


def reversed_lanes(values):
    columns = values.shape[1]
    index = columns - 1 - lax.broadcasted_iota(jnp.int32, values.shape, 1)
    return jnp.take_along_axis(values, index, axis=1, mode="promise_in_bounds")


def cg_kernel(
    thickness_ref,
    got_ref,
    out_ref,
    field_ref,
    image_ref,
    east_ref,
    west_ref,
    north_ref,
    south_ref,
    total_ref,
    side_ref,
    turned_ref,
    ends_ref,
    surface_ref,
    residual_ref,
):
    tiles, rows, columns = image_ref.shape
    levels = thickness_ref.shape[0]
    lane = lax.broadcasted_iota(jnp.int32, (rows, columns), 1)
    row = lax.broadcasted_iota(jnp.int32, (rows, columns), 0)
    near = lax.broadcasted_iota(jnp.int32, (8, columns), 0)
    chunk = min(CHUNK, tiles)

    def over_tiles(body, carry):
        def some(base, inner):
            rolled = {}
            for step in range(chunk):
                inner = body(base, step, rolled, inner)
            return inner

        if tiles == chunk:
            return some(0, carry)
        return lax.fori_loop(0, tiles // chunk, lambda at, inner: some(at * chunk, inner), carry)

    def shift(base, by):
        if isinstance(base, int):
            return (base + by) % tiles
        return lax.rem(base + by + tiles, tiles)

    def first_row(tile):
        at = tile * rows + 8
        return at if isinstance(at, int) else pl.multiple_of(at, 8)

    def field(tile, by=0):
        return field_ref[pl.ds(first_row(tile) + by, rows), :]

    def turned(base, step, rolled, by):
        key = (step, by)
        if key not in rolled:
            rolled[key] = pltpu.roll(field(shift(base, step)), by, 1)
        return rolled[key]

    def flips(tile, one, other, mask):
        code = jnp.where(mask, 1 << (23 + one), 1 << (23 + other))
        return (got_ref[tile, 12:13, :] & code) != 0

    def flip_sides(tile):
        return flips(tile, 0, 1, lane >= columns // 2)

    def flip_ends(tile):
        return flips(tile, 2, 3, near == 7)

    def neighbours(base, step, rolled):
        tile = shift(base, step)
        own = field(tile)
        east = turned(base, step, rolled, columns - 1)
        west = turned(base, step, rolled, 1)
        side = jnp.where(
            lane >= columns // 2,
            turned(base, step + 1, rolled, columns - 1),
            turned(base, step - 1, rolled, 1),
        )
        ends = jnp.where(
            near == 7,
            field_ref[pl.ds(first_row(shift(base, step + NTX)), 1), :],
            field_ref[pl.ds(first_row(shift(base, step - NTX)) + rows - 1, 1), :],
        )
        ends = jnp.where(flip_ends(tile), reversed_lanes(ends), ends)
        return own, east, west, field(tile, 1), field(tile, -1), side, reversed_rows(side), ends

    levels_sum = sum_of(thickness_ref, levels)
    padding = jnp.zeros((8, columns), jnp.float32)
    field_ref[0:8, :] = padding
    field_ref[tiles * rows + 8 : tiles * rows + 16, :] = padding

    def read_depth(base, step, rolled, carry):
        tile = shift(base, step)
        pairs = got_ref[tile, 16:24, :]
        upper = lax.shift_left(pairs & 0xFFFF, 4)
        lower = lax.shift_left(lax.shift_right_logical(pairs, 16), 4)
        upper = upper | lax.shift_right_logical(got_ref[tile, 14:15, :], 4 * near) & 15
        lower = lower | lax.shift_right_logical(got_ref[tile, 15:16, :], 4 * near) & 15
        steps = jnp.concatenate([upper, lower], axis=0).astype(jnp.float32)
        field_ref[pl.ds(first_row(tile), rows), :] = jnp.sqrt(steps * (levels_sum / STEPS))
        return carry

    over_tiles(read_depth, 0)

    def weights(base, step, rolled, carry):
        tile = shift(base, step)
        own, east, west, north, south, side, side_turned, ends = neighbours(base, step, rolled)
        own = coupling_coef * own
        east = jnp.where(lane == columns - 1, 0.0, own * east)
        west = jnp.where(lane == 0, 0.0, own * west)
        north = jnp.where(row == rows - 1, 0.0, own * north)
        south = jnp.where(row == 0, 0.0, own * south)
        edge = jnp.logical_or(lane == 0, lane == columns - 1)
        side = jnp.where(edge, own * jnp.where(flip_sides(tile), side_turned, side), 0.0)
        upper = jnp.where(near == 0, own[0:8] * ends, 0.0)
        lower = jnp.where(near == 7, own[rows - 8 : rows] * ends, 0.0)
        east_ref[tile], west_ref[tile], north_ref[tile], south_ref[tile] = east, west, north, south
        side_ref[tile] = jnp.where(flip_sides(tile), 0.0, side)
        turned_ref[tile] = jnp.where(flip_sides(tile), side, 0.0)
        both = jnp.concatenate([upper, lower], axis=0)
        ends_ref[tile] = both
        total_ref[tile] = 1.0 + ((east + west) + (north + south)) + (side + both)
        return carry

    over_tiles(weights, 0)

    def begin(base, step, rolled, norm):
        def read(by):
            key = by % tiles
            if key not in rolled:
                other = shift(base, by)
                rolled[key] = unpacked(got_ref[other, 0:8, :], got_ref[other, 8:16, :])
            return rolled[key]

        def edge_of(by, at):
            steps = got_ref[shift(base, by), at : at + 1, :] & 0x7FFFFF
            return (steps.astype(jnp.float32) - MIDDLE) * read(by)[2]

        tile = shift(base, step)
        wet = field(tile) > 0.0
        upper, lower, _ = read(step)
        value = jnp.concatenate([upper, lower], axis=0)
        target = jnp.where(flip_sides(tile)[:, columns - 1 : columns], rows - 1 - row, row)
        edge = jnp.where(lane == target, edge_of(step + 1, 13), 0.0)
        edge = jnp.sum(edge, axis=1, keepdims=True)
        end = jnp.broadcast_to(edge_of(step + NTX, 12), (8, columns))
        end = jnp.where(flip_ends(tile), reversed_lanes(end), end)
        end = jnp.concatenate([end] * (rows // 8), axis=0)
        value = value - jnp.where(lane == columns - 1, edge, 0.0)
        value = value - jnp.where(row == rows - 1, end, 0.0)
        value = jnp.where(wet, value, 0.0)
        residual_ref[tile] = value
        surface_ref[tile] = jnp.zeros_like(value)
        return norm + value * value

    def all_of(total):
        return jnp.sum(total, keepdims=True)

    zero = jnp.zeros((rows, columns), jnp.float32)

    def iteration(_, state):
        norm, ratio = state

        def turn(base, step, rolled, carry):
            tile = shift(base, step)
            field_ref[pl.ds(first_row(tile), rows), :] = residual_ref[tile] + ratio * field(tile)
            return carry

        over_tiles(turn, 0)

        def apply(base, step, rolled, total):
            tile = shift(base, step)
            own, east, west, north, south, side, side_turned, ends = neighbours(base, step, rolled)
            others = (
                (east_ref[tile] * east + west_ref[tile] * west)
                + (north_ref[tile] * north + south_ref[tile] * south)
                + (side_ref[tile] * side + turned_ref[tile] * side_turned)
                + ends_ref[tile] * jnp.concatenate([ends] * (rows // 8), axis=0)
            )
            image = total_ref[tile] * own - others
            image_ref[tile] = image
            return total + own * image

        step_size = norm / all_of(over_tiles(apply, zero))

        def advance(base, step, rolled, total):
            tile = shift(base, step)
            surface_ref[tile] = surface_ref[tile] + step_size * field(tile)
            residual = residual_ref[tile] - step_size * image_ref[tile]
            residual_ref[tile] = residual
            return total + residual * residual

        later = all_of(over_tiles(advance, zero))
        return later, later / norm

    norm = all_of(over_tiles(begin, zero))
    lax.fori_loop(0, ITERS, iteration, (norm, jnp.zeros_like(norm)))

    def finish(base, step, rolled, carry):
        tile = shift(base, step)
        rests = []
        for at, ref in ((0, surface_ref), (16, residual_ref)):
            upper, lower = ref[tile, 0:8], ref[tile, 8:16]
            exponent = exponent_for(jnp.maximum(jnp.abs(upper), jnp.abs(lower)))
            words, rest = packed(upper, lower, exponent, gain_of(exponent))
            out_ref[tile, at : at + 8] = words
            rests.append(rest)
        out_ref[tile, 8:16] = jnp.where(near < 4, rests[0], pltpu.roll(rests[1], 4, 0))
        return carry

    over_tiles(finish, 0)


def cg_of(got, thickness, rows):
    tiles, _, columns = got.shape
    field = pltpu.VMEM((tiles, rows, columns), jnp.float32)
    return pl.pallas_call(
        cg_kernel,
        in_specs=[
            pl.BlockSpec(memory_space=pltpu.SMEM),
            pl.BlockSpec(memory_space=pltpu.VMEM),
        ],
        out_specs=pl.BlockSpec(memory_space=pltpu.VMEM),
        out_shape=jax.ShapeDtypeStruct(got.shape, jnp.int32),
        scratch_shapes=[pltpu.VMEM((tiles * rows + 16, columns), jnp.float32)] + [field] * 11,
        compiler_params=pltpu.CompilerParams(
            vmem_limit_bytes=(4 << 20) + 16 * tiles * rows * columns * 4
        ),
    )(thickness, got)


def home_kernel(home_ref, surface_ref, residual_ref):
    for member in range(home_ref.shape[0]):
        rest = home_ref[member, 8:16]
        upper, lower, _ = unpacked(home_ref[member, 0:8], rest)
        surface_ref[member, 0:8] = upper
        surface_ref[member, 8:16] = lower
        upper, lower, _ = unpacked(home_ref[member, 16:24], pltpu.roll(rest, 4, 0))
        residual_ref[member, 0:8] = upper
        residual_ref[member, 8:16] = lower


def home_of(home, members, rows):
    columns = home.shape[2]
    step = 8 if members % 8 == 0 else 1
    result = jax.ShapeDtypeStruct((members, rows, columns), jnp.float32)
    return pl.pallas_call(
        home_kernel,
        grid=(members // step,),
        in_specs=[pl.BlockSpec((step,) + home.shape[1:], lambda at: (at, 0, 0))],
        out_specs=[pl.BlockSpec((step, rows, columns), lambda at: (at, 0, 0))] * 2,
        out_shape=[result, result],
        compiler_params=pltpu.CompilerParams(vmem_limit_bytes=8 << 20),
    )(home)


def on_device(zonal, meridional, fraction, thickness, land_mask, edge_codes):
    tiles = lax.axis_size("tile")
    members, _, rows, columns = zonal.shape
    message = message_of(zonal, meridional, fraction, thickness, land_mask, edge_codes)
    if tiles > members:
        message = jnp.pad(message, ((0, tiles - members), (0, 0), (0, 0)))
    got = lax.all_to_all(message, "tile", split_axis=0, concat_axis=0, tiled=True)
    back = cg_of(got, thickness, rows)
    home = lax.all_to_all(back, "tile", split_axis=0, concat_axis=0, tiled=True)
    return tuple(home_of(home, members, rows))


def solution(mesh):
    in_specs = (
        P(None, None, "tile", None),
        P(None, None, "tile", None),
        P(None, "tile", None),
        P(),
        P("tile", None),
        P("tile", None),
    )
    out_specs = (P(None, "tile", None), P(None, "tile", None))
    return jax.shard_map(
        on_device, mesh=mesh, in_specs=in_specs, out_specs=out_specs, check_vma=False
    )
```

```python
import functools

import jax
import jax.numpy as jnp
from jax import lax
from jax.experimental import pallas as pl
from jax.experimental.pallas import tpu as pltpu
from jax.sharding import PartitionSpec as P

NTX = 16
ITERS = 4
CHUNK = 8
STEPS = 1048575.0
MIDDLE = 4194304.0

coupling_coef = 0.25


def power_of_two(exponent):
    power = lax.shift_left(jnp.ones_like(exponent), exponent & 15).astype(jnp.float32)
    for bit in (16, 32, 64):
        power = jnp.where((exponent & bit) != 0, power * 2.0**bit, power)
    return power


def exponent_for(largest):
    for by in (4, 2, 1):
        largest = jnp.maximum(largest, pltpu.roll(largest, by, 0))
    log = jnp.log(jnp.maximum(largest, 2.0**-90)) * 1.4426950408889634
    return jnp.clip(jnp.floor(log + 0.01).astype(jnp.int32) + 97, 0, 127)


def steps_of(values, gain):
    shifted = jnp.minimum(values * gain + 3.0 * MIDDLE, 4.0 * MIDDLE - 1.0)
    return shifted.astype(jnp.int32) - int(2.0 * MIDDLE)


def packed(upper, lower, exponent, gain):
    upper = steps_of(upper, gain)
    lower = steps_of(lower, gain)
    words = upper | lax.shift_left(lower, 23)
    high = lax.shift_right_logical(lower, 9)
    sub = lax.broadcasted_iota(jnp.int32, high.shape, 0)
    part = lax.shift_right_logical(exponent, 4 * sub) & 15
    rest = high | lax.shift_left(pltpu.roll(high, 4, 0), 14) | lax.shift_left(part, 28)
    return words, rest


def gain_of(exponent):
    return power_of_two(127 - exponent) * 2.0**-9


def unpacked(words, rest):
    sub = lax.broadcasted_iota(jnp.int32, words.shape, 0)
    part = lax.shift_right_logical(rest, 28)
    exponent = part[0:1] + 16 * part[1:2]
    step = power_of_two(exponent) * 2.0**-118
    upper = words & 0x7FFFFF
    high = jnp.where(sub < 4, rest, pltpu.roll(lax.shift_right_logical(rest, 14), 4, 0)) & 0x3FFF
    lower = lax.shift_right_logical(words, 23) | lax.shift_left(high, 9)
    return (
        (upper.astype(jnp.float32) - MIDDLE) * step,
        (lower.astype(jnp.float32) - MIDDLE) * step,
        step,
    )


def message_kernel(
    thickness_ref,
    codes_ref,
    zonal_hbm,
    meridional_hbm,
    fraction_hbm,
    land_hbm,
    out_hbm,
    zonal_ref,
    meridional_ref,
    fraction_ref,
    land_ref,
    out_ref,
    in_sems,
    out_sems,
):
    members, levels, rows, columns = zonal_ref.shape
    group = members // out_sems.shape[0]

    def copies_in(at):
        part = pl.ds(at * group, group)
        return (
            pltpu.make_async_copy(zonal_hbm.at[part], zonal_ref.at[part], in_sems.at[0, at]),
            pltpu.make_async_copy(
                meridional_hbm.at[part], meridional_ref.at[part], in_sems.at[1, at]
            ),
        )

    def copy_out(at):
        part = pl.ds(at * group, group)
        return pltpu.make_async_copy(out_ref.at[part], out_hbm.at[part], out_sems.at[at])

    land_copy = pltpu.make_async_copy(land_hbm, land_ref, in_sems.at[2, 0])
    fraction_copy = pltpu.make_async_copy(fraction_hbm, fraction_ref, in_sems.at[2, 1])
    fraction_copy.start()
    land_copy.start()
    for at in range(members // group):
        for copy in copies_in(at):
            copy.start()
    fraction_copy.wait()
    land_copy.wait()
    lane = lax.broadcasted_iota(jnp.int32, (rows, columns), 1)
    row = lax.broadcasted_iota(jnp.int32, (rows, columns), 0)
    place = lax.broadcasted_iota(jnp.int32, (8, columns), 0)
    code = [jnp.where(codes_ref[0, side] == 1, 1 << (23 + side), 0) for side in range(4)]
    flags = (code[0] + code[1]) + (code[2] + code[3])
    parts = [
        thickness_ref[level] * fraction_ref[level].astype(jnp.float32) for level in range(levels)
    ]
    depth = functools.reduce(lambda one, other: one + other, parts)
    scale = STEPS / sum_of(thickness_ref, levels)
    steps = jnp.where(land_ref[...] == 1, depth * scale + 0.5, 0.0).astype(jnp.int32)
    upper, lower = steps[0:8], steps[8:16]
    pairs = lax.shift_right_logical(upper, 4) | lax.shift_left(
        lax.shift_right_logical(lower, 4), 16
    )

    def gathered(values):
        values = lax.shift_left(values & 15, 4 * place)
        for by in (4, 2, 1):
            values = values | pltpu.roll(values, by, 0)
        return values

    low = jnp.where(place == 6, gathered(upper), gathered(lower))

    def one(member):
        along = parts[0] * zonal_ref[member, 0].astype(jnp.float32)
        across = parts[0] * meridional_ref[member, 0].astype(jnp.float32)
        for level in range(1, levels):
            along = along + parts[level] * zonal_ref[member, level].astype(jnp.float32)
            across = across + parts[level] * meridional_ref[member, level].astype(jnp.float32)
        east = jnp.where(lane == columns - 1, 0.0, pltpu.roll(along, columns - 1, 1))
        north = jnp.where(row == rows - 1, 0.0, pltpu.roll(across, rows - 1, 0))
        value = along - east + across - north
        first = jnp.where(lane == row, along[:, 0:1], 0.0)
        first = first[0:8] + first[8:16]
        for by in (4, 2, 1):
            first = first + pltpu.roll(first, by, 0)
        edges = jnp.where(place == 5, first, across[0:1])
        largest = jnp.maximum(jnp.abs(value[0:8]), jnp.abs(value[8:16]))
        exponent = exponent_for(jnp.maximum(largest, jnp.abs(edges)))
        gain = gain_of(exponent)
        words, rest = packed(value[0:8], value[8:16], exponent, gain)
        edges = steps_of(edges, gain) | flags
        out_ref[member, 0:8] = words
        out_ref[member, 8:16] = jnp.where(place < 4, rest, jnp.where(place < 6, edges, low))
        out_ref[member, 16:24] = pairs

    def some(at, carry):
        for copy in copies_in(at):
            copy.wait()
        for member in range(group):
            one(at * group + member)
        copy_out(at).start()
        return carry

    lax.fori_loop(0, members // group, some, 0)
    for at in range(members // group):
        copy_out(at).wait()


def sum_of(thickness_ref, levels):
    whole = thickness_ref[0]
    for level in range(1, levels):
        whole = whole + thickness_ref[level]
    return whole


def message_of(zonal, meridional, fraction, thickness, land_mask, codes):
    members, _, _, columns = zonal.shape
    group = 8 if members % 8 == 0 else 1
    return pl.pallas_call(
        message_kernel,
        in_specs=[pl.BlockSpec(memory_space=pltpu.SMEM)] * 2
        + [pl.BlockSpec(memory_space=pl.ANY)] * 4,
        out_specs=pl.BlockSpec(memory_space=pl.ANY),
        out_shape=jax.ShapeDtypeStruct((members, 24, columns), jnp.int32),
        scratch_shapes=[
            pltpu.VMEM(zonal.shape, zonal.dtype),
            pltpu.VMEM(meridional.shape, meridional.dtype),
            pltpu.VMEM(fraction.shape, fraction.dtype),
            pltpu.VMEM(land_mask.shape, land_mask.dtype),
            pltpu.VMEM((members, 24, columns), jnp.int32),
            pltpu.SemaphoreType.DMA((3, max(2, members // group))),
            pltpu.SemaphoreType.DMA((members // group,)),
        ],
        compiler_params=pltpu.CompilerParams(vmem_limit_bytes=60 << 20),
    )(thickness, codes, zonal, meridional, fraction, land_mask)


def reversed_rows(values):
    groups = values.shape[0] // 8
    index = 7 - lax.broadcasted_iota(jnp.int32, (8, values.shape[1]), 0)
    pieces = [
        jnp.take_along_axis(
            values[8 * at : 8 * at + 8], index, axis=0, mode="promise_in_bounds"
        )
        for at in reversed(range(groups))
    ]
    return jnp.concatenate(pieces, axis=0)


def reversed_lanes(values):
    columns = values.shape[1]
    index = columns - 1 - lax.broadcasted_iota(jnp.int32, values.shape, 1)
    return jnp.take_along_axis(values, index, axis=1, mode="promise_in_bounds")


def cg_kernel(
    thickness_ref,
    got_ref,
    out_ref,
    field_ref,
    image_ref,
    east_ref,
    west_ref,
    north_ref,
    south_ref,
    total_ref,
    side_ref,
    turned_ref,
    ends_ref,
    surface_ref,
    residual_ref,
):
    tiles, rows, columns = image_ref.shape
    levels = thickness_ref.shape[0]
    lane = lax.broadcasted_iota(jnp.int32, (rows, columns), 1)
    row = lax.broadcasted_iota(jnp.int32, (rows, columns), 0)
    near = lax.broadcasted_iota(jnp.int32, (8, columns), 0)
    chunk = min(CHUNK, tiles)

    def over_tiles(body, carry):
        def some(base, inner):
            rolled = {}
            for step in range(chunk):
                inner = body(base, step, rolled, inner)
            return inner

        if tiles == chunk:
            return some(0, carry)
        return lax.fori_loop(0, tiles // chunk, lambda at, inner: some(at * chunk, inner), carry)

    def shift(base, by):
        if isinstance(base, int):
            return (base + by) % tiles
        return lax.rem(base + by + tiles, tiles)

    def first_row(tile):
        at = tile * rows + 8
        return at if isinstance(at, int) else pl.multiple_of(at, 8)

    def field(tile, by=0):
        return field_ref[pl.ds(first_row(tile) + by, rows), :]

    def turned(base, step, rolled, by):
        key = (step, by)
        if key not in rolled:
            rolled[key] = pltpu.roll(field(shift(base, step)), by, 1)
        return rolled[key]

    def flips(tile, one, other, mask):
        code = jnp.where(mask, 1 << (23 + one), 1 << (23 + other))
        return (got_ref[tile, 12:13, :] & code) != 0

    def flip_sides(tile):
        return flips(tile, 0, 1, lane >= columns // 2)

    def flip_ends(tile):
        return flips(tile, 2, 3, near == 7)

    def neighbours(base, step, rolled):
        tile = shift(base, step)
        own = field(tile)
        east = turned(base, step, rolled, columns - 1)
        west = turned(base, step, rolled, 1)
        side = jnp.where(
            lane >= columns // 2,
            turned(base, step + 1, rolled, columns - 1),
            turned(base, step - 1, rolled, 1),
        )
        ends = jnp.where(
            near == 7,
            field_ref[pl.ds(first_row(shift(base, step + NTX)), 1), :],
            field_ref[pl.ds(first_row(shift(base, step - NTX)) + rows - 1, 1), :],
        )
        ends = jnp.where(flip_ends(tile), reversed_lanes(ends), ends)
        return own, east, west, field(tile, 1), field(tile, -1), side, reversed_rows(side), ends

    levels_sum = sum_of(thickness_ref, levels)
    padding = jnp.zeros((8, columns), jnp.float32)
    field_ref[0:8, :] = padding
    field_ref[tiles * rows + 8 : tiles * rows + 16, :] = padding

    def read_depth(base, step, rolled, carry):
        tile = shift(base, step)
        pairs = got_ref[tile, 16:24, :]
        upper = lax.shift_left(pairs & 0xFFFF, 4)
        lower = lax.shift_left(lax.shift_right_logical(pairs, 16), 4)
        upper = upper | lax.shift_right_logical(got_ref[tile, 14:15, :], 4 * near) & 15
        lower = lower | lax.shift_right_logical(got_ref[tile, 15:16, :], 4 * near) & 15
        steps = jnp.concatenate([upper, lower], axis=0).astype(jnp.float32)
        field_ref[pl.ds(first_row(tile), rows), :] = jnp.sqrt(steps * (levels_sum / STEPS))
        return carry

    over_tiles(read_depth, 0)

    def weights(base, step, rolled, carry):
        tile = shift(base, step)
        own, east, west, north, south, side, side_turned, ends = neighbours(base, step, rolled)
        own = coupling_coef * own
        east = jnp.where(lane == columns - 1, 0.0, own * east)
        west = jnp.where(lane == 0, 0.0, own * west)
        north = jnp.where(row == rows - 1, 0.0, own * north)
        south = jnp.where(row == 0, 0.0, own * south)
        edge = jnp.logical_or(lane == 0, lane == columns - 1)
        side = jnp.where(edge, own * jnp.where(flip_sides(tile), side_turned, side), 0.0)
        upper = jnp.where(near == 0, own[0:8] * ends, 0.0)
        lower = jnp.where(near == 7, own[rows - 8 : rows] * ends, 0.0)
        east_ref[tile], west_ref[tile], north_ref[tile], south_ref[tile] = east, west, north, south
        side_ref[tile] = jnp.where(flip_sides(tile), 0.0, side)
        turned_ref[tile] = jnp.where(flip_sides(tile), side, 0.0)
        both = jnp.concatenate([upper, lower], axis=0)
        ends_ref[tile] = both
        total_ref[tile] = 1.0 + ((east + west) + (north + south)) + (side + both)
        return carry

    over_tiles(weights, 0)

    def begin(base, step, rolled, norm):
        def read(by):
            key = by % tiles
            if key not in rolled:
                other = shift(base, by)
                rolled[key] = unpacked(got_ref[other, 0:8, :], got_ref[other, 8:16, :])
            return rolled[key]

        def edge_of(by, at):
            steps = got_ref[shift(base, by), at : at + 1, :] & 0x7FFFFF
            return (steps.astype(jnp.float32) - MIDDLE) * read(by)[2]

        tile = shift(base, step)
        wet = field(tile) > 0.0
        upper, lower, _ = read(step)
        value = jnp.concatenate([upper, lower], axis=0)
        target = jnp.where(flip_sides(tile)[:, columns - 1 : columns], rows - 1 - row, row)
        edge = jnp.where(lane == target, edge_of(step + 1, 13), 0.0)
        edge = jnp.sum(edge, axis=1, keepdims=True)
        end = jnp.broadcast_to(edge_of(step + NTX, 12), (8, columns))
        end = jnp.where(flip_ends(tile), reversed_lanes(end), end)
        end = jnp.concatenate([end] * (rows // 8), axis=0)
        value = value - jnp.where(lane == columns - 1, edge, 0.0)
        value = value - jnp.where(row == rows - 1, end, 0.0)
        value = jnp.where(wet, value, 0.0)
        residual_ref[tile] = value
        surface_ref[tile] = jnp.zeros_like(value)
        return norm + value * value

    def all_of(total):
        return jnp.sum(total, keepdims=True)

    zero = jnp.zeros((rows, columns), jnp.float32)

    def iteration(_, state):
        norm, ratio = state

        def turn(base, step, rolled, carry):
            tile = shift(base, step)
            field_ref[pl.ds(first_row(tile), rows), :] = residual_ref[tile] + ratio * field(tile)
            return carry

        over_tiles(turn, 0)

        def apply(base, step, rolled, total):
            tile = shift(base, step)
            own, east, west, north, south, side, side_turned, ends = neighbours(base, step, rolled)
            others = (
                (east_ref[tile] * east + west_ref[tile] * west)
                + (north_ref[tile] * north + south_ref[tile] * south)
                + (side_ref[tile] * side + turned_ref[tile] * side_turned)
                + ends_ref[tile] * jnp.concatenate([ends] * (rows // 8), axis=0)
            )
            image = total_ref[tile] * own - others
            image_ref[tile] = image
            return total + own * image

        step_size = norm / all_of(over_tiles(apply, zero))

        def advance(base, step, rolled, total):
            tile = shift(base, step)
            surface_ref[tile] = surface_ref[tile] + step_size * field(tile)
            residual = residual_ref[tile] - step_size * image_ref[tile]
            residual_ref[tile] = residual
            return total + residual * residual

        later = all_of(over_tiles(advance, zero))
        return later, later / norm

    norm = all_of(over_tiles(begin, zero))
    lax.fori_loop(0, ITERS, iteration, (norm, jnp.zeros_like(norm)))

    def finish(base, step, rolled, carry):
        tile = shift(base, step)
        rests = []
        for at, ref in ((0, surface_ref), (16, residual_ref)):
            upper, lower = ref[tile, 0:8], ref[tile, 8:16]
            exponent = exponent_for(jnp.maximum(jnp.abs(upper), jnp.abs(lower)))
            words, rest = packed(upper, lower, exponent, gain_of(exponent))
            out_ref[tile, at : at + 8] = words
            rests.append(rest)
        out_ref[tile, 8:16] = jnp.where(near < 4, rests[0], pltpu.roll(rests[1], 4, 0))
        return carry

    over_tiles(finish, 0)


def cg_of(got, thickness, rows):
    tiles, _, columns = got.shape
    field = pltpu.VMEM((tiles, rows, columns), jnp.float32)
    return pl.pallas_call(
        cg_kernel,
        in_specs=[
            pl.BlockSpec(memory_space=pltpu.SMEM),
            pl.BlockSpec(memory_space=pltpu.VMEM),
        ],
        out_specs=pl.BlockSpec(memory_space=pltpu.VMEM),
        out_shape=jax.ShapeDtypeStruct(got.shape, jnp.int32),
        scratch_shapes=[pltpu.VMEM((tiles * rows + 16, columns), jnp.float32)] + [field] * 11,
        compiler_params=pltpu.CompilerParams(
            vmem_limit_bytes=(4 << 20) + 16 * tiles * rows * columns * 4
        ),
    )(thickness, got)


def home_kernel(home_ref, surface_ref, residual_ref):
    for member in range(home_ref.shape[0]):
        rest = home_ref[member, 8:16]
        upper, lower, _ = unpacked(home_ref[member, 0:8], rest)
        surface_ref[member, 0:8] = upper
        surface_ref[member, 8:16] = lower
        upper, lower, _ = unpacked(home_ref[member, 16:24], pltpu.roll(rest, 4, 0))
        residual_ref[member, 0:8] = upper
        residual_ref[member, 8:16] = lower


def home_of(home, members, rows):
    columns = home.shape[2]
    step = 16 if members % 16 == 0 else 1
    result = jax.ShapeDtypeStruct((members, rows, columns), jnp.float32)
    return pl.pallas_call(
        home_kernel,
        grid=(members // step,),
        in_specs=[pl.BlockSpec((step,) + home.shape[1:], lambda at: (at, 0, 0))],
        out_specs=[pl.BlockSpec((step, rows, columns), lambda at: (at, 0, 0))] * 2,
        out_shape=[result, result],
        compiler_params=pltpu.CompilerParams(vmem_limit_bytes=8 << 20),
    )(home)


def on_device(zonal, meridional, fraction, thickness, land_mask, edge_codes):
    tiles = lax.axis_size("tile")
    members, _, rows, columns = zonal.shape
    message = message_of(zonal, meridional, fraction, thickness, land_mask, edge_codes)
    if tiles > members:
        message = jnp.pad(message, ((0, tiles - members), (0, 0), (0, 0)))
    got = lax.all_to_all(message, "tile", split_axis=0, concat_axis=0, tiled=True)
    back = cg_of(got, thickness, rows)
    home = lax.all_to_all(back, "tile", split_axis=0, concat_axis=0, tiled=True)
    return tuple(home_of(home, members, rows))


def solution(mesh):
    in_specs = (
        P(None, None, "tile", None),
        P(None, None, "tile", None),
        P(None, "tile", None),
        P(),
        P("tile", None),
        P("tile", None),
    )
    out_specs = (P(None, "tile", None), P(None, "tile", None))
    return jax.shard_map(
        on_device, mesh=mesh, in_specs=in_specs, out_specs=out_specs, check_vma=False
    )
```

```python
import functools

import jax
import jax.numpy as jnp
from jax import lax
from jax.experimental import pallas as pl
from jax.experimental.pallas import tpu as pltpu
from jax.sharding import PartitionSpec as P

NTX = 16
ITERS = 4
CHUNK = 32
BITS = 18
STEPS = 2.0**BITS - 1.0
MIDDLE = 2.0 ** (BITS - 1)
ROUNDING = 2.0**23
PIECES = 5

coupling_coef = 0.25


def power_of_two(exponent):
    power = lax.shift_left(jnp.ones_like(exponent), exponent & 15).astype(jnp.float32)
    for bit in (16, 32, 64):
        power = jnp.where((exponent & bit) != 0, power * 2.0**bit, power)
    return power


def exponent_for(largest):
    for by in (4, 2, 1):
        largest = jnp.maximum(largest, pltpu.roll(largest, by, 0))
    log = jnp.log(jnp.maximum(largest, 2.0**-90)) * 1.4426950408889634
    return jnp.clip(jnp.floor(log + 0.01).astype(jnp.int32) + 97, 0, 127)


def steps_of(values, gain):
    shifted = values * gain + (ROUNDING + MIDDLE)
    return jnp.minimum(shifted, ROUNDING + STEPS).astype(jnp.int32) - int(ROUNDING)


def gain_of(exponent):
    return power_of_two(127 - exponent) * 2.0 ** (96 - 127 + BITS - 1)


def gathered(values):
    sub = lax.broadcasted_iota(jnp.int32, values.shape, 0)
    values = lax.shift_left(values & 15, 4 * sub)
    for by in (4, 2, 1):
        values = values | pltpu.roll(values, by, 0)
    return values


def packed(upper, lower):
    words = upper | lax.shift_left(lower, BITS)
    return words, gathered(lax.shift_right_logical(lower, BITS - 4))


def unpacked(words, high):
    sub = lax.broadcasted_iota(jnp.int32, words.shape, 0)
    upper = words & ((1 << BITS) - 1)
    high = lax.shift_right_logical(jnp.broadcast_to(high, words.shape), 4 * sub) & 15
    return upper, lax.shift_right_logical(words, BITS) | lax.shift_left(high, BITS - 4)


def step_of(exponent):
    return power_of_two(exponent) * 2.0 ** (-96 - (BITS - 1))


def values_of(steps, step):
    return (steps.astype(jnp.float32) - MIDDLE) * step


def eight(ref, at, piece):
    return jnp.concatenate([ref[at, piece], ref[at, piece + 1]], axis=0)


def put_eight(ref, at, piece, values):
    ref[at, piece] = values[0:4]
    ref[at, piece + 1] = values[4:8]


def message_kernel(
    thickness_ref,
    codes_ref,
    zonal_hbm,
    meridional_hbm,
    fraction_hbm,
    land_hbm,
    out_hbm,
    zonal_ref,
    meridional_ref,
    fraction_ref,
    land_ref,
    out_ref,
    in_sems,
    out_sems,
):
    members, levels, rows, columns = zonal_ref.shape
    group = members // out_sems.shape[0]

    def copies_in(at):
        part = pl.ds(at * group, group)
        return (
            pltpu.make_async_copy(zonal_hbm.at[part], zonal_ref.at[part], in_sems.at[0, at]),
            pltpu.make_async_copy(
                meridional_hbm.at[part], meridional_ref.at[part], in_sems.at[1, at]
            ),
        )

    def copy_out(at):
        part = pl.ds(at * group, group)
        return pltpu.make_async_copy(out_ref.at[part], out_hbm.at[part], out_sems.at[at])

    land_copy = pltpu.make_async_copy(land_hbm, land_ref, in_sems.at[2, 0])
    fraction_copy = pltpu.make_async_copy(fraction_hbm, fraction_ref, in_sems.at[2, 1])
    fraction_copy.start()
    land_copy.start()
    for at in range(members // group):
        for copy in copies_in(at):
            copy.start()
    fraction_copy.wait()
    land_copy.wait()
    lane = lax.broadcasted_iota(jnp.int32, (rows, columns), 1)
    row = lax.broadcasted_iota(jnp.int32, (rows, columns), 0)
    place = lax.broadcasted_iota(jnp.int32, (8, columns), 0)
    code = [jnp.where(codes_ref[0, side] == 1, 1 << (BITS + side), 0) for side in range(4)]
    flags = (code[0] + code[1]) + (code[2] + code[3])
    parts = [
        thickness_ref[level] * fraction_ref[level].astype(jnp.float32) for level in range(levels)
    ]
    depth = functools.reduce(lambda one, other: one + other, parts)
    root = jnp.sqrt(depth * (1.0 / sum_of(thickness_ref, levels)))
    steps = jnp.where(land_ref[...] == 1, jnp.minimum(root * STEPS + 0.5, STEPS), 0.0)
    steps = steps.astype(jnp.int32)
    roots, roots_high = packed(steps[0:8], steps[8:16])

    def one(member):
        along = parts[0] * zonal_ref[member, 0].astype(jnp.float32)
        across = parts[0] * meridional_ref[member, 0].astype(jnp.float32)
        for level in range(1, levels):
            along = along + parts[level] * zonal_ref[member, level].astype(jnp.float32)
            across = across + parts[level] * meridional_ref[member, level].astype(jnp.float32)
        east = jnp.where(lane == columns - 1, 0.0, pltpu.roll(along, columns - 1, 1))
        north = jnp.where(row == rows - 1, 0.0, pltpu.roll(across, rows - 1, 0))
        value = along - east + across - north
        first = jnp.where(lane == row, along[:, 0:1], 0.0)
        first = first[0:8] + first[8:16]
        for by in (4, 2, 1):
            first = first + pltpu.roll(first, by, 0)
        edges = jnp.where(place == 3, first, across[0:1])
        largest = jnp.maximum(jnp.abs(value[0:8]), jnp.abs(value[8:16]))
        exponent = exponent_for(jnp.maximum(largest, jnp.abs(edges)))
        gain = gain_of(exponent)
        words, high = packed(steps_of(value[0:8], gain), steps_of(value[8:16], gain))
        edges = steps_of(edges, gain) | jnp.where(
            place == 3, lax.shift_left(exponent, BITS), flags
        )
        last = jnp.where(place == 0, high, jnp.where(place == 1, roots_high, edges))
        put_eight(out_ref, member, 0, words)
        put_eight(out_ref, member, 2, roots)
        out_ref[member, 4] = last[0:4]

    def some(at, carry):
        for copy in copies_in(at):
            copy.wait()
        for member in range(group):
            one(at * group + member)
        copy_out(at).start()
        return carry

    lax.fori_loop(0, members // group, some, 0)
    for at in range(members // group):
        copy_out(at).wait()


def sum_of(thickness_ref, levels):
    whole = thickness_ref[0]
    for level in range(1, levels):
        whole = whole + thickness_ref[level]
    return whole


def message_of(zonal, meridional, fraction, thickness, land_mask, codes):
    members, _, _, columns = zonal.shape
    group = 8 if members % 8 == 0 else 1
    return pl.pallas_call(
        message_kernel,
        in_specs=[pl.BlockSpec(memory_space=pltpu.SMEM)] * 2
        + [pl.BlockSpec(memory_space=pl.ANY)] * 4,
        out_specs=pl.BlockSpec(memory_space=pl.ANY),
        out_shape=jax.ShapeDtypeStruct((members, PIECES, 4, columns), jnp.int32),
        scratch_shapes=[
            pltpu.VMEM(zonal.shape, zonal.dtype),
            pltpu.VMEM(meridional.shape, meridional.dtype),
            pltpu.VMEM(fraction.shape, fraction.dtype),
            pltpu.VMEM(land_mask.shape, land_mask.dtype),
            pltpu.VMEM((members, PIECES, 4, columns), jnp.int32),
            pltpu.SemaphoreType.DMA((3, max(2, members // group))),
            pltpu.SemaphoreType.DMA((members // group,)),
        ],
        compiler_params=pltpu.CompilerParams(vmem_limit_bytes=60 << 20),
    )(thickness, codes, zonal, meridional, fraction, land_mask)


def reversed_rows(values):
    groups = values.shape[0] // 8
    index = 7 - lax.broadcasted_iota(jnp.int32, (8, values.shape[1]), 0)
    pieces = [
        jnp.take_along_axis(
            values[8 * at : 8 * at + 8], index, axis=0, mode="promise_in_bounds"
        )
        for at in reversed(range(groups))
    ]
    return jnp.concatenate(pieces, axis=0)


def reversed_lanes(values):
    columns = values.shape[1]
    index = columns - 1 - lax.broadcasted_iota(jnp.int32, values.shape, 1)
    return jnp.take_along_axis(values, index, axis=1, mode="promise_in_bounds")


def cg_kernel(
    thickness_ref,
    got_ref,
    out_ref,
    field_ref,
    image_ref,
    east_ref,
    west_ref,
    north_ref,
    south_ref,
    total_ref,
    direction_ref,
    product_ref,
    side_ref,
    turned_ref,
    ends_ref,
    surface_ref,
    residual_ref,
):
    tiles, rows, columns = image_ref.shape
    levels = thickness_ref.shape[0]
    lane = lax.broadcasted_iota(jnp.int32, (rows, columns), 1)
    row = lax.broadcasted_iota(jnp.int32, (rows, columns), 0)
    near = lax.broadcasted_iota(jnp.int32, (8, columns), 0)
    chunk = min(CHUNK, tiles)

    def over_tiles(body, carry):
        def some(base, inner):
            rolled = {}
            for step in range(chunk):
                inner = body(base, step, rolled, inner)
            return inner

        if tiles == chunk:
            return some(0, carry)
        return lax.fori_loop(0, tiles // chunk, lambda at, inner: some(at * chunk, inner), carry)

    def shift(base, by):
        if isinstance(base, int):
            return (base + by) % tiles
        return lax.rem(base + by + tiles, tiles)

    def first_row(tile):
        at = tile * rows + 8
        return at if isinstance(at, int) else pl.multiple_of(at, 8)

    def field(tile, by=0):
        return field_ref[pl.ds(first_row(tile) + by, rows), :]

    def turned(base, step, rolled, by):
        key = (step, by)
        if key not in rolled:
            rolled[key] = pltpu.roll(field(shift(base, step)), by, 1)
        return rolled[key]

    def flips(tile, one, other, mask):
        code = jnp.where(mask, 1 << (BITS + one), 1 << (BITS + other))
        return (got_ref[tile, 4, 2:3, :] & code) != 0

    def flip_sides(tile):
        return flips(tile, 0, 1, lane >= columns // 2)

    def flip_ends(tile):
        return flips(tile, 2, 3, near == 7)

    def neighbours(base, step, rolled):
        tile = shift(base, step)
        own = field(tile)
        east = turned(base, step, rolled, columns - 1)
        west = turned(base, step, rolled, 1)
        side = jnp.where(
            lane >= columns // 2,
            turned(base, step + 1, rolled, columns - 1),
            turned(base, step - 1, rolled, 1),
        )
        ends = jnp.where(
            near == 7,
            field_ref[pl.ds(first_row(shift(base, step + NTX)), 1), :],
            field_ref[pl.ds(first_row(shift(base, step - NTX)) + rows - 1, 1), :],
        )
        ends = jnp.where(flip_ends(tile), reversed_lanes(ends), ends)
        return own, east, west, field(tile, 1), field(tile, -1), side, reversed_rows(side), ends

    levels_sum = sum_of(thickness_ref, levels)
    padding = jnp.zeros((8, columns), jnp.float32)
    field_ref[0:8, :] = padding
    field_ref[tiles * rows + 8 : tiles * rows + 16, :] = padding

    def read_depth(base, step, rolled, carry):
        tile = shift(base, step)
        upper, lower = unpacked(eight(got_ref, tile, 2), got_ref[tile, 4, 1:2, :])
        steps = jnp.concatenate([upper, lower], axis=0).astype(jnp.float32)
        field_ref[pl.ds(first_row(tile), rows), :] = steps * (1.0 / STEPS)
        return carry

    over_tiles(read_depth, 0)

    def weights(base, step, rolled, carry):
        tile = shift(base, step)
        own, east, west, north, south, side, side_turned, ends = neighbours(base, step, rolled)
        own = (coupling_coef * levels_sum) * own
        east = jnp.where(lane == columns - 1, 0.0, own * east)
        west = jnp.where(lane == 0, 0.0, own * west)
        north = jnp.where(row == rows - 1, 0.0, own * north)
        south = jnp.where(row == 0, 0.0, own * south)
        edge = jnp.logical_or(lane == 0, lane == columns - 1)
        side = jnp.where(edge, own * jnp.where(flip_sides(tile), side_turned, side), 0.0)
        upper = jnp.where(near == 0, own[0:8] * ends, 0.0)
        lower = jnp.where(near == 7, own[rows - 8 : rows] * ends, 0.0)
        east_ref[tile], west_ref[tile], north_ref[tile], south_ref[tile] = east, west, north, south
        side_ref[tile] = jnp.where(flip_sides(tile), 0.0, side)
        turned_ref[tile] = jnp.where(flip_sides(tile), side, 0.0)
        both = jnp.concatenate([upper, lower], axis=0)
        ends_ref[tile] = both
        total_ref[tile] = 1.0 + ((east + west) + (north + south)) + (side + both)
        return carry

    over_tiles(weights, 0)

    def begin(base, step, rolled, carry):
        def step_at(by):
            key = by % tiles
            if key not in rolled:
                row_of = got_ref[shift(base, by), 4, 3:4, :]
                rolled[key] = step_of(lax.shift_right_logical(row_of, BITS))
            return rolled[key]

        def edge_of(by, at):
            steps = got_ref[shift(base, by), 4, at : at + 1, :] & ((1 << BITS) - 1)
            return values_of(steps, step_at(by))

        tile = shift(base, step)
        wet = field(tile) > 0.0
        upper, lower = unpacked(eight(got_ref, tile, 0), got_ref[tile, 4, 0:1, :])
        value = values_of(jnp.concatenate([upper, lower], axis=0), step_at(step))
        target = jnp.where(flip_sides(tile)[:, columns - 1 : columns], rows - 1 - row, row)
        edge = jnp.where(lane == target, edge_of(step + 1, 3), 0.0)
        edge = jnp.sum(edge, axis=1, keepdims=True)
        end = jnp.broadcast_to(edge_of(step + NTX, 2), (8, columns))
        end = jnp.where(flip_ends(tile), reversed_lanes(end), end)
        end = jnp.concatenate([end] * (rows // 8), axis=0)
        value = value - jnp.where(lane == columns - 1, edge, 0.0)
        value = value - jnp.where(row == rows - 1, end, 0.0)
        value = jnp.where(wet, value, 0.0)
        residual_ref[tile] = value
        return carry

    def all_of(total):
        return jnp.sum(total, keepdims=True)

    zero = jnp.zeros((rows, columns), jnp.float32)

    def apply(base, step, rolled, totals):
        tile = shift(base, step)
        own, east, west, north, south, side, side_turned, ends = neighbours(base, step, rolled)
        others = (
            (east_ref[tile] * east + west_ref[tile] * west)
            + (north_ref[tile] * north + south_ref[tile] * south)
            + (side_ref[tile] * side + turned_ref[tile] * side_turned)
            + ends_ref[tile] * jnp.concatenate([ends] * (rows // 8), axis=0)
        )
        image = total_ref[tile] * own - others
        image_ref[tile] = image
        return totals[0] + own * own, totals[1] + own * image

    def sums():
        squares, products = over_tiles(apply, (zero, zero))
        return all_of(squares), all_of(products)

    def copy_back(base, step, rolled, carry):
        tile = shift(base, step)
        field_ref[pl.ds(first_row(tile), rows), :] = residual_ref[tile]
        return carry

    over_tiles(begin, 0)
    over_tiles(copy_back, 0)

    norm, product = sums()
    size = norm / product

    def first(base, step, rolled, carry):
        tile = shift(base, step)
        own, image = field(tile), image_ref[tile]
        direction_ref[tile] = own
        product_ref[tile] = image
        surface_ref[tile] = size * own
        field_ref[pl.ds(first_row(tile), rows), :] = own - size * image
        return carry

    over_tiles(first, 0)

    def next_sizes(state):
        norm, size = state
        later, product = sums()
        ratio = later / norm
        return later, ratio, later / (product - ratio * (later / size))

    def middle(_, state):
        later, ratio, size = next_sizes(state)

        def advance(base, step, rolled, carry):
            tile = shift(base, step)
            own = field(tile)
            direction = own + ratio * direction_ref[tile]
            image = image_ref[tile] + ratio * product_ref[tile]
            direction_ref[tile] = direction
            product_ref[tile] = image
            surface_ref[tile] = surface_ref[tile] + size * direction
            field_ref[pl.ds(first_row(tile), rows), :] = own - size * image
            return carry

        over_tiles(advance, 0)
        return later, size

    state = lax.fori_loop(1, ITERS - 1, middle, (norm, size))
    _, ratio, last_size = next_sizes(state)

    def finish(base, step, rolled, carry):
        tile = shift(base, step)
        own = field(tile)
        direction = own + ratio * direction_ref[tile]
        image = image_ref[tile] + ratio * product_ref[tile]
        results = (surface_ref[tile] + last_size * direction, own - last_size * image)
        lasts = []
        for at, result in enumerate(results):
            upper, lower = result[0:8], result[8:16]
            exponent = exponent_for(jnp.maximum(jnp.abs(upper), jnp.abs(lower)))
            gain = gain_of(exponent)
            words, high = packed(steps_of(upper, gain), steps_of(lower, gain))
            put_eight(out_ref, tile, 2 * at, words)
            lasts += [high, exponent]
        last = jnp.where(near < 2, jnp.where(near == 0, lasts[0], lasts[1]),
                         jnp.where(near == 2, lasts[2], lasts[3]))
        out_ref[tile, 4] = last[0:4]
        return carry

    over_tiles(finish, 0)


def cg_of(got, thickness, rows):
    tiles, columns = got.shape[0], got.shape[-1]
    field = pltpu.VMEM((tiles, rows, columns), jnp.float32)
    return pl.pallas_call(
        cg_kernel,
        in_specs=[
            pl.BlockSpec(memory_space=pltpu.SMEM),
            pl.BlockSpec(memory_space=pltpu.VMEM),
        ],
        out_specs=pl.BlockSpec(memory_space=pltpu.VMEM),
        out_shape=jax.ShapeDtypeStruct(got.shape, jnp.int32),
        scratch_shapes=[pltpu.VMEM((tiles * rows + 16, columns), jnp.float32)] + [field] * 13,
        compiler_params=pltpu.CompilerParams(
            vmem_limit_bytes=(4 << 20) + 18 * tiles * rows * columns * 4
        ),
    )(thickness, got)


def home_kernel(home_ref, surface_ref, residual_ref):
    for member in range(home_ref.shape[0]):
        for at, ref in enumerate((surface_ref, residual_ref)):
            upper, lower = unpacked(
                eight(home_ref, member, 2 * at), home_ref[member, 4, 2 * at : 2 * at + 1, :]
            )
            step = step_of(home_ref[member, 4, 2 * at + 1 : 2 * at + 2, :])
            ref[member, 0:8] = values_of(upper, step)
            ref[member, 8:16] = values_of(lower, step)


def home_of(home, members, rows):
    columns = home.shape[-1]
    step = 16 if members % 16 == 0 else 1
    result = jax.ShapeDtypeStruct((members, rows, columns), jnp.float32)
    return pl.pallas_call(
        home_kernel,
        grid=(members // step,),
        in_specs=[pl.BlockSpec((step,) + home.shape[1:], lambda at: (at, 0, 0, 0))],
        out_specs=[pl.BlockSpec((step, rows, columns), lambda at: (at, 0, 0))] * 2,
        out_shape=[result, result],
        compiler_params=pltpu.CompilerParams(vmem_limit_bytes=8 << 20),
    )(home)


def on_device(zonal, meridional, fraction, thickness, land_mask, edge_codes):
    tiles = lax.axis_size("tile")
    members, _, rows, columns = zonal.shape
    message = message_of(zonal, meridional, fraction, thickness, land_mask, edge_codes)
    if tiles > members:
        message = jnp.pad(message, ((0, tiles - members), (0, 0), (0, 0), (0, 0)))
    got = lax.all_to_all(message, "tile", split_axis=0, concat_axis=0, tiled=True)
    back = cg_of(got, thickness, rows)
    home = lax.all_to_all(back, "tile", split_axis=0, concat_axis=0, tiled=True)
    return tuple(home_of(home, members, rows))


def solution(mesh):
    in_specs = (
        P(None, None, "tile", None),
        P(None, None, "tile", None),
        P(None, "tile", None),
        P(),
        P("tile", None),
        P("tile", None),
    )
    out_specs = (P(None, "tile", None), P(None, "tile", None))
    return jax.shard_map(
        on_device, mesh=mesh, in_specs=in_specs, out_specs=out_specs, check_vma=False
    )
```

```python
import functools

import jax
import jax.numpy as jnp
from jax import lax
from jax.experimental import pallas as pl
from jax.experimental.pallas import tpu as pltpu
from jax.sharding import PartitionSpec as P

NTX = 16
ITERS = 4
CHUNK = 32
BITS = 18
STEPS = 2.0**BITS - 1.0
MIDDLE = 2.0 ** (BITS - 1)
ROUNDING = 2.0**23
PIECES = 5

coupling_coef = 0.25


def power_of_two(exponent):
    power = lax.shift_left(jnp.ones_like(exponent), exponent & 15).astype(jnp.float32)
    for bit in (16, 32, 64):
        power = jnp.where((exponent & bit) != 0, power * 2.0**bit, power)
    return power


def exponent_for(largest):
    for by in (4, 2, 1):
        largest = jnp.maximum(largest, pltpu.roll(largest, by, 0))
    log = jnp.log(jnp.maximum(largest, 2.0**-90)) * 1.4426950408889634
    return jnp.clip(jnp.floor(log + 0.01).astype(jnp.int32) + 97, 0, 127)


def steps_of(values, gain):
    shifted = values * gain + (ROUNDING + MIDDLE)
    return jnp.minimum(shifted, ROUNDING + STEPS).astype(jnp.int32) - int(ROUNDING)


def gain_of(exponent):
    return power_of_two(127 - exponent) * 2.0 ** (96 - 127 + BITS - 1)


def gathered(values):
    sub = lax.broadcasted_iota(jnp.int32, values.shape, 0)
    values = lax.shift_left(values & 15, 4 * sub)
    for by in (4, 2, 1):
        values = values | pltpu.roll(values, by, 0)
    return values


def packed(upper, lower):
    words = upper | lax.shift_left(lower, BITS)
    return words, gathered(lax.shift_right_logical(lower, BITS - 4))


def unpacked(words, high):
    sub = lax.broadcasted_iota(jnp.int32, words.shape, 0)
    upper = words & ((1 << BITS) - 1)
    high = lax.shift_right_logical(jnp.broadcast_to(high, words.shape), 4 * sub) & 15
    return upper, lax.shift_right_logical(words, BITS) | lax.shift_left(high, BITS - 4)


def step_of(exponent):
    return power_of_two(exponent) * 2.0 ** (-96 - (BITS - 1))


def values_of(steps, step):
    return (steps.astype(jnp.float32) - MIDDLE) * step


def eight(ref, at, piece):
    return jnp.concatenate([ref[at, piece], ref[at, piece + 1]], axis=0)


def put_eight(ref, at, piece, values):
    ref[at, piece] = values[0:4]
    ref[at, piece + 1] = values[4:8]


def message_kernel(
    thickness_ref,
    codes_ref,
    zonal_hbm,
    meridional_hbm,
    fraction_hbm,
    land_hbm,
    out_hbm,
    zonal_ref,
    meridional_ref,
    fraction_ref,
    land_ref,
    out_ref,
    in_sems,
    out_sems,
):
    members, levels, rows, columns = zonal_ref.shape
    group = members // out_sems.shape[0]

    def copies_in(at):
        part = pl.ds(at * group, group)
        return (
            pltpu.make_async_copy(zonal_hbm.at[part], zonal_ref.at[part], in_sems.at[0, at]),
            pltpu.make_async_copy(
                meridional_hbm.at[part], meridional_ref.at[part], in_sems.at[1, at]
            ),
        )

    def copy_out(at):
        part = pl.ds(at * group, group)
        return pltpu.make_async_copy(out_ref.at[part], out_hbm.at[part], out_sems.at[at])

    land_copy = pltpu.make_async_copy(land_hbm, land_ref, in_sems.at[2, 0])
    fraction_copy = pltpu.make_async_copy(fraction_hbm, fraction_ref, in_sems.at[2, 1])
    fraction_copy.start()
    land_copy.start()
    for at in range(members // group):
        for copy in copies_in(at):
            copy.start()
    fraction_copy.wait()
    land_copy.wait()
    lane = lax.broadcasted_iota(jnp.int32, (rows, columns), 1)
    row = lax.broadcasted_iota(jnp.int32, (rows, columns), 0)
    place = lax.broadcasted_iota(jnp.int32, (8, columns), 0)
    code = [jnp.where(codes_ref[0, side] == 1, 1 << (BITS + side), 0) for side in range(4)]
    flags = (code[0] + code[1]) + (code[2] + code[3])
    parts = [
        thickness_ref[level] * fraction_ref[level].astype(jnp.float32) for level in range(levels)
    ]
    depth = functools.reduce(lambda one, other: one + other, parts)
    root = jnp.sqrt(depth * (1.0 / sum_of(thickness_ref, levels)))
    steps = jnp.where(land_ref[...] == 1, jnp.minimum(root * STEPS + 0.5, STEPS), 0.0)
    steps = steps.astype(jnp.int32)
    roots, roots_high = packed(steps[0:8], steps[8:16])

    def one(member):
        along = parts[0] * zonal_ref[member, 0].astype(jnp.float32)
        across = parts[0] * meridional_ref[member, 0].astype(jnp.float32)
        for level in range(1, levels):
            along = along + parts[level] * zonal_ref[member, level].astype(jnp.float32)
            across = across + parts[level] * meridional_ref[member, level].astype(jnp.float32)
        east = jnp.where(lane == columns - 1, 0.0, pltpu.roll(along, columns - 1, 1))
        north = jnp.where(row == rows - 1, 0.0, pltpu.roll(across, rows - 1, 0))
        value = along - east + across - north
        first = jnp.where(lane == row, along[:, 0:1], 0.0)
        first = first[0:8] + first[8:16]
        for by in (4, 2, 1):
            first = first + pltpu.roll(first, by, 0)
        edges = jnp.where(place == 3, first, across[0:1])
        largest = jnp.maximum(jnp.abs(value[0:8]), jnp.abs(value[8:16]))
        exponent = exponent_for(jnp.maximum(largest, jnp.abs(edges)))
        gain = gain_of(exponent)
        words, high = packed(steps_of(value[0:8], gain), steps_of(value[8:16], gain))
        edges = steps_of(edges, gain) | jnp.where(
            place == 3, lax.shift_left(exponent, BITS), flags
        )
        last = jnp.where(place == 0, high, jnp.where(place == 1, roots_high, edges))
        put_eight(out_ref, member, 0, words)
        put_eight(out_ref, member, 2, roots)
        out_ref[member, 4] = last[0:4]

    def some(at, carry):
        for copy in copies_in(at):
            copy.wait()
        for member in range(group):
            one(at * group + member)
        copy_out(at).start()
        return carry

    lax.fori_loop(0, members // group, some, 0)
    for at in range(members // group):
        copy_out(at).wait()


def sum_of(thickness_ref, levels):
    whole = thickness_ref[0]
    for level in range(1, levels):
        whole = whole + thickness_ref[level]
    return whole


def message_of(zonal, meridional, fraction, thickness, land_mask, codes):
    members, _, _, columns = zonal.shape
    group = 4 if members % 4 == 0 else 1
    return pl.pallas_call(
        message_kernel,
        in_specs=[pl.BlockSpec(memory_space=pltpu.SMEM)] * 2
        + [pl.BlockSpec(memory_space=pl.ANY)] * 4,
        out_specs=pl.BlockSpec(memory_space=pl.ANY),
        out_shape=jax.ShapeDtypeStruct((members, PIECES, 4, columns), jnp.int32),
        scratch_shapes=[
            pltpu.VMEM(zonal.shape, zonal.dtype),
            pltpu.VMEM(meridional.shape, meridional.dtype),
            pltpu.VMEM(fraction.shape, fraction.dtype),
            pltpu.VMEM(land_mask.shape, land_mask.dtype),
            pltpu.VMEM((members, PIECES, 4, columns), jnp.int32),
            pltpu.SemaphoreType.DMA((3, max(2, members // group))),
            pltpu.SemaphoreType.DMA((members // group,)),
        ],
        compiler_params=pltpu.CompilerParams(vmem_limit_bytes=60 << 20),
    )(thickness, codes, zonal, meridional, fraction, land_mask)


def reversed_rows(values):
    groups = values.shape[0] // 8
    index = 7 - lax.broadcasted_iota(jnp.int32, (8, values.shape[1]), 0)
    pieces = [
        jnp.take_along_axis(
            values[8 * at : 8 * at + 8], index, axis=0, mode="promise_in_bounds"
        )
        for at in reversed(range(groups))
    ]
    return jnp.concatenate(pieces, axis=0)


def reversed_lanes(values):
    columns = values.shape[1]
    index = columns - 1 - lax.broadcasted_iota(jnp.int32, values.shape, 1)
    return jnp.take_along_axis(values, index, axis=1, mode="promise_in_bounds")


def cg_kernel(
    thickness_ref,
    got_ref,
    out_ref,
    field_ref,
    image_ref,
    east_ref,
    west_ref,
    north_ref,
    south_ref,
    total_ref,
    direction_ref,
    product_ref,
    side_ref,
    turned_ref,
    ends_ref,
    surface_ref,
    root_ref,
):
    tiles, rows, columns = image_ref.shape
    levels = thickness_ref.shape[0]
    lane = lax.broadcasted_iota(jnp.int32, (rows, columns), 1)
    row = lax.broadcasted_iota(jnp.int32, (rows, columns), 0)
    near = lax.broadcasted_iota(jnp.int32, (8, columns), 0)
    chunk = min(CHUNK, tiles)

    def over_tiles(body, carry):
        def some(base, inner):
            rolled = {}
            for step in range(chunk):
                inner = body(base, step, rolled, inner)
            return inner

        if tiles == chunk:
            return some(0, carry)
        return lax.fori_loop(0, tiles // chunk, lambda at, inner: some(at * chunk, inner), carry)

    def shift(base, by):
        if isinstance(base, int):
            return (base + by) % tiles
        return lax.rem(base + by + tiles, tiles)

    def first_row(tile):
        at = tile * rows + 8
        return at if isinstance(at, int) else pl.multiple_of(at, 8)

    def field(tile, by=0, ref=field_ref):
        return ref[pl.ds(first_row(tile) + by, rows), :]

    def turned(base, step, rolled, by, ref):
        key = (step, by)
        if key not in rolled:
            rolled[key] = pltpu.roll(field(shift(base, step), 0, ref), by, 1)
        return rolled[key]

    def flips(tile, one, other, mask):
        code = jnp.where(mask, 1 << (BITS + one), 1 << (BITS + other))
        return (got_ref[tile, 4, 2:3, :] & code) != 0

    def flip_sides(tile):
        return flips(tile, 0, 1, lane >= columns // 2)

    def flip_ends(tile):
        return flips(tile, 2, 3, near == 7)

    def neighbours(base, step, rolled, ref):
        tile = shift(base, step)
        own = field(tile, 0, ref)
        east = turned(base, step, rolled, columns - 1, ref)
        west = turned(base, step, rolled, 1, ref)
        side = jnp.where(
            lane >= columns // 2,
            turned(base, step + 1, rolled, columns - 1, ref),
            turned(base, step - 1, rolled, 1, ref),
        )
        ends = jnp.where(
            near == 7,
            ref[pl.ds(first_row(shift(base, step + NTX)), 1), :],
            ref[pl.ds(first_row(shift(base, step - NTX)) + rows - 1, 1), :],
        )
        ends = jnp.where(flip_ends(tile), reversed_lanes(ends), ends)
        north, south = field(tile, 1, ref), field(tile, -1, ref)
        return own, east, west, north, south, side, reversed_rows(side), ends

    levels_sum = sum_of(thickness_ref, levels)
    padding = jnp.zeros((8, columns), jnp.float32)
    for ref in (field_ref, root_ref):
        ref[0:8, :] = padding
        ref[tiles * rows + 8 : tiles * rows + 16, :] = padding

    def read_depth(base, step, rolled, carry):
        tile = shift(base, step)
        upper, lower = unpacked(eight(got_ref, tile, 2), got_ref[tile, 4, 1:2, :])
        steps = jnp.concatenate([upper, lower], axis=0).astype(jnp.float32)
        root_ref[pl.ds(first_row(tile), rows), :] = steps * (1.0 / STEPS)
        return carry

    over_tiles(read_depth, 0)

    def weights(base, step, rolled, carry):
        tile = shift(base, step)
        own, east, west, north, south, side, side_turned, ends = neighbours(
            base, step, rolled, root_ref
        )
        wet = own > 0.0
        own = (coupling_coef * levels_sum) * own
        east = jnp.where(lane == columns - 1, 0.0, own * east)
        west = jnp.where(lane == 0, 0.0, own * west)
        north = jnp.where(row == rows - 1, 0.0, own * north)
        south = jnp.where(row == 0, 0.0, own * south)
        edge = jnp.logical_or(lane == 0, lane == columns - 1)
        side = jnp.where(edge, own * jnp.where(flip_sides(tile), side_turned, side), 0.0)
        upper = jnp.where(near == 0, own[0:8] * ends, 0.0)
        lower = jnp.where(near == 7, own[rows - 8 : rows] * ends, 0.0)
        east_ref[tile], west_ref[tile], north_ref[tile], south_ref[tile] = east, west, north, south
        side_ref[tile] = jnp.where(flip_sides(tile), 0.0, side)
        turned_ref[tile] = jnp.where(flip_sides(tile), side, 0.0)
        both = jnp.concatenate([upper, lower], axis=0)
        ends_ref[tile] = both
        total_ref[tile] = 1.0 + ((east + west) + (north + south)) + (side + both)

        def step_at(by):
            key = ("step", by % tiles)
            if key not in rolled:
                row_of = got_ref[shift(base, by), 4, 3:4, :]
                rolled[key] = step_of(lax.shift_right_logical(row_of, BITS))
            return rolled[key]

        def edge_of(by, at):
            steps = got_ref[shift(base, by), 4, at : at + 1, :] & ((1 << BITS) - 1)
            return values_of(steps, step_at(by))

        upper, lower = unpacked(eight(got_ref, tile, 0), got_ref[tile, 4, 0:1, :])
        value = values_of(jnp.concatenate([upper, lower], axis=0), step_at(step))
        target = jnp.where(flip_sides(tile)[:, columns - 1 : columns], rows - 1 - row, row)
        edge = jnp.where(lane == target, edge_of(step + 1, 3), 0.0)
        edge = jnp.sum(edge, axis=1, keepdims=True)
        end = jnp.broadcast_to(edge_of(step + NTX, 2), (8, columns))
        end = jnp.where(flip_ends(tile), reversed_lanes(end), end)
        end = jnp.concatenate([end] * (rows // 8), axis=0)
        value = value - jnp.where(lane == columns - 1, edge, 0.0)
        value = value - jnp.where(row == rows - 1, end, 0.0)
        value = jnp.where(wet, value, 0.0)
        field_ref[pl.ds(first_row(tile), rows), :] = value
        return carry

    over_tiles(weights, 0)

    def all_of(total):
        return jnp.sum(total, keepdims=True)

    zero = jnp.zeros((rows, columns), jnp.float32)

    def apply(base, step, rolled, totals):
        tile = shift(base, step)
        own, east, west, north, south, side, side_turned, ends = neighbours(
            base, step, rolled, field_ref
        )
        others = (
            (east_ref[tile] * east + west_ref[tile] * west)
            + (north_ref[tile] * north + south_ref[tile] * south)
            + (side_ref[tile] * side + turned_ref[tile] * side_turned)
            + ends_ref[tile] * jnp.concatenate([ends] * (rows // 8), axis=0)
        )
        image = total_ref[tile] * own - others
        image_ref[tile] = image
        return totals[0] + own * own, totals[1] + own * image

    def sums():
        squares, products = over_tiles(apply, (zero, zero))
        return all_of(squares), all_of(products)

    norm, product = sums()
    size = norm / product

    def first(base, step, rolled, carry):
        tile = shift(base, step)
        own, image = field(tile), image_ref[tile]
        direction_ref[tile] = own
        product_ref[tile] = image
        surface_ref[tile] = size * own
        field_ref[pl.ds(first_row(tile), rows), :] = own - size * image
        return carry

    over_tiles(first, 0)

    def next_sizes(state):
        inverse, last = state
        norm, product = sums()
        ratio = norm * inverse
        product = product - ratio * ratio * last
        return norm, product, ratio, norm / product

    def middle(_, state):
        norm, product, ratio, size = next_sizes(state)

        def advance(base, step, rolled, carry):
            tile = shift(base, step)
            own = field(tile)
            direction = own + ratio * direction_ref[tile]
            image = image_ref[tile] + ratio * product_ref[tile]
            direction_ref[tile] = direction
            product_ref[tile] = image
            surface_ref[tile] = surface_ref[tile] + size * direction
            field_ref[pl.ds(first_row(tile), rows), :] = own - size * image
            return carry

        over_tiles(advance, 0)
        return 1.0 / norm, product

    state = lax.fori_loop(1, ITERS - 1, middle, (1.0 / norm, product))
    _, _, ratio, last_size = next_sizes(state)

    def finish(base, step, rolled, carry):
        tile = shift(base, step)
        own = field(tile)
        direction = own + ratio * direction_ref[tile]
        image = image_ref[tile] + ratio * product_ref[tile]
        results = (surface_ref[tile] + last_size * direction, own - last_size * image)
        lasts = []
        for at, result in enumerate(results):
            upper, lower = result[0:8], result[8:16]
            exponent = exponent_for(jnp.maximum(jnp.abs(upper), jnp.abs(lower)))
            gain = gain_of(exponent)
            words, high = packed(steps_of(upper, gain), steps_of(lower, gain))
            put_eight(out_ref, tile, 2 * at, words)
            lasts += [high, exponent]
        last = jnp.where(near < 2, jnp.where(near == 0, lasts[0], lasts[1]),
                         jnp.where(near == 2, lasts[2], lasts[3]))
        out_ref[tile, 4] = last[0:4]
        return carry

    over_tiles(finish, 0)


def cg_of(got, thickness, rows):
    tiles, columns = got.shape[0], got.shape[-1]
    field = pltpu.VMEM((tiles, rows, columns), jnp.float32)
    padded = pltpu.VMEM((tiles * rows + 16, columns), jnp.float32)
    return pl.pallas_call(
        cg_kernel,
        in_specs=[
            pl.BlockSpec(memory_space=pltpu.SMEM),
            pl.BlockSpec(memory_space=pltpu.VMEM),
        ],
        out_specs=pl.BlockSpec(memory_space=pltpu.VMEM),
        out_shape=jax.ShapeDtypeStruct(got.shape, jnp.int32),
        scratch_shapes=[padded] + [field] * 12 + [padded],
        compiler_params=pltpu.CompilerParams(
            vmem_limit_bytes=(4 << 20) + 18 * tiles * rows * columns * 4
        ),
    )(thickness, got)


def home_kernel(home_ref, surface_ref, residual_ref):
    for member in range(home_ref.shape[0]):
        for at, ref in enumerate((surface_ref, residual_ref)):
            upper, lower = unpacked(
                eight(home_ref, member, 2 * at), home_ref[member, 4, 2 * at : 2 * at + 1, :]
            )
            step = step_of(home_ref[member, 4, 2 * at + 1 : 2 * at + 2, :])
            ref[member, 0:8] = values_of(upper, step)
            ref[member, 8:16] = values_of(lower, step)


def home_of(home, members, rows):
    columns = home.shape[-1]
    step = 16 if members % 16 == 0 else 1
    result = jax.ShapeDtypeStruct((members, rows, columns), jnp.float32)
    return pl.pallas_call(
        home_kernel,
        grid=(members // step,),
        in_specs=[pl.BlockSpec((step,) + home.shape[1:], lambda at: (at, 0, 0, 0))],
        out_specs=[pl.BlockSpec((step, rows, columns), lambda at: (at, 0, 0))] * 2,
        out_shape=[result, result],
        compiler_params=pltpu.CompilerParams(vmem_limit_bytes=8 << 20),
    )(home)


def on_device(zonal, meridional, fraction, thickness, land_mask, edge_codes):
    tiles = lax.axis_size("tile")
    members, _, rows, columns = zonal.shape
    message = message_of(zonal, meridional, fraction, thickness, land_mask, edge_codes)
    if tiles > members:
        message = jnp.pad(message, ((0, tiles - members), (0, 0), (0, 0), (0, 0)))
    got = lax.all_to_all(message, "tile", split_axis=0, concat_axis=0, tiled=True)
    back = cg_of(got, thickness, rows)
    home = lax.all_to_all(back, "tile", split_axis=0, concat_axis=0, tiled=True)
    return tuple(home_of(home, members, rows))


def solution(mesh):
    in_specs = (
        P(None, None, "tile", None),
        P(None, None, "tile", None),
        P(None, "tile", None),
        P(),
        P("tile", None),
        P("tile", None),
    )
    out_specs = (P(None, "tile", None), P(None, "tile", None))
    return jax.shard_map(
        on_device, mesh=mesh, in_specs=in_specs, out_specs=out_specs, check_vma=False
    )
```

```python
import functools

import jax
import jax.numpy as jnp
from jax import lax
from jax.experimental import pallas as pl
from jax.experimental.pallas import tpu as pltpu
from jax.sharding import PartitionSpec as P

NTX = 16
ITERS = 4
CHUNK = 32
BITS = 18
STEPS = 2.0**BITS - 1.0
MIDDLE = 2.0 ** (BITS - 1)
ROUNDING = 2.0**23
PIECES = 5

coupling_coef = 0.25


def power_of_two(exponent):
    power = lax.shift_left(jnp.ones_like(exponent), exponent & 15).astype(jnp.float32)
    for bit in (16, 32, 64):
        power = jnp.where((exponent & bit) != 0, power * 2.0**bit, power)
    return power


def exponent_for(largest):
    for by in (4, 2, 1):
        largest = jnp.maximum(largest, pltpu.roll(largest, by, 0))
    log = jnp.log(jnp.maximum(largest, 2.0**-90)) * 1.4426950408889634
    return jnp.clip(jnp.floor(log + 0.01).astype(jnp.int32) + 97, 0, 127)


def steps_of(values, gain):
    shifted = values * gain + (ROUNDING + MIDDLE)
    return jnp.minimum(shifted, ROUNDING + STEPS).astype(jnp.int32) - int(ROUNDING)


def gain_of(exponent):
    return power_of_two(127 - exponent) * 2.0 ** (96 - 127 + BITS - 1)


def gathered(values):
    sub = lax.broadcasted_iota(jnp.int32, values.shape, 0)
    values = lax.shift_left(values & 15, 4 * sub)
    for by in (4, 2, 1):
        values = values | pltpu.roll(values, by, 0)
    return values


def packed(upper, lower):
    words = upper | lax.shift_left(lower, BITS)
    return words, gathered(lax.shift_right_logical(lower, BITS - 4))


def unpacked(words, high):
    sub = lax.broadcasted_iota(jnp.int32, words.shape, 0)
    upper = words & ((1 << BITS) - 1)
    high = lax.shift_right_logical(jnp.broadcast_to(high, words.shape), 4 * sub) & 15
    return upper, lax.shift_right_logical(words, BITS) | lax.shift_left(high, BITS - 4)


def step_of(exponent):
    return power_of_two(exponent) * 2.0 ** (-96 - (BITS - 1))


def values_of(steps, step):
    return (steps.astype(jnp.float32) - MIDDLE) * step


def eight(ref, at, piece):
    return jnp.concatenate([ref[at, piece], ref[at, piece + 1]], axis=0)


def put_eight(ref, at, piece, values):
    ref[at, piece] = values[0:4]
    ref[at, piece + 1] = values[4:8]


def message_kernel(
    thickness_ref,
    codes_ref,
    zonal_hbm,
    meridional_hbm,
    fraction_hbm,
    land_hbm,
    out_hbm,
    zonal_ref,
    meridional_ref,
    fraction_ref,
    land_ref,
    out_ref,
    in_sems,
    out_sems,
):
    members, levels, rows, columns = zonal_ref.shape
    group = members // out_sems.shape[0]

    def copies_in(at):
        part = pl.ds(at * group, group)
        return (
            pltpu.make_async_copy(zonal_hbm.at[part], zonal_ref.at[part], in_sems.at[0, at]),
            pltpu.make_async_copy(
                meridional_hbm.at[part], meridional_ref.at[part], in_sems.at[1, at]
            ),
        )

    def copy_out(at):
        part = pl.ds(at * group, group)
        return pltpu.make_async_copy(out_ref.at[part], out_hbm.at[part], out_sems.at[at])

    land_copy = pltpu.make_async_copy(land_hbm, land_ref, in_sems.at[2, 0])
    fraction_copy = pltpu.make_async_copy(fraction_hbm, fraction_ref, in_sems.at[2, 1])
    fraction_copy.start()
    land_copy.start()
    for at in range(members // group):
        for copy in copies_in(at):
            copy.start()
    fraction_copy.wait()
    land_copy.wait()
    lane = lax.broadcasted_iota(jnp.int32, (rows, columns), 1)
    row = lax.broadcasted_iota(jnp.int32, (rows, columns), 0)
    place = lax.broadcasted_iota(jnp.int32, (8, columns), 0)
    code = [jnp.where(codes_ref[0, side] == 1, 1 << (BITS + side), 0) for side in range(4)]
    flags = (code[0] + code[1]) + (code[2] + code[3])
    parts = [
        thickness_ref[level] * fraction_ref[level].astype(jnp.float32) for level in range(levels)
    ]
    depth = functools.reduce(lambda one, other: one + other, parts)
    root = jnp.sqrt(depth * (1.0 / sum_of(thickness_ref, levels)))
    steps = jnp.where(land_ref[...] == 1, jnp.minimum(root * STEPS + 0.5, STEPS), 0.0)
    steps = steps.astype(jnp.int32)
    roots, roots_high = packed(steps[0:8], steps[8:16])

    def one(member):
        along = parts[0] * zonal_ref[member, 0].astype(jnp.float32)
        across = parts[0] * meridional_ref[member, 0].astype(jnp.float32)
        for level in range(1, levels):
            along = along + parts[level] * zonal_ref[member, level].astype(jnp.float32)
            across = across + parts[level] * meridional_ref[member, level].astype(jnp.float32)
        east = jnp.where(lane == columns - 1, 0.0, pltpu.roll(along, columns - 1, 1))
        north = jnp.where(row == rows - 1, 0.0, pltpu.roll(across, rows - 1, 0))
        value = along - east + across - north
        first = jnp.where(lane == row, along[:, 0:1], 0.0)
        first = first[0:8] + first[8:16]
        for by in (4, 2, 1):
            first = first + pltpu.roll(first, by, 0)
        edges = jnp.where(place == 3, first, across[0:1])
        largest = jnp.maximum(jnp.abs(value[0:8]), jnp.abs(value[8:16]))
        exponent = exponent_for(jnp.maximum(largest, jnp.abs(edges)))
        gain = gain_of(exponent)
        words, high = packed(steps_of(value[0:8], gain), steps_of(value[8:16], gain))
        edges = steps_of(edges, gain) | jnp.where(
            place == 3, lax.shift_left(exponent, BITS), flags
        )
        last = jnp.where(place == 0, high, jnp.where(place == 1, roots_high, edges))
        put_eight(out_ref, member, 0, words)
        put_eight(out_ref, member, 2, roots)
        out_ref[member, 4] = last[0:4]

    def some(at, carry):
        for copy in copies_in(at):
            copy.wait()
        for member in range(group):
            one(at * group + member)
        copy_out(at).start()
        return carry

    lax.fori_loop(0, members // group, some, 0)
    for at in range(members // group):
        copy_out(at).wait()


def sum_of(thickness_ref, levels):
    whole = thickness_ref[0]
    for level in range(1, levels):
        whole = whole + thickness_ref[level]
    return whole


def message_of(zonal, meridional, fraction, thickness, land_mask, codes):
    members, _, _, columns = zonal.shape
    group = 16 if members % 16 == 0 else 1
    return pl.pallas_call(
        message_kernel,
        in_specs=[pl.BlockSpec(memory_space=pltpu.SMEM)] * 2
        + [pl.BlockSpec(memory_space=pl.ANY)] * 4,
        out_specs=pl.BlockSpec(memory_space=pl.ANY),
        out_shape=jax.ShapeDtypeStruct((members, PIECES, 4, columns), jnp.int32),
        scratch_shapes=[
            pltpu.VMEM(zonal.shape, zonal.dtype),
            pltpu.VMEM(meridional.shape, meridional.dtype),
            pltpu.VMEM(fraction.shape, fraction.dtype),
            pltpu.VMEM(land_mask.shape, land_mask.dtype),
            pltpu.VMEM((members, PIECES, 4, columns), jnp.int32),
            pltpu.SemaphoreType.DMA((3, max(2, members // group))),
            pltpu.SemaphoreType.DMA((members // group,)),
        ],
        compiler_params=pltpu.CompilerParams(vmem_limit_bytes=60 << 20),
    )(thickness, codes, zonal, meridional, fraction, land_mask)


def reversed_rows(values):
    groups = values.shape[0] // 8
    index = 7 - lax.broadcasted_iota(jnp.int32, (8, values.shape[1]), 0)
    pieces = [
        jnp.take_along_axis(
            values[8 * at : 8 * at + 8], index, axis=0, mode="promise_in_bounds"
        )
        for at in reversed(range(groups))
    ]
    return jnp.concatenate(pieces, axis=0)


def reversed_lanes(values):
    columns = values.shape[1]
    index = columns - 1 - lax.broadcasted_iota(jnp.int32, values.shape, 1)
    return jnp.take_along_axis(values, index, axis=1, mode="promise_in_bounds")


def cg_kernel(
    thickness_ref,
    got_ref,
    out_ref,
    field_ref,
    image_ref,
    east_ref,
    west_ref,
    north_ref,
    south_ref,
    total_ref,
    direction_ref,
    product_ref,
    side_ref,
    turned_ref,
    ends_ref,
    surface_ref,
    root_ref,
):
    tiles, rows, columns = image_ref.shape
    levels = thickness_ref.shape[0]
    lane = lax.broadcasted_iota(jnp.int32, (rows, columns), 1)
    row = lax.broadcasted_iota(jnp.int32, (rows, columns), 0)
    near = lax.broadcasted_iota(jnp.int32, (8, columns), 0)
    chunk = min(CHUNK, tiles)

    def over_tiles(body, carry):
        def some(base, inner):
            rolled = {}
            for step in range(chunk):
                inner = body(base, step, rolled, inner)
            return inner

        if tiles == chunk:
            return some(0, carry)
        return lax.fori_loop(0, tiles // chunk, lambda at, inner: some(at * chunk, inner), carry)

    def shift(base, by):
        if isinstance(base, int):
            return (base + by) % tiles
        return lax.rem(base + by + tiles, tiles)

    def first_row(tile):
        at = tile * rows + 8
        return at if isinstance(at, int) else pl.multiple_of(at, 8)

    def field(tile, by=0, ref=field_ref):
        return ref[pl.ds(first_row(tile) + by, rows), :]

    def turned(base, step, rolled, by, ref):
        key = (step, by)
        if key not in rolled:
            rolled[key] = pltpu.roll(field(shift(base, step), 0, ref), by, 1)
        return rolled[key]

    def flips(tile, one, other, mask):
        code = jnp.where(mask, 1 << (BITS + one), 1 << (BITS + other))
        return (got_ref[tile, 4, 2:3, :] & code) != 0

    def flip_sides(tile):
        return flips(tile, 0, 1, lane >= columns // 2)

    def flip_ends(tile):
        return flips(tile, 2, 3, near == 7)

    def neighbours(base, step, rolled, ref):
        tile = shift(base, step)
        own = field(tile, 0, ref)
        east = turned(base, step, rolled, columns - 1, ref)
        west = turned(base, step, rolled, 1, ref)
        side = jnp.where(
            lane >= columns // 2,
            turned(base, step + 1, rolled, columns - 1, ref),
            turned(base, step - 1, rolled, 1, ref),
        )
        ends = jnp.where(
            near == 7,
            ref[pl.ds(first_row(shift(base, step + NTX)), 1), :],
            ref[pl.ds(first_row(shift(base, step - NTX)) + rows - 1, 1), :],
        )
        ends = jnp.where(flip_ends(tile), reversed_lanes(ends), ends)
        north, south = field(tile, 1, ref), field(tile, -1, ref)
        return own, east, west, north, south, side, reversed_rows(side), ends

    levels_sum = sum_of(thickness_ref, levels)
    padding = jnp.zeros((8, columns), jnp.float32)
    for ref in (field_ref, root_ref):
        ref[0:8, :] = padding
        ref[tiles * rows + 8 : tiles * rows + 16, :] = padding

    def read_depth(base, step, rolled, carry):
        tile = shift(base, step)
        upper, lower = unpacked(eight(got_ref, tile, 2), got_ref[tile, 4, 1:2, :])
        steps = jnp.concatenate([upper, lower], axis=0).astype(jnp.float32)
        root_ref[pl.ds(first_row(tile), rows), :] = steps * (1.0 / STEPS)
        return carry

    over_tiles(read_depth, 0)

    def weights(base, step, rolled, carry):
        tile = shift(base, step)
        own, east, west, north, south, side, side_turned, ends = neighbours(
            base, step, rolled, root_ref
        )
        wet = own > 0.0
        own = (coupling_coef * levels_sum) * own
        east = jnp.where(lane == columns - 1, 0.0, own * east)
        west = jnp.where(lane == 0, 0.0, own * west)
        north = jnp.where(row == rows - 1, 0.0, own * north)
        south = jnp.where(row == 0, 0.0, own * south)
        edge = jnp.logical_or(lane == 0, lane == columns - 1)
        side = jnp.where(edge, own * jnp.where(flip_sides(tile), side_turned, side), 0.0)
        upper = jnp.where(near == 0, own[0:8] * ends, 0.0)
        lower = jnp.where(near == 7, own[rows - 8 : rows] * ends, 0.0)
        east_ref[tile], west_ref[tile], north_ref[tile], south_ref[tile] = east, west, north, south
        side_ref[tile] = jnp.where(flip_sides(tile), 0.0, side)
        turned_ref[tile] = jnp.where(flip_sides(tile), side, 0.0)
        both = jnp.concatenate([upper, lower], axis=0)
        ends_ref[tile] = both
        total_ref[tile] = 1.0 + ((east + west) + (north + south)) + (side + both)

        def step_at(by):
            key = ("step", by % tiles)
            if key not in rolled:
                row_of = got_ref[shift(base, by), 4, 3:4, :]
                rolled[key] = step_of(lax.shift_right_logical(row_of, BITS))
            return rolled[key]

        def edge_of(by, at):
            steps = got_ref[shift(base, by), 4, at : at + 1, :] & ((1 << BITS) - 1)
            return values_of(steps, step_at(by))

        upper, lower = unpacked(eight(got_ref, tile, 0), got_ref[tile, 4, 0:1, :])
        value = values_of(jnp.concatenate([upper, lower], axis=0), step_at(step))
        target = jnp.where(flip_sides(tile)[:, columns - 1 : columns], rows - 1 - row, row)
        edge = jnp.where(lane == target, edge_of(step + 1, 3), 0.0)
        edge = jnp.sum(edge, axis=1, keepdims=True)
        end = jnp.broadcast_to(edge_of(step + NTX, 2), (8, columns))
        end = jnp.where(flip_ends(tile), reversed_lanes(end), end)
        end = jnp.concatenate([end] * (rows // 8), axis=0)
        value = value - jnp.where(lane == columns - 1, edge, 0.0)
        value = value - jnp.where(row == rows - 1, end, 0.0)
        value = jnp.where(wet, value, 0.0)
        field_ref[pl.ds(first_row(tile), rows), :] = value
        return carry

    over_tiles(weights, 0)

    def all_of(total):
        return jnp.sum(total, keepdims=True)

    zero = jnp.zeros((rows, columns), jnp.float32)

    def apply(base, step, rolled, totals):
        tile = shift(base, step)
        own, east, west, north, south, side, side_turned, ends = neighbours(
            base, step, rolled, field_ref
        )
        others = (
            (east_ref[tile] * east + west_ref[tile] * west)
            + (north_ref[tile] * north + south_ref[tile] * south)
            + (side_ref[tile] * side + turned_ref[tile] * side_turned)
            + ends_ref[tile] * jnp.concatenate([ends] * (rows // 8), axis=0)
        )
        image = total_ref[tile] * own - others
        image_ref[tile] = image
        return totals[0] + own * own, totals[1] + own * image

    def sums():
        squares, products = over_tiles(apply, (zero, zero))
        return all_of(squares), all_of(products)

    norm, product = sums()
    size = norm / product

    def first(base, step, rolled, carry):
        tile = shift(base, step)
        own, image = field(tile), image_ref[tile]
        direction_ref[tile] = own
        product_ref[tile] = image
        surface_ref[tile] = size * own
        field_ref[pl.ds(first_row(tile), rows), :] = own - size * image
        return carry

    over_tiles(first, 0)

    def next_sizes(state):
        inverse, last = state
        norm, product = sums()
        ratio = norm * inverse
        product = product - ratio * ratio * last
        return norm, product, ratio, norm / product

    def middle(_, state):
        norm, product, ratio, size = next_sizes(state)

        def advance(base, step, rolled, carry):
            tile = shift(base, step)
            own = field(tile)
            direction = own + ratio * direction_ref[tile]
            image = image_ref[tile] + ratio * product_ref[tile]
            direction_ref[tile] = direction
            product_ref[tile] = image
            surface_ref[tile] = surface_ref[tile] + size * direction
            field_ref[pl.ds(first_row(tile), rows), :] = own - size * image
            return carry

        over_tiles(advance, 0)
        return 1.0 / norm, product

    state = lax.fori_loop(1, ITERS - 1, middle, (1.0 / norm, product))
    _, _, ratio, last_size = next_sizes(state)

    def finish(base, step, rolled, carry):
        tile = shift(base, step)
        own = field(tile)
        direction = own + ratio * direction_ref[tile]
        image = image_ref[tile] + ratio * product_ref[tile]
        results = (surface_ref[tile] + last_size * direction, own - last_size * image)
        lasts = []
        for at, result in enumerate(results):
            upper, lower = result[0:8], result[8:16]
            exponent = exponent_for(jnp.maximum(jnp.abs(upper), jnp.abs(lower)))
            gain = gain_of(exponent)
            words, high = packed(steps_of(upper, gain), steps_of(lower, gain))
            put_eight(out_ref, tile, 2 * at, words)
            lasts += [high, exponent]
        last = jnp.where(near < 2, jnp.where(near == 0, lasts[0], lasts[1]),
                         jnp.where(near == 2, lasts[2], lasts[3]))
        out_ref[tile, 4] = last[0:4]
        return carry

    over_tiles(finish, 0)


def cg_of(got, thickness, rows):
    tiles, columns = got.shape[0], got.shape[-1]
    field = pltpu.VMEM((tiles, rows, columns), jnp.float32)
    padded = pltpu.VMEM((tiles * rows + 16, columns), jnp.float32)
    return pl.pallas_call(
        cg_kernel,
        in_specs=[
            pl.BlockSpec(memory_space=pltpu.SMEM),
            pl.BlockSpec(memory_space=pltpu.VMEM),
        ],
        out_specs=pl.BlockSpec(memory_space=pltpu.VMEM),
        out_shape=jax.ShapeDtypeStruct(got.shape, jnp.int32),
        scratch_shapes=[padded] + [field] * 12 + [padded],
        compiler_params=pltpu.CompilerParams(
            vmem_limit_bytes=(4 << 20) + 18 * tiles * rows * columns * 4
        ),
    )(thickness, got)


def home_kernel(home_ref, surface_ref, residual_ref):
    for member in range(home_ref.shape[0]):
        for at, ref in enumerate((surface_ref, residual_ref)):
            upper, lower = unpacked(
                eight(home_ref, member, 2 * at), home_ref[member, 4, 2 * at : 2 * at + 1, :]
            )
            step = step_of(home_ref[member, 4, 2 * at + 1 : 2 * at + 2, :])
            ref[member, 0:8] = values_of(upper, step)
            ref[member, 8:16] = values_of(lower, step)


def home_of(home, members, rows):
    columns = home.shape[-1]
    step = 16 if members % 16 == 0 else 1
    result = jax.ShapeDtypeStruct((members, rows, columns), jnp.float32)
    return pl.pallas_call(
        home_kernel,
        grid=(members // step,),
        in_specs=[pl.BlockSpec((step,) + home.shape[1:], lambda at: (at, 0, 0, 0))],
        out_specs=[pl.BlockSpec((step, rows, columns), lambda at: (at, 0, 0))] * 2,
        out_shape=[result, result],
        compiler_params=pltpu.CompilerParams(vmem_limit_bytes=8 << 20),
    )(home)


def on_device(zonal, meridional, fraction, thickness, land_mask, edge_codes):
    tiles = lax.axis_size("tile")
    members, _, rows, columns = zonal.shape
    message = message_of(zonal, meridional, fraction, thickness, land_mask, edge_codes)
    if tiles > members:
        message = jnp.pad(message, ((0, tiles - members), (0, 0), (0, 0), (0, 0)))
    got = lax.all_to_all(message, "tile", split_axis=0, concat_axis=0, tiled=True)
    back = cg_of(got, thickness, rows)
    home = lax.all_to_all(back, "tile", split_axis=0, concat_axis=0, tiled=True)
    return tuple(home_of(home, members, rows))


def solution(mesh):
    in_specs = (
        P(None, None, "tile", None),
        P(None, None, "tile", None),
        P(None, "tile", None),
        P(),
        P("tile", None),
        P("tile", None),
    )
    out_specs = (P(None, "tile", None), P(None, "tile", None))
    return jax.shard_map(
        on_device, mesh=mesh, in_specs=in_specs, out_specs=out_specs, check_vma=False
    )
```

```python
import functools

import jax
import jax.numpy as jnp
from jax import lax
from jax.experimental import pallas as pl
from jax.experimental.pallas import tpu as pltpu
from jax.sharding import PartitionSpec as P

NTX = 16
ITERS = 4
CHUNK = 32
BITS = 18
STEPS = 2.0**BITS - 1.0
MIDDLE = 2.0 ** (BITS - 1)
ROUNDING = 2.0**23
PIECES = 5

coupling_coef = 0.25


def power_of_two(exponent):
    power = lax.shift_left(jnp.ones_like(exponent), exponent & 15).astype(jnp.float32)
    for bit in (16, 32, 64):
        power = jnp.where((exponent & bit) != 0, power * 2.0**bit, power)
    return power


def exponent_for(largest):
    for by in (4, 2, 1):
        largest = jnp.maximum(largest, pltpu.roll(largest, by, 0))
    log = jnp.log(jnp.maximum(largest, 2.0**-90)) * 1.4426950408889634
    return jnp.clip(jnp.floor(log + 0.01).astype(jnp.int32) + 97, 0, 127)


def steps_of(values, gain):
    shifted = values * gain + (ROUNDING + MIDDLE)
    return jnp.minimum(shifted, ROUNDING + STEPS).astype(jnp.int32) - int(ROUNDING)


def gain_of(exponent):
    return power_of_two(127 - exponent) * 2.0 ** (96 - 127 + BITS - 1)


def gathered(values):
    sub = lax.broadcasted_iota(jnp.int32, values.shape, 0)
    values = lax.shift_left(values & 15, 4 * sub)
    for by in (4, 2, 1):
        values = values | pltpu.roll(values, by, 0)
    return values


def packed(upper, lower):
    words = upper | lax.shift_left(lower, BITS)
    return words, gathered(lax.shift_right_logical(lower, BITS - 4))


def unpacked(words, high):
    sub = lax.broadcasted_iota(jnp.int32, words.shape, 0)
    upper = words & ((1 << BITS) - 1)
    high = lax.shift_right_logical(jnp.broadcast_to(high, words.shape), 4 * sub) & 15
    return upper, lax.shift_right_logical(words, BITS) | lax.shift_left(high, BITS - 4)


def step_of(exponent):
    return power_of_two(exponent) * 2.0 ** (-96 - (BITS - 1))


def values_of(steps, step):
    return (steps.astype(jnp.float32) - MIDDLE) * step


def eight(ref, at, piece):
    return jnp.concatenate([ref[at, piece], ref[at, piece + 1]], axis=0)


def put_eight(ref, at, piece, values):
    ref[at, piece] = values[0:4]
    ref[at, piece + 1] = values[4:8]


def message_kernel(
    group,
    thickness_hbm,
    codes_hbm,
    zonal_hbm,
    meridional_hbm,
    fraction_hbm,
    land_hbm,
    out_hbm,
    thickness_ref,
    codes_ref,
    zonal_ref,
    meridional_ref,
    fraction_ref,
    land_ref,
    out_ref,
    in_sems,
    out_sems,
):
    members, levels, rows, columns = zonal_ref.shape

    def copies_in(at):
        part = pl.ds(at * group, group)
        return (
            pltpu.make_async_copy(zonal_hbm.at[part], zonal_ref.at[part], in_sems.at[0, at]),
            pltpu.make_async_copy(
                meridional_hbm.at[part], meridional_ref.at[part], in_sems.at[1, at]
            ),
        )

    def copy_out(at):
        part = pl.ds(at * group, group)
        return pltpu.make_async_copy(out_ref.at[part], out_hbm.at[part], out_sems.at[at])

    small = [
        pltpu.make_async_copy(source, target, in_sems.at[2, at])
        for at, (source, target) in enumerate(
            (
                (fraction_hbm, fraction_ref),
                (thickness_hbm, thickness_ref),
                (land_hbm, land_ref),
                (codes_hbm, codes_ref),
            )
        )
    ]
    for copy in small:
        copy.start()
    for at in range(members // group):
        for copy in copies_in(at):
            copy.start()
    for copy in small:
        copy.wait()
    lane = lax.broadcasted_iota(jnp.int32, (rows, columns), 1)
    row = lax.broadcasted_iota(jnp.int32, (rows, columns), 0)
    place = lax.broadcasted_iota(jnp.int32, (8, columns), 0)
    code = [jnp.where(codes_ref[0, side] == 1, 1 << (BITS + side), 0) for side in range(4)]
    flags = (code[0] + code[1]) + (code[2] + code[3])
    parts = [
        thickness_ref[level] * fraction_ref[level].astype(jnp.float32) for level in range(levels)
    ]
    depth = functools.reduce(lambda one, other: one + other, parts)
    root = jnp.sqrt(depth * (1.0 / sum_of(thickness_ref, levels)))
    steps = jnp.where(land_ref[...] == 1, jnp.minimum(root * STEPS + 0.5, STEPS), 0.0)
    steps = steps.astype(jnp.int32)
    roots, roots_high = packed(steps[0:8], steps[8:16])

    def one(member):
        along = parts[0] * zonal_ref[member, 0].astype(jnp.float32)
        across = parts[0] * meridional_ref[member, 0].astype(jnp.float32)
        for level in range(1, levels):
            along = along + parts[level] * zonal_ref[member, level].astype(jnp.float32)
            across = across + parts[level] * meridional_ref[member, level].astype(jnp.float32)
        east = jnp.where(lane == columns - 1, 0.0, pltpu.roll(along, columns - 1, 1))
        north = jnp.where(row == rows - 1, 0.0, pltpu.roll(across, rows - 1, 0))
        value = along - east + across - north
        first = jnp.where(lane == row, along[:, 0:1], 0.0)
        first = first[0:8] + first[8:16]
        for by in (4, 2, 1):
            first = first + pltpu.roll(first, by, 0)
        edges = jnp.where(place == 3, first, across[0:1])
        largest = jnp.maximum(jnp.abs(value[0:8]), jnp.abs(value[8:16]))
        exponent = exponent_for(jnp.maximum(largest, jnp.abs(edges)))
        gain = gain_of(exponent)
        words, high = packed(steps_of(value[0:8], gain), steps_of(value[8:16], gain))
        edges = steps_of(edges, gain) | jnp.where(
            place == 3, lax.shift_left(exponent, BITS), flags
        )
        last = jnp.where(place == 0, high, jnp.where(place == 1, roots_high, edges))
        put_eight(out_ref, member, 0, words)
        put_eight(out_ref, member, 2, roots)
        out_ref[member, 4] = last[0:4]

    def some(at, carry):
        for copy in copies_in(at):
            copy.wait()
        for member in range(group):
            one(at * group + member)
        copy_out(at).start()
        return carry

    lax.fori_loop(0, members // group, some, 0)
    for at in range(members // group):
        copy_out(at).wait()


def sum_of(thickness_ref, levels):
    whole = thickness_ref[0]
    for level in range(1, levels):
        whole = whole + thickness_ref[level]
    return whole


def message_of(zonal, meridional, fraction, thickness, land_mask, codes):
    members, _, _, columns = zonal.shape
    group = 8 if members % 8 == 0 else 1
    return pl.pallas_call(
        functools.partial(message_kernel, group),
        in_specs=[pl.BlockSpec(memory_space=pl.ANY)] * 6,
        out_specs=pl.BlockSpec(memory_space=pl.ANY),
        out_shape=jax.ShapeDtypeStruct((members, PIECES, 4, columns), jnp.int32),
        scratch_shapes=[
            pltpu.SMEM(thickness.shape, thickness.dtype),
            pltpu.SMEM(codes.shape, codes.dtype),
            pltpu.VMEM(zonal.shape, zonal.dtype),
            pltpu.VMEM(meridional.shape, meridional.dtype),
            pltpu.VMEM(fraction.shape, fraction.dtype),
            pltpu.VMEM(land_mask.shape, land_mask.dtype),
            pltpu.VMEM((members, PIECES, 4, columns), jnp.int32),
            pltpu.SemaphoreType.DMA((3, max(4, members // group))),
            pltpu.SemaphoreType.DMA((members // group,)),
        ],
        compiler_params=pltpu.CompilerParams(vmem_limit_bytes=60 << 20),
    )(thickness, codes, zonal, meridional, fraction, land_mask)


def reversed_rows(values):
    groups = values.shape[0] // 8
    index = 7 - lax.broadcasted_iota(jnp.int32, (8, values.shape[1]), 0)
    pieces = [
        jnp.take_along_axis(
            values[8 * at : 8 * at + 8], index, axis=0, mode="promise_in_bounds"
        )
        for at in reversed(range(groups))
    ]
    return jnp.concatenate(pieces, axis=0)


def reversed_lanes(values):
    columns = values.shape[1]
    index = columns - 1 - lax.broadcasted_iota(jnp.int32, values.shape, 1)
    return jnp.take_along_axis(values, index, axis=1, mode="promise_in_bounds")


def cg_kernel(
    thickness_hbm,
    got_ref,
    out_ref,
    field_ref,
    image_ref,
    east_ref,
    west_ref,
    north_ref,
    south_ref,
    total_ref,
    direction_ref,
    product_ref,
    side_ref,
    turned_ref,
    ends_ref,
    surface_ref,
    root_ref,
    thickness_ref,
    thickness_sem,
):
    tiles, rows, columns = image_ref.shape
    levels = thickness_ref.shape[0]
    lane = lax.broadcasted_iota(jnp.int32, (rows, columns), 1)
    row = lax.broadcasted_iota(jnp.int32, (rows, columns), 0)
    near = lax.broadcasted_iota(jnp.int32, (8, columns), 0)
    chunk = min(CHUNK, tiles)

    def over_tiles(body, carry):
        def some(base, inner):
            rolled = {}
            for step in range(chunk):
                inner = body(base, step, rolled, inner)
            return inner

        if tiles == chunk:
            return some(0, carry)
        return lax.fori_loop(0, tiles // chunk, lambda at, inner: some(at * chunk, inner), carry)

    def shift(base, by):
        if isinstance(base, int):
            return (base + by) % tiles
        return lax.rem(base + by + tiles, tiles)

    def first_row(tile):
        at = tile * rows + 8
        return at if isinstance(at, int) else pl.multiple_of(at, 8)

    def field(tile, by=0, ref=field_ref):
        return ref[pl.ds(first_row(tile) + by, rows), :]

    def turned(base, step, rolled, by, ref):
        key = (step, by)
        if key not in rolled:
            rolled[key] = pltpu.roll(field(shift(base, step), 0, ref), by, 1)
        return rolled[key]

    def flips(tile, one, other, mask):
        code = jnp.where(mask, 1 << (BITS + one), 1 << (BITS + other))
        return (got_ref[tile, 4, 2:3, :] & code) != 0

    def flip_sides(tile):
        return flips(tile, 0, 1, lane >= columns // 2)

    def flip_ends(tile):
        return flips(tile, 2, 3, near == 7)

    def neighbours(base, step, rolled, ref):
        tile = shift(base, step)
        own = field(tile, 0, ref)
        east = turned(base, step, rolled, columns - 1, ref)
        west = turned(base, step, rolled, 1, ref)
        side = jnp.where(
            lane >= columns // 2,
            turned(base, step + 1, rolled, columns - 1, ref),
            turned(base, step - 1, rolled, 1, ref),
        )
        ends = jnp.where(
            near == 7,
            ref[pl.ds(first_row(shift(base, step + NTX)), 1), :],
            ref[pl.ds(first_row(shift(base, step - NTX)) + rows - 1, 1), :],
        )
        ends = jnp.where(flip_ends(tile), reversed_lanes(ends), ends)
        north, south = field(tile, 1, ref), field(tile, -1, ref)
        return own, east, west, north, south, side, reversed_rows(side), ends

    thickness_copy = pltpu.make_async_copy(thickness_hbm, thickness_ref, thickness_sem)
    thickness_copy.start()
    padding = jnp.zeros((8, columns), jnp.float32)
    for ref in (field_ref, root_ref):
        ref[0:8, :] = padding
        ref[tiles * rows + 8 : tiles * rows + 16, :] = padding

    def read_depth(base, step, rolled, carry):
        tile = shift(base, step)
        upper, lower = unpacked(eight(got_ref, tile, 2), got_ref[tile, 4, 1:2, :])
        steps = jnp.concatenate([upper, lower], axis=0).astype(jnp.float32)
        root_ref[pl.ds(first_row(tile), rows), :] = steps * (1.0 / STEPS)
        return carry

    over_tiles(read_depth, 0)
    thickness_copy.wait()
    levels_sum = sum_of(thickness_ref, levels)

    def weights(base, step, rolled, carry):
        tile = shift(base, step)
        own, east, west, north, south, side, side_turned, ends = neighbours(
            base, step, rolled, root_ref
        )
        wet = own > 0.0
        own = (coupling_coef * levels_sum) * own
        east = jnp.where(lane == columns - 1, 0.0, own * east)
        west = jnp.where(lane == 0, 0.0, own * west)
        north = jnp.where(row == rows - 1, 0.0, own * north)
        south = jnp.where(row == 0, 0.0, own * south)
        edge = jnp.logical_or(lane == 0, lane == columns - 1)
        side = jnp.where(edge, own * jnp.where(flip_sides(tile), side_turned, side), 0.0)
        upper = jnp.where(near == 0, own[0:8] * ends, 0.0)
        lower = jnp.where(near == 7, own[rows - 8 : rows] * ends, 0.0)
        east_ref[tile], west_ref[tile], north_ref[tile], south_ref[tile] = east, west, north, south
        side_ref[tile] = jnp.where(flip_sides(tile), 0.0, side)
        turned_ref[tile] = jnp.where(flip_sides(tile), side, 0.0)
        both = jnp.concatenate([upper, lower], axis=0)
        ends_ref[tile] = both
        total_ref[tile] = 1.0 + ((east + west) + (north + south)) + (side + both)

        def step_at(by):
            key = ("step", by % tiles)
            if key not in rolled:
                row_of = got_ref[shift(base, by), 4, 3:4, :]
                rolled[key] = step_of(lax.shift_right_logical(row_of, BITS))
            return rolled[key]

        def edge_of(by, at):
            steps = got_ref[shift(base, by), 4, at : at + 1, :] & ((1 << BITS) - 1)
            return values_of(steps, step_at(by))

        upper, lower = unpacked(eight(got_ref, tile, 0), got_ref[tile, 4, 0:1, :])
        value = values_of(jnp.concatenate([upper, lower], axis=0), step_at(step))
        target = jnp.where(flip_sides(tile)[:, columns - 1 : columns], rows - 1 - row, row)
        edge = jnp.where(lane == target, edge_of(step + 1, 3), 0.0)
        edge = jnp.sum(edge, axis=1, keepdims=True)
        end = jnp.broadcast_to(edge_of(step + NTX, 2), (8, columns))
        end = jnp.where(flip_ends(tile), reversed_lanes(end), end)
        end = jnp.concatenate([end] * (rows // 8), axis=0)
        value = value - jnp.where(lane == columns - 1, edge, 0.0)
        value = value - jnp.where(row == rows - 1, end, 0.0)
        value = jnp.where(wet, value, 0.0)
        field_ref[pl.ds(first_row(tile), rows), :] = value
        return carry

    over_tiles(weights, 0)

    def all_of(total):
        return jnp.sum(total, keepdims=True)

    zero = jnp.zeros((rows, columns), jnp.float32)

    def apply(base, step, rolled, totals):
        tile = shift(base, step)
        own, east, west, north, south, side, side_turned, ends = neighbours(
            base, step, rolled, field_ref
        )
        others = (
            (east_ref[tile] * east + west_ref[tile] * west)
            + (north_ref[tile] * north + south_ref[tile] * south)
            + (side_ref[tile] * side + turned_ref[tile] * side_turned)
            + ends_ref[tile] * jnp.concatenate([ends] * (rows // 8), axis=0)
        )
        image = total_ref[tile] * own - others
        image_ref[tile] = image
        return totals[0] + own * own, totals[1] + own * image

    def sums():
        squares, products = over_tiles(apply, (zero, zero))
        return all_of(squares), all_of(products)

    norm, product = sums()
    size = norm / product

    def first(base, step, rolled, carry):
        tile = shift(base, step)
        own, image = field(tile), image_ref[tile]
        direction_ref[tile] = own
        product_ref[tile] = image
        surface_ref[tile] = size * own
        field_ref[pl.ds(first_row(tile), rows), :] = own - size * image
        return carry

    over_tiles(first, 0)

    def next_sizes(state):
        inverse, last = state
        norm, product = sums()
        ratio = norm * inverse
        product = product - ratio * ratio * last
        return norm, product, ratio, norm / product

    def middle(_, state):
        norm, product, ratio, size = next_sizes(state)

        def advance(base, step, rolled, carry):
            tile = shift(base, step)
            own = field(tile)
            direction = own + ratio * direction_ref[tile]
            image = image_ref[tile] + ratio * product_ref[tile]
            direction_ref[tile] = direction
            product_ref[tile] = image
            surface_ref[tile] = surface_ref[tile] + size * direction
            field_ref[pl.ds(first_row(tile), rows), :] = own - size * image
            return carry

        over_tiles(advance, 0)
        return 1.0 / norm, product

    state = lax.fori_loop(1, ITERS - 1, middle, (1.0 / norm, product))
    _, _, ratio, last_size = next_sizes(state)

    def finish(base, step, rolled, carry):
        tile = shift(base, step)
        own = field(tile)
        direction = own + ratio * direction_ref[tile]
        image = image_ref[tile] + ratio * product_ref[tile]
        results = (surface_ref[tile] + last_size * direction, own - last_size * image)
        lasts = []
        for at, result in enumerate(results):
            upper, lower = result[0:8], result[8:16]
            exponent = exponent_for(jnp.maximum(jnp.abs(upper), jnp.abs(lower)))
            gain = gain_of(exponent)
            words, high = packed(steps_of(upper, gain), steps_of(lower, gain))
            put_eight(out_ref, tile, 2 * at, words)
            lasts += [high, exponent]
        last = jnp.where(near < 2, jnp.where(near == 0, lasts[0], lasts[1]),
                         jnp.where(near == 2, lasts[2], lasts[3]))
        out_ref[tile, 4] = last[0:4]
        return carry

    over_tiles(finish, 0)


def cg_of(got, thickness, rows):
    tiles, columns = got.shape[0], got.shape[-1]
    field = pltpu.VMEM((tiles, rows, columns), jnp.float32)
    padded = pltpu.VMEM((tiles * rows + 16, columns), jnp.float32)
    return pl.pallas_call(
        cg_kernel,
        in_specs=[
            pl.BlockSpec(memory_space=pl.ANY),
            pl.BlockSpec(memory_space=pltpu.VMEM),
        ],
        out_specs=pl.BlockSpec(memory_space=pltpu.VMEM),
        out_shape=jax.ShapeDtypeStruct(got.shape, jnp.int32),
        scratch_shapes=[padded]
        + [field] * 12
        + [padded, pltpu.SMEM(thickness.shape, thickness.dtype), pltpu.SemaphoreType.DMA],
        compiler_params=pltpu.CompilerParams(
            vmem_limit_bytes=(4 << 20) + 18 * tiles * rows * columns * 4
        ),
    )(thickness, got)


def home_kernel(home_ref, surface_ref, residual_ref):
    for member in range(home_ref.shape[0]):
        for at, ref in enumerate((surface_ref, residual_ref)):
            upper, lower = unpacked(
                eight(home_ref, member, 2 * at), home_ref[member, 4, 2 * at : 2 * at + 1, :]
            )
            step = step_of(home_ref[member, 4, 2 * at + 1 : 2 * at + 2, :])
            ref[member, 0:8] = values_of(upper, step)
            ref[member, 8:16] = values_of(lower, step)


def home_of(home, members, rows):
    columns = home.shape[-1]
    step = 16 if members % 16 == 0 else 1
    result = jax.ShapeDtypeStruct((members, rows, columns), jnp.float32)
    return pl.pallas_call(
        home_kernel,
        grid=(members // step,),
        in_specs=[pl.BlockSpec((step,) + home.shape[1:], lambda at: (at, 0, 0, 0))],
        out_specs=[pl.BlockSpec((step, rows, columns), lambda at: (at, 0, 0))] * 2,
        out_shape=[result, result],
        compiler_params=pltpu.CompilerParams(vmem_limit_bytes=8 << 20),
    )(home)


def on_device(zonal, meridional, fraction, thickness, land_mask, edge_codes):
    tiles = lax.axis_size("tile")
    members, _, rows, columns = zonal.shape
    message = message_of(zonal, meridional, fraction, thickness, land_mask, edge_codes)
    if tiles > members:
        message = jnp.pad(message, ((0, tiles - members), (0, 0), (0, 0), (0, 0)))
    got = lax.all_to_all(message, "tile", split_axis=0, concat_axis=0, tiled=True)
    back = cg_of(got, thickness, rows)
    home = lax.all_to_all(back, "tile", split_axis=0, concat_axis=0, tiled=True)
    return tuple(home_of(home, members, rows))


def solution(mesh):
    in_specs = (
        P(None, None, "tile", None),
        P(None, None, "tile", None),
        P(None, "tile", None),
        P(),
        P("tile", None),
        P("tile", None),
    )
    out_specs = (P(None, "tile", None), P(None, "tile", None))
    return jax.shard_map(
        on_device, mesh=mesh, in_specs=in_specs, out_specs=out_specs, check_vma=False
    )
```

```python
import functools

import jax
import jax.numpy as jnp
from jax import lax
from jax.experimental import pallas as pl
from jax.experimental.pallas import tpu as pltpu
from jax.sharding import PartitionSpec as P

NTX = 16
ITERS = 4
CHUNK = 32
BITS = 18
STEPS = 2.0**BITS - 1.0
MIDDLE = 2.0 ** (BITS - 1)
ROUNDING = 2.0**23
PIECES = 5

coupling_coef = 0.25


def power_of_two(exponent):
    power = lax.shift_left(jnp.ones_like(exponent), exponent & 15).astype(jnp.float32)
    for bit in (16, 32, 64):
        power = jnp.where((exponent & bit) != 0, power * 2.0**bit, power)
    return power


def exponent_for(largest):
    for by in (4, 2, 1):
        largest = jnp.maximum(largest, pltpu.roll(largest, by, 0))
    log = jnp.log(jnp.maximum(largest, 2.0**-90)) * 1.4426950408889634
    return jnp.clip(jnp.floor(log + 0.01).astype(jnp.int32) + 97, 0, 127)


def steps_of(values, gain):
    shifted = values * gain + (ROUNDING + MIDDLE)
    return jnp.minimum(shifted, ROUNDING + STEPS).astype(jnp.int32) - int(ROUNDING)


def gain_of(exponent):
    return power_of_two(127 - exponent) * 2.0 ** (96 - 127 + BITS - 1)


def gathered(values):
    sub = lax.broadcasted_iota(jnp.int32, values.shape, 0)
    values = lax.shift_left(values & 15, 4 * sub)
    for by in (4, 2, 1):
        values = values | pltpu.roll(values, by, 0)
    return values


def packed(upper, lower):
    words = upper | lax.shift_left(lower, BITS)
    return words, gathered(lax.shift_right_logical(lower, BITS - 4))


def unpacked(words, high):
    sub = lax.broadcasted_iota(jnp.int32, words.shape, 0)
    upper = words & ((1 << BITS) - 1)
    high = lax.shift_right_logical(jnp.broadcast_to(high, words.shape), 4 * sub) & 15
    return upper, lax.shift_right_logical(words, BITS) | lax.shift_left(high, BITS - 4)


def step_of(exponent):
    return power_of_two(exponent) * 2.0 ** (-96 - (BITS - 1))


def values_of(steps, step):
    return (steps.astype(jnp.float32) - MIDDLE) * step


def eight(ref, at, piece):
    return jnp.concatenate([ref[at, piece], ref[at, piece + 1]], axis=0)


def put_eight(ref, at, piece, values):
    ref[at, piece] = values[0:4]
    ref[at, piece + 1] = values[4:8]


def message_kernel(
    group,
    thickness_hbm,
    codes_hbm,
    zonal_hbm,
    meridional_hbm,
    fraction_hbm,
    land_hbm,
    out_hbm,
    thickness_ref,
    codes_ref,
    zonal_ref,
    meridional_ref,
    fraction_ref,
    land_ref,
    out_ref,
    in_sems,
    out_sems,
):
    members, levels, rows, columns = zonal_ref.shape

    def copies_in(at):
        part = pl.ds(at * group, group)
        return (
            pltpu.make_async_copy(zonal_hbm.at[part], zonal_ref.at[part], in_sems.at[0, at]),
            pltpu.make_async_copy(
                meridional_hbm.at[part], meridional_ref.at[part], in_sems.at[1, at]
            ),
        )

    def copy_out(at):
        part = pl.ds(at * group, group)
        return pltpu.make_async_copy(out_ref.at[part], out_hbm.at[part], out_sems.at[at])

    small = [
        pltpu.make_async_copy(source, target, in_sems.at[2, at])
        for at, (source, target) in enumerate(
            (
                (fraction_hbm, fraction_ref),
                (thickness_hbm, thickness_ref),
                (land_hbm, land_ref),
                (codes_hbm, codes_ref),
            )
        )
    ]
    for copy in small:
        copy.start()
    for at in range(members // group):
        for copy in copies_in(at):
            copy.start()
    for copy in small:
        copy.wait()
    lane = lax.broadcasted_iota(jnp.int32, (rows, columns), 1)
    row = lax.broadcasted_iota(jnp.int32, (rows, columns), 0)
    place = lax.broadcasted_iota(jnp.int32, (8, columns), 0)
    code = [jnp.where(codes_ref[0, side] == 1, 1 << (BITS + side), 0) for side in range(4)]
    flags = (code[0] + code[1]) + (code[2] + code[3])
    parts = [
        thickness_ref[level] * fraction_ref[level].astype(jnp.float32) for level in range(levels)
    ]
    depth = functools.reduce(lambda one, other: one + other, parts)
    root = jnp.sqrt(depth * (1.0 / sum_of(thickness_ref, levels)))
    steps = jnp.where(land_ref[...] == 1, jnp.minimum(root * STEPS + 0.5, STEPS), 0.0)
    steps = steps.astype(jnp.int32)
    roots, roots_high = packed(steps[0:8], steps[8:16])

    def one(member):
        along = parts[0] * zonal_ref[member, 0].astype(jnp.float32)
        across = parts[0] * meridional_ref[member, 0].astype(jnp.float32)
        for level in range(1, levels):
            along = along + parts[level] * zonal_ref[member, level].astype(jnp.float32)
            across = across + parts[level] * meridional_ref[member, level].astype(jnp.float32)
        east = jnp.where(lane == columns - 1, 0.0, pltpu.roll(along, columns - 1, 1))
        north = jnp.where(row == rows - 1, 0.0, pltpu.roll(across, rows - 1, 0))
        value = along - east + across - north
        first = jnp.where(lane == row, along[:, 0:1], 0.0)
        first = first[0:8] + first[8:16]
        for by in (4, 2, 1):
            first = first + pltpu.roll(first, by, 0)
        edges = jnp.where(place == 3, first, across[0:1])
        largest = jnp.maximum(jnp.abs(value[0:8]), jnp.abs(value[8:16]))
        exponent = exponent_for(jnp.maximum(largest, jnp.abs(edges)))
        gain = gain_of(exponent)
        words, high = packed(steps_of(value[0:8], gain), steps_of(value[8:16], gain))
        edges = steps_of(edges, gain) | jnp.where(
            place == 3, lax.shift_left(exponent, BITS), flags
        )
        last = jnp.where(place == 0, high, jnp.where(place == 1, roots_high, edges))
        put_eight(out_ref, member, 0, words)
        put_eight(out_ref, member, 2, roots)
        out_ref[member, 4] = last[0:4]

    def some(at, carry):
        for copy in copies_in(at):
            copy.wait()
        for member in range(group):
            one(at * group + member)
        copy_out(at).start()
        return carry

    lax.fori_loop(0, members // group, some, 0)
    for at in range(members // group):
        copy_out(at).wait()


def sum_of(thickness_ref, levels):
    whole = thickness_ref[0]
    for level in range(1, levels):
        whole = whole + thickness_ref[level]
    return whole


def message_of(zonal, meridional, fraction, thickness, land_mask, codes):
    members, _, _, columns = zonal.shape
    group = 8 if members % 8 == 0 else 1
    return pl.pallas_call(
        functools.partial(message_kernel, group),
        in_specs=[pl.BlockSpec(memory_space=pl.ANY)] * 6,
        out_specs=pl.BlockSpec(memory_space=pl.ANY),
        out_shape=jax.ShapeDtypeStruct((members, PIECES, 4, columns), jnp.int32),
        scratch_shapes=[
            pltpu.SMEM(thickness.shape, thickness.dtype),
            pltpu.SMEM(codes.shape, codes.dtype),
            pltpu.VMEM(zonal.shape, zonal.dtype),
            pltpu.VMEM(meridional.shape, meridional.dtype),
            pltpu.VMEM(fraction.shape, fraction.dtype),
            pltpu.VMEM(land_mask.shape, land_mask.dtype),
            pltpu.VMEM((members, PIECES, 4, columns), jnp.int32),
            pltpu.SemaphoreType.DMA((3, max(4, members // group))),
            pltpu.SemaphoreType.DMA((members // group,)),
        ],
        compiler_params=pltpu.CompilerParams(vmem_limit_bytes=60 << 20),
    )(thickness, codes, zonal, meridional, fraction, land_mask)


def reversed_rows(values):
    groups = values.shape[0] // 8
    index = 7 - lax.broadcasted_iota(jnp.int32, (8, values.shape[1]), 0)
    pieces = [
        jnp.take_along_axis(
            values[8 * at : 8 * at + 8], index, axis=0, mode="promise_in_bounds"
        )
        for at in reversed(range(groups))
    ]
    return jnp.concatenate(pieces, axis=0)


def reversed_lanes(values):
    columns = values.shape[1]
    index = columns - 1 - lax.broadcasted_iota(jnp.int32, values.shape, 1)
    return jnp.take_along_axis(values, index, axis=1, mode="promise_in_bounds")


def cg_kernel(
    thickness_hbm,
    got_ref,
    out_ref,
    field_ref,
    image_ref,
    east_ref,
    west_ref,
    north_ref,
    south_ref,
    total_ref,
    direction_ref,
    product_ref,
    side_ref,
    turned_ref,
    ends_ref,
    surface_ref,
    root_ref,
    thickness_ref,
    thickness_sem,
):
    tiles, rows, columns = image_ref.shape
    levels = thickness_ref.shape[0]
    lane = lax.broadcasted_iota(jnp.int32, (rows, columns), 1)
    row = lax.broadcasted_iota(jnp.int32, (rows, columns), 0)
    near = lax.broadcasted_iota(jnp.int32, (8, columns), 0)
    chunk = min(CHUNK, tiles)

    def over_tiles(body, carry):
        def some(base, inner):
            rolled = {}
            for step in range(chunk):
                inner = body(base, step, rolled, inner)
            return inner

        if tiles == chunk:
            return some(0, carry)
        return lax.fori_loop(0, tiles // chunk, lambda at, inner: some(at * chunk, inner), carry)

    def shift(base, by):
        if isinstance(base, int):
            return (base + by) % tiles
        return lax.rem(base + by + tiles, tiles)

    def first_row(tile):
        at = tile * rows + 8
        return at if isinstance(at, int) else pl.multiple_of(at, 8)

    def field(tile, by=0, ref=field_ref):
        return ref[pl.ds(first_row(tile) + by, rows), :]

    def turned(base, step, rolled, by, ref):
        key = (step, by)
        if key not in rolled:
            rolled[key] = pltpu.roll(field(shift(base, step), 0, ref), by, 1)
        return rolled[key]

    def flips(tile, one, other, mask):
        code = jnp.where(mask, 1 << (BITS + one), 1 << (BITS + other))
        return (got_ref[tile, 4, 2:3, :] & code) != 0

    def flip_sides(tile):
        return flips(tile, 0, 1, lane >= columns // 2)

    def flip_ends(tile):
        return flips(tile, 2, 3, near == 7)

    def neighbours(base, step, rolled, ref):
        tile = shift(base, step)
        own = field(tile, 0, ref)
        east = turned(base, step, rolled, columns - 1, ref)
        west = turned(base, step, rolled, 1, ref)
        side = jnp.where(
            lane >= columns // 2,
            turned(base, step + 1, rolled, columns - 1, ref),
            turned(base, step - 1, rolled, 1, ref),
        )
        ends = jnp.where(
            near == 7,
            ref[pl.ds(first_row(shift(base, step + NTX)), 1), :],
            ref[pl.ds(first_row(shift(base, step - NTX)) + rows - 1, 1), :],
        )
        ends = jnp.where(flip_ends(tile), reversed_lanes(ends), ends)
        north, south = field(tile, 1, ref), field(tile, -1, ref)
        return own, east, west, north, south, side, reversed_rows(side), ends

    thickness_copy = pltpu.make_async_copy(thickness_hbm, thickness_ref, thickness_sem)
    thickness_copy.start()
    padding = jnp.zeros((8, columns), jnp.float32)
    for ref in (field_ref, root_ref):
        ref[0:8, :] = padding
        ref[tiles * rows + 8 : tiles * rows + 16, :] = padding

    def read_depth(base, step, rolled, carry):
        tile = shift(base, step)
        upper, lower = unpacked(eight(got_ref, tile, 2), got_ref[tile, 4, 1:2, :])
        steps = jnp.concatenate([upper, lower], axis=0).astype(jnp.float32)
        root_ref[pl.ds(first_row(tile), rows), :] = steps * (1.0 / STEPS)
        return carry

    over_tiles(read_depth, 0)
    thickness_copy.wait()
    levels_sum = sum_of(thickness_ref, levels)

    def weights(base, step, rolled, carry):
        tile = shift(base, step)
        own, east, west, north, south, side, side_turned, ends = neighbours(
            base, step, rolled, root_ref
        )
        wet = own > 0.0
        own = (coupling_coef * levels_sum) * own
        east = jnp.where(lane == columns - 1, 0.0, own * east)
        west = jnp.where(lane == 0, 0.0, own * west)
        north = jnp.where(row == rows - 1, 0.0, own * north)
        south = jnp.where(row == 0, 0.0, own * south)
        edge = jnp.logical_or(lane == 0, lane == columns - 1)
        side = jnp.where(edge, own * jnp.where(flip_sides(tile), side_turned, side), 0.0)
        upper = jnp.where(near == 0, own[0:8] * ends, 0.0)
        lower = jnp.where(near == 7, own[rows - 8 : rows] * ends, 0.0)
        east_ref[tile], west_ref[tile], north_ref[tile], south_ref[tile] = east, west, north, south
        side_ref[tile] = jnp.where(flip_sides(tile), 0.0, side)
        turned_ref[tile] = jnp.where(flip_sides(tile), side, 0.0)
        both = jnp.concatenate([upper, lower], axis=0)
        ends_ref[tile] = both
        total_ref[tile] = 1.0 + ((east + west) + (north + south)) + (side + both)

        def step_at(by):
            key = ("step", by % tiles)
            if key not in rolled:
                row_of = got_ref[shift(base, by), 4, 3:4, :]
                rolled[key] = step_of(lax.shift_right_logical(row_of, BITS))
            return rolled[key]

        def edge_of(by, at):
            steps = got_ref[shift(base, by), 4, at : at + 1, :] & ((1 << BITS) - 1)
            return values_of(steps, step_at(by))

        upper, lower = unpacked(eight(got_ref, tile, 0), got_ref[tile, 4, 0:1, :])
        value = values_of(jnp.concatenate([upper, lower], axis=0), step_at(step))
        target = jnp.where(flip_sides(tile)[:, columns - 1 : columns], rows - 1 - row, row)
        edge = jnp.where(lane == target, edge_of(step + 1, 3), 0.0)
        edge = jnp.sum(edge, axis=1, keepdims=True)
        end = jnp.broadcast_to(edge_of(step + NTX, 2), (8, columns))
        end = jnp.where(flip_ends(tile), reversed_lanes(end), end)
        end = jnp.concatenate([end] * (rows // 8), axis=0)
        value = value - jnp.where(lane == columns - 1, edge, 0.0)
        value = value - jnp.where(row == rows - 1, end, 0.0)
        value = jnp.where(wet, value, 0.0)
        field_ref[pl.ds(first_row(tile), rows), :] = value
        return carry

    over_tiles(weights, 0)

    def all_of(total):
        return jnp.sum(total, keepdims=True)

    zero = jnp.zeros((rows, columns), jnp.float32)

    def apply(base, step, rolled, totals):
        tile = shift(base, step)
        own, east, west, north, south, side, side_turned, ends = neighbours(
            base, step, rolled, field_ref
        )
        others = (
            (east_ref[tile] * east + west_ref[tile] * west)
            + (north_ref[tile] * north + south_ref[tile] * south)
            + (side_ref[tile] * side + turned_ref[tile] * side_turned)
            + ends_ref[tile] * jnp.concatenate([ends] * (rows // 8), axis=0)
        )
        image = total_ref[tile] * own - others
        image_ref[tile] = image
        return totals[0] + own * own, totals[1] + own * image

    def sums():
        squares, products = over_tiles(apply, (zero, zero))
        return all_of(squares), all_of(products)

    norm, product = sums()
    size = norm / product

    def first(base, step, rolled, carry):
        tile = shift(base, step)
        own, image = field(tile), image_ref[tile]
        direction_ref[tile] = own
        product_ref[tile] = image
        surface_ref[tile] = size * own
        field_ref[pl.ds(first_row(tile), rows), :] = own - size * image
        return carry

    over_tiles(first, 0)

    def next_sizes(state):
        inverse, last = state
        norm, product = sums()
        ratio = norm * inverse
        product = product - ratio * ratio * last
        return norm, product, ratio, norm / product

    def middle(_, state):
        norm, product, ratio, size = next_sizes(state)

        def advance(base, step, rolled, carry):
            tile = shift(base, step)
            own = field(tile)
            direction = own + ratio * direction_ref[tile]
            image = image_ref[tile] + ratio * product_ref[tile]
            direction_ref[tile] = direction
            product_ref[tile] = image
            surface_ref[tile] = surface_ref[tile] + size * direction
            field_ref[pl.ds(first_row(tile), rows), :] = own - size * image
            return carry

        over_tiles(advance, 0)
        return 1.0 / norm, product

    state = lax.fori_loop(1, ITERS - 1, middle, (1.0 / norm, product))
    _, _, ratio, last_size = next_sizes(state)

    def finish(base, step, rolled, carry):
        tile = shift(base, step)
        own = field(tile)
        direction = own + ratio * direction_ref[tile]
        image = image_ref[tile] + ratio * product_ref[tile]
        results = (surface_ref[tile] + last_size * direction, own - last_size * image)
        lasts = []
        for at, result in enumerate(results):
            upper, lower = result[0:8], result[8:16]
            exponent = exponent_for(jnp.maximum(jnp.abs(upper), jnp.abs(lower)))
            gain = gain_of(exponent)
            words, high = packed(steps_of(upper, gain), steps_of(lower, gain))
            put_eight(out_ref, tile, 2 * at, words)
            lasts += [high, exponent]
        last = jnp.where(near < 2, jnp.where(near == 0, lasts[0], lasts[1]),
                         jnp.where(near == 2, lasts[2], lasts[3]))
        out_ref[tile, 4] = last[0:4]
        return carry

    over_tiles(finish, 0)


def cg_of(got, thickness, rows):
    tiles, columns = got.shape[0], got.shape[-1]
    field = pltpu.VMEM((tiles, rows, columns), jnp.float32)
    padded = pltpu.VMEM((tiles * rows + 16, columns), jnp.float32)
    return pl.pallas_call(
        cg_kernel,
        in_specs=[
            pl.BlockSpec(memory_space=pl.ANY),
            pl.BlockSpec(memory_space=pltpu.VMEM),
        ],
        out_specs=pl.BlockSpec(memory_space=pltpu.VMEM),
        out_shape=jax.ShapeDtypeStruct(got.shape, jnp.int32),
        scratch_shapes=[padded]
        + [field] * 12
        + [padded, pltpu.SMEM(thickness.shape, thickness.dtype), pltpu.SemaphoreType.DMA],
        compiler_params=pltpu.CompilerParams(
            vmem_limit_bytes=(4 << 20) + 18 * tiles * rows * columns * 4
        ),
    )(thickness, got)


def home_kernel(home_ref, surface_ref, residual_ref):
    for member in range(home_ref.shape[0]):
        for at, ref in enumerate((surface_ref, residual_ref)):
            upper, lower = unpacked(
                eight(home_ref, member, 2 * at), home_ref[member, 4, 2 * at : 2 * at + 1, :]
            )
            step = step_of(home_ref[member, 4, 2 * at + 1 : 2 * at + 2, :])
            ref[member, 0:8] = values_of(upper, step)
            ref[member, 8:16] = values_of(lower, step)


def home_of(home, members, rows):
    columns = home.shape[-1]
    step = 32 if members % 32 == 0 else 1
    result = jax.ShapeDtypeStruct((members, rows, columns), jnp.float32)
    return pl.pallas_call(
        home_kernel,
        grid=(members // step,),
        in_specs=[pl.BlockSpec((step,) + home.shape[1:], lambda at: (at, 0, 0, 0))],
        out_specs=[pl.BlockSpec((step, rows, columns), lambda at: (at, 0, 0))] * 2,
        out_shape=[result, result],
        compiler_params=pltpu.CompilerParams(vmem_limit_bytes=8 << 20),
    )(home)


def on_device(zonal, meridional, fraction, thickness, land_mask, edge_codes):
    tiles = lax.axis_size("tile")
    members, _, rows, columns = zonal.shape
    message = message_of(zonal, meridional, fraction, thickness, land_mask, edge_codes)
    if tiles > members:
        message = jnp.pad(message, ((0, tiles - members), (0, 0), (0, 0), (0, 0)))
    got = lax.all_to_all(message, "tile", split_axis=0, concat_axis=0, tiled=True)
    back = cg_of(got, thickness, rows)
    home = lax.all_to_all(back, "tile", split_axis=0, concat_axis=0, tiled=True)
    return tuple(home_of(home, members, rows))


def solution(mesh):
    in_specs = (
        P(None, None, "tile", None),
        P(None, None, "tile", None),
        P(None, "tile", None),
        P(),
        P("tile", None),
        P("tile", None),
    )
    out_specs = (P(None, "tile", None), P(None, "tile", None))
    return jax.shard_map(
        on_device, mesh=mesh, in_specs=in_specs, out_specs=out_specs, check_vma=False
    )
```

```python
import functools

import jax
import jax.numpy as jnp
from jax import lax
from jax.experimental import pallas as pl
from jax.experimental.pallas import tpu as pltpu
from jax.sharding import PartitionSpec as P

NTX = 16
ITERS = 4
CHUNK = 32
BITS = 18
STEPS = 2.0**BITS - 1.0
MIDDLE = 2.0 ** (BITS - 1)
ROUNDING = 2.0**23
PIECES = 5

coupling_coef = 0.25


def power_of_two(exponent):
    power = lax.shift_left(jnp.ones_like(exponent), exponent & 15).astype(jnp.float32)
    for bit in (16, 32, 64):
        power = jnp.where((exponent & bit) != 0, power * 2.0**bit, power)
    return power


def exponent_for(largest):
    for by in (4, 2, 1):
        largest = jnp.maximum(largest, pltpu.roll(largest, by, 0))
    log = jnp.log(jnp.maximum(largest, 2.0**-90)) * 1.4426950408889634
    return jnp.clip(jnp.floor(log + 0.01).astype(jnp.int32) + 97, 0, 127)


def steps_of(values, gain):
    shifted = values * gain + (ROUNDING + MIDDLE)
    return jnp.minimum(shifted, ROUNDING + STEPS).astype(jnp.int32) - int(ROUNDING)


def gain_of(exponent):
    return power_of_two(127 - exponent) * 2.0 ** (96 - 127 + BITS - 1)


def gathered(values):
    sub = lax.broadcasted_iota(jnp.int32, values.shape, 0)
    values = lax.shift_left(values & 15, 4 * sub)
    for by in (4, 2, 1):
        values = values | pltpu.roll(values, by, 0)
    return values


def packed(upper, lower):
    words = upper | lax.shift_left(lower, BITS)
    return words, gathered(lax.shift_right_logical(lower, BITS - 4))


def unpacked(words, high):
    sub = lax.broadcasted_iota(jnp.int32, words.shape, 0)
    upper = words & ((1 << BITS) - 1)
    high = lax.shift_right_logical(jnp.broadcast_to(high, words.shape), 4 * sub) & 15
    return upper, lax.shift_right_logical(words, BITS) | lax.shift_left(high, BITS - 4)


def step_of(exponent):
    return power_of_two(exponent) * 2.0 ** (-96 - (BITS - 1))


def values_of(steps, step):
    return (steps.astype(jnp.float32) - MIDDLE) * step


def eight(ref, at, piece):
    return jnp.concatenate([ref[at, piece], ref[at, piece + 1]], axis=0)


def put_eight(ref, at, piece, values):
    ref[at, piece] = values[0:4]
    ref[at, piece + 1] = values[4:8]


def message_kernel(
    group,
    thickness_hbm,
    codes_hbm,
    zonal_hbm,
    meridional_hbm,
    fraction_hbm,
    land_hbm,
    out_hbm,
    thickness_ref,
    codes_ref,
    zonal_ref,
    meridional_ref,
    fraction_ref,
    land_ref,
    out_ref,
    in_sems,
    out_sems,
):
    members, levels, rows, columns = zonal_ref.shape

    def copies_in(at):
        part = pl.ds(at * group, group)
        return (
            pltpu.make_async_copy(zonal_hbm.at[part], zonal_ref.at[part], in_sems.at[0, at]),
            pltpu.make_async_copy(
                meridional_hbm.at[part], meridional_ref.at[part], in_sems.at[1, at]
            ),
        )

    def copy_out(at):
        part = pl.ds(at * group, group)
        return pltpu.make_async_copy(out_ref.at[part], out_hbm.at[part], out_sems.at[at])

    small = [
        pltpu.make_async_copy(source, target, in_sems.at[2, at])
        for at, (source, target) in enumerate(
            (
                (fraction_hbm, fraction_ref),
                (thickness_hbm, thickness_ref),
                (land_hbm, land_ref),
                (codes_hbm, codes_ref),
            )
        )
    ]
    for copy in small:
        copy.start()
    for at in range(members // group):
        for copy in copies_in(at):
            copy.start()
    for copy in small:
        copy.wait()
    lane = lax.broadcasted_iota(jnp.int32, (rows, columns), 1)
    row = lax.broadcasted_iota(jnp.int32, (rows, columns), 0)
    place = lax.broadcasted_iota(jnp.int32, (8, columns), 0)
    code = [jnp.where(codes_ref[0, side] == 1, 1 << (BITS + side), 0) for side in range(4)]
    flags = (code[0] + code[1]) + (code[2] + code[3])
    parts = [
        thickness_ref[level] * fraction_ref[level].astype(jnp.float32) for level in range(levels)
    ]
    depth = functools.reduce(lambda one, other: one + other, parts)
    root = jnp.sqrt(depth * (1.0 / sum_of(thickness_ref, levels)))
    steps = jnp.where(land_ref[...] == 1, jnp.minimum(root * STEPS + 0.5, STEPS), 0.0)
    steps = steps.astype(jnp.int32)
    roots, roots_high = packed(steps[0:8], steps[8:16])

    def one(member):
        along = parts[0] * zonal_ref[member, 0].astype(jnp.float32)
        across = parts[0] * meridional_ref[member, 0].astype(jnp.float32)
        for level in range(1, levels):
            along = along + parts[level] * zonal_ref[member, level].astype(jnp.float32)
            across = across + parts[level] * meridional_ref[member, level].astype(jnp.float32)
        east = jnp.where(lane == columns - 1, 0.0, pltpu.roll(along, columns - 1, 1))
        north = jnp.where(row == rows - 1, 0.0, pltpu.roll(across, rows - 1, 0))
        value = along - east + across - north
        first = jnp.where(lane == row, along[:, 0:1], 0.0)
        first = first[0:8] + first[8:16]
        for by in (4, 2, 1):
            first = first + pltpu.roll(first, by, 0)
        edges = jnp.where(place == 3, first, across[0:1])
        largest = jnp.maximum(jnp.abs(value[0:8]), jnp.abs(value[8:16]))
        exponent = exponent_for(jnp.maximum(largest, jnp.abs(edges)))
        gain = gain_of(exponent)
        words, high = packed(steps_of(value[0:8], gain), steps_of(value[8:16], gain))
        edges = steps_of(edges, gain) | jnp.where(
            place == 3, lax.shift_left(exponent, BITS), flags
        )
        last = jnp.where(place == 0, high, jnp.where(place == 1, roots_high, edges))
        put_eight(out_ref, member, 0, words)
        put_eight(out_ref, member, 2, roots)
        out_ref[member, 4] = last[0:4]

    def some(at, carry):
        for copy in copies_in(at):
            copy.wait()
        for member in range(group):
            one(at * group + member)
        copy_out(at).start()
        return carry

    for at in range(members // group):
        some(at, 0)
    for at in range(members // group):
        copy_out(at).wait()


def sum_of(thickness_ref, levels):
    whole = thickness_ref[0]
    for level in range(1, levels):
        whole = whole + thickness_ref[level]
    return whole


def message_of(zonal, meridional, fraction, thickness, land_mask, codes):
    members, _, _, columns = zonal.shape
    group = 8 if members % 8 == 0 else 1
    return pl.pallas_call(
        functools.partial(message_kernel, group),
        in_specs=[pl.BlockSpec(memory_space=pl.ANY)] * 6,
        out_specs=pl.BlockSpec(memory_space=pl.ANY),
        out_shape=jax.ShapeDtypeStruct((members, PIECES, 4, columns), jnp.int32),
        scratch_shapes=[
            pltpu.SMEM(thickness.shape, thickness.dtype),
            pltpu.SMEM(codes.shape, codes.dtype),
            pltpu.VMEM(zonal.shape, zonal.dtype),
            pltpu.VMEM(meridional.shape, meridional.dtype),
            pltpu.VMEM(fraction.shape, fraction.dtype),
            pltpu.VMEM(land_mask.shape, land_mask.dtype),
            pltpu.VMEM((members, PIECES, 4, columns), jnp.int32),
            pltpu.SemaphoreType.DMA((3, max(4, members // group))),
            pltpu.SemaphoreType.DMA((members // group,)),
        ],
        compiler_params=pltpu.CompilerParams(vmem_limit_bytes=60 << 20),
    )(thickness, codes, zonal, meridional, fraction, land_mask)


def reversed_rows(values):
    groups = values.shape[0] // 8
    index = 7 - lax.broadcasted_iota(jnp.int32, (8, values.shape[1]), 0)
    pieces = [
        jnp.take_along_axis(
            values[8 * at : 8 * at + 8], index, axis=0, mode="promise_in_bounds"
        )
        for at in reversed(range(groups))
    ]
    return jnp.concatenate(pieces, axis=0)


def reversed_lanes(values):
    columns = values.shape[1]
    index = columns - 1 - lax.broadcasted_iota(jnp.int32, values.shape, 1)
    return jnp.take_along_axis(values, index, axis=1, mode="promise_in_bounds")


def cg_kernel(
    thickness_hbm,
    got_ref,
    out_ref,
    field_ref,
    image_ref,
    east_ref,
    west_ref,
    north_ref,
    south_ref,
    total_ref,
    direction_ref,
    product_ref,
    side_ref,
    turned_ref,
    ends_ref,
    surface_ref,
    root_ref,
    thickness_ref,
    thickness_sem,
):
    tiles, rows, columns = image_ref.shape
    levels = thickness_ref.shape[0]
    lane = lax.broadcasted_iota(jnp.int32, (rows, columns), 1)
    row = lax.broadcasted_iota(jnp.int32, (rows, columns), 0)
    near = lax.broadcasted_iota(jnp.int32, (8, columns), 0)
    chunk = min(CHUNK, tiles)

    def over_tiles(body, carry):
        def some(base, inner):
            rolled = {}
            for step in range(chunk):
                inner = body(base, step, rolled, inner)
            return inner

        if tiles == chunk:
            return some(0, carry)
        return lax.fori_loop(0, tiles // chunk, lambda at, inner: some(at * chunk, inner), carry)

    def shift(base, by):
        if isinstance(base, int):
            return (base + by) % tiles
        return lax.rem(base + by + tiles, tiles)

    def first_row(tile):
        at = tile * rows + 8
        return at if isinstance(at, int) else pl.multiple_of(at, 8)

    def field(tile, by=0, ref=field_ref):
        return ref[pl.ds(first_row(tile) + by, rows), :]

    def turned(base, step, rolled, by, ref):
        key = (step, by)
        if key not in rolled:
            rolled[key] = pltpu.roll(field(shift(base, step), 0, ref), by, 1)
        return rolled[key]

    def flips(tile, one, other, mask):
        code = jnp.where(mask, 1 << (BITS + one), 1 << (BITS + other))
        return (got_ref[tile, 4, 2:3, :] & code) != 0

    def flip_sides(tile):
        return flips(tile, 0, 1, lane >= columns // 2)

    def flip_ends(tile):
        return flips(tile, 2, 3, near == 7)

    def neighbours(base, step, rolled, ref):
        tile = shift(base, step)
        own = field(tile, 0, ref)
        east = turned(base, step, rolled, columns - 1, ref)
        west = turned(base, step, rolled, 1, ref)
        side = jnp.where(
            lane >= columns // 2,
            turned(base, step + 1, rolled, columns - 1, ref),
            turned(base, step - 1, rolled, 1, ref),
        )
        ends = jnp.where(
            near == 7,
            ref[pl.ds(first_row(shift(base, step + NTX)), 1), :],
            ref[pl.ds(first_row(shift(base, step - NTX)) + rows - 1, 1), :],
        )
        ends = jnp.where(flip_ends(tile), reversed_lanes(ends), ends)
        north, south = field(tile, 1, ref), field(tile, -1, ref)
        return own, east, west, north, south, side, reversed_rows(side), ends

    thickness_copy = pltpu.make_async_copy(thickness_hbm, thickness_ref, thickness_sem)
    thickness_copy.start()
    padding = jnp.zeros((8, columns), jnp.float32)
    for ref in (field_ref, root_ref):
        ref[0:8, :] = padding
        ref[tiles * rows + 8 : tiles * rows + 16, :] = padding

    def read_depth(base, step, rolled, carry):
        tile = shift(base, step)
        upper, lower = unpacked(eight(got_ref, tile, 2), got_ref[tile, 4, 1:2, :])
        steps = jnp.concatenate([upper, lower], axis=0).astype(jnp.float32)
        root_ref[pl.ds(first_row(tile), rows), :] = steps * (1.0 / STEPS)
        return carry

    over_tiles(read_depth, 0)
    thickness_copy.wait()
    levels_sum = sum_of(thickness_ref, levels)

    def weights(base, step, rolled, carry):
        tile = shift(base, step)
        own, east, west, north, south, side, side_turned, ends = neighbours(
            base, step, rolled, root_ref
        )
        wet = own > 0.0
        own = (coupling_coef * levels_sum) * own
        east = jnp.where(lane == columns - 1, 0.0, own * east)
        west = jnp.where(lane == 0, 0.0, own * west)
        north = jnp.where(row == rows - 1, 0.0, own * north)
        south = jnp.where(row == 0, 0.0, own * south)
        edge = jnp.logical_or(lane == 0, lane == columns - 1)
        side = jnp.where(edge, own * jnp.where(flip_sides(tile), side_turned, side), 0.0)
        upper = jnp.where(near == 0, own[0:8] * ends, 0.0)
        lower = jnp.where(near == 7, own[rows - 8 : rows] * ends, 0.0)
        east_ref[tile], west_ref[tile], north_ref[tile], south_ref[tile] = east, west, north, south
        side_ref[tile] = jnp.where(flip_sides(tile), 0.0, side)
        turned_ref[tile] = jnp.where(flip_sides(tile), side, 0.0)
        both = jnp.concatenate([upper, lower], axis=0)
        ends_ref[tile] = both
        total_ref[tile] = 1.0 + ((east + west) + (north + south)) + (side + both)

        def step_at(by):
            key = ("step", by % tiles)
            if key not in rolled:
                row_of = got_ref[shift(base, by), 4, 3:4, :]
                rolled[key] = step_of(lax.shift_right_logical(row_of, BITS))
            return rolled[key]

        def edge_of(by, at):
            steps = got_ref[shift(base, by), 4, at : at + 1, :] & ((1 << BITS) - 1)
            return values_of(steps, step_at(by))

        upper, lower = unpacked(eight(got_ref, tile, 0), got_ref[tile, 4, 0:1, :])
        value = values_of(jnp.concatenate([upper, lower], axis=0), step_at(step))
        target = jnp.where(flip_sides(tile)[:, columns - 1 : columns], rows - 1 - row, row)
        edge = jnp.where(lane == target, edge_of(step + 1, 3), 0.0)
        edge = jnp.sum(edge, axis=1, keepdims=True)
        end = jnp.broadcast_to(edge_of(step + NTX, 2), (8, columns))
        end = jnp.where(flip_ends(tile), reversed_lanes(end), end)
        end = jnp.concatenate([end] * (rows // 8), axis=0)
        value = value - jnp.where(lane == columns - 1, edge, 0.0)
        value = value - jnp.where(row == rows - 1, end, 0.0)
        value = jnp.where(wet, value, 0.0)
        field_ref[pl.ds(first_row(tile), rows), :] = value
        return carry

    over_tiles(weights, 0)

    def all_of(total):
        return jnp.sum(total, keepdims=True)

    zero = jnp.zeros((rows, columns), jnp.float32)

    def apply(base, step, rolled, totals):
        tile = shift(base, step)
        own, east, west, north, south, side, side_turned, ends = neighbours(
            base, step, rolled, field_ref
        )
        others = (
            (east_ref[tile] * east + west_ref[tile] * west)
            + (north_ref[tile] * north + south_ref[tile] * south)
            + (side_ref[tile] * side + turned_ref[tile] * side_turned)
            + ends_ref[tile] * jnp.concatenate([ends] * (rows // 8), axis=0)
        )
        image = total_ref[tile] * own - others
        image_ref[tile] = image
        return totals[0] + own * own, totals[1] + own * image

    def sums():
        squares, products = over_tiles(apply, (zero, zero))
        return all_of(squares), all_of(products)

    norm, product = sums()
    size = norm / product

    def first(base, step, rolled, carry):
        tile = shift(base, step)
        own, image = field(tile), image_ref[tile]
        direction_ref[tile] = own
        product_ref[tile] = image
        surface_ref[tile] = size * own
        field_ref[pl.ds(first_row(tile), rows), :] = own - size * image
        return carry

    over_tiles(first, 0)

    def next_sizes(state):
        inverse, last = state
        norm, product = sums()
        ratio = norm * inverse
        product = product - ratio * ratio * last
        return norm, product, ratio, norm / product

    def middle(_, state):
        norm, product, ratio, size = next_sizes(state)

        def advance(base, step, rolled, carry):
            tile = shift(base, step)
            own = field(tile)
            direction = own + ratio * direction_ref[tile]
            image = image_ref[tile] + ratio * product_ref[tile]
            direction_ref[tile] = direction
            product_ref[tile] = image
            surface_ref[tile] = surface_ref[tile] + size * direction
            field_ref[pl.ds(first_row(tile), rows), :] = own - size * image
            return carry

        over_tiles(advance, 0)
        return 1.0 / norm, product

    state = lax.fori_loop(1, ITERS - 1, middle, (1.0 / norm, product))
    _, _, ratio, last_size = next_sizes(state)

    def finish(base, step, rolled, carry):
        tile = shift(base, step)
        own = field(tile)
        direction = own + ratio * direction_ref[tile]
        image = image_ref[tile] + ratio * product_ref[tile]
        results = (surface_ref[tile] + last_size * direction, own - last_size * image)
        lasts = []
        for at, result in enumerate(results):
            upper, lower = result[0:8], result[8:16]
            exponent = exponent_for(jnp.maximum(jnp.abs(upper), jnp.abs(lower)))
            gain = gain_of(exponent)
            words, high = packed(steps_of(upper, gain), steps_of(lower, gain))
            put_eight(out_ref, tile, 2 * at, words)
            lasts += [high, exponent]
        last = jnp.where(near < 2, jnp.where(near == 0, lasts[0], lasts[1]),
                         jnp.where(near == 2, lasts[2], lasts[3]))
        out_ref[tile, 4] = last[0:4]
        return carry

    over_tiles(finish, 0)


def cg_of(got, thickness, rows):
    tiles, columns = got.shape[0], got.shape[-1]
    field = pltpu.VMEM((tiles, rows, columns), jnp.float32)
    padded = pltpu.VMEM((tiles * rows + 16, columns), jnp.float32)
    return pl.pallas_call(
        cg_kernel,
        in_specs=[
            pl.BlockSpec(memory_space=pl.ANY),
            pl.BlockSpec(memory_space=pltpu.VMEM),
        ],
        out_specs=pl.BlockSpec(memory_space=pltpu.VMEM),
        out_shape=jax.ShapeDtypeStruct(got.shape, jnp.int32),
        scratch_shapes=[padded]
        + [field] * 12
        + [padded, pltpu.SMEM(thickness.shape, thickness.dtype), pltpu.SemaphoreType.DMA],
        compiler_params=pltpu.CompilerParams(
            vmem_limit_bytes=(4 << 20) + 18 * tiles * rows * columns * 4
        ),
    )(thickness, got)


def home_kernel(home_ref, surface_ref, residual_ref):
    for member in range(home_ref.shape[0]):
        for at, ref in enumerate((surface_ref, residual_ref)):
            upper, lower = unpacked(
                eight(home_ref, member, 2 * at), home_ref[member, 4, 2 * at : 2 * at + 1, :]
            )
            step = step_of(home_ref[member, 4, 2 * at + 1 : 2 * at + 2, :])
            ref[member, 0:8] = values_of(upper, step)
            ref[member, 8:16] = values_of(lower, step)


def home_of(home, members, rows):
    columns = home.shape[-1]
    step = 16 if members % 16 == 0 else 1
    result = jax.ShapeDtypeStruct((members, rows, columns), jnp.float32)
    return pl.pallas_call(
        home_kernel,
        grid=(members // step,),
        in_specs=[pl.BlockSpec((step,) + home.shape[1:], lambda at: (at, 0, 0, 0))],
        out_specs=[pl.BlockSpec((step, rows, columns), lambda at: (at, 0, 0))] * 2,
        out_shape=[result, result],
        compiler_params=pltpu.CompilerParams(vmem_limit_bytes=8 << 20),
    )(home)


def on_device(zonal, meridional, fraction, thickness, land_mask, edge_codes):
    tiles = lax.axis_size("tile")
    members, _, rows, columns = zonal.shape
    message = message_of(zonal, meridional, fraction, thickness, land_mask, edge_codes)
    if tiles > members:
        message = jnp.pad(message, ((0, tiles - members), (0, 0), (0, 0), (0, 0)))
    got = lax.all_to_all(message, "tile", split_axis=0, concat_axis=0, tiled=True)
    back = cg_of(got, thickness, rows)
    home = lax.all_to_all(back, "tile", split_axis=0, concat_axis=0, tiled=True)
    return tuple(home_of(home, members, rows))


def solution(mesh):
    in_specs = (
        P(None, None, "tile", None),
        P(None, None, "tile", None),
        P(None, "tile", None),
        P(),
        P("tile", None),
        P("tile", None),
    )
    out_specs = (P(None, "tile", None), P(None, "tile", None))
    return jax.shard_map(
        on_device, mesh=mesh, in_specs=in_specs, out_specs=out_specs, check_vma=False
    )
```
